32 devices in a mesh: dp: 16 (over z, y, core), seq: 2 (over x).
Axes of the slice: x: 2, y: 2, z: 4, core: 2. Of those that a mesh axis runs over, the one named last changes fastest.
Arguments:
- frames: bfloat16 [32, 1728, 768], P('dp', 'seq'), may hold values from -6 to 6
- targets: bfloat16 [32, 1728, 768], P('dp', 'seq'), may hold values from -6 to 6
- lead_index: int32 [32], P('dp'), may hold values from 0 to 39
- lead_counts: int32 [16, 40], P('dp'), may hold values from 15 to 855, as said below
- first_gain: bfloat16 [768], P('seq'), may hold values from 0.099609375 to 1.8984375
- first_shift: bfloat16 [768], P('seq'), may hold values from -0.19921875 to 0.19921875
- query_weight: bfloat16 [768, 768], P('seq'), may hold values from -0.3125 to 0.3125
- key_weight: bfloat16 [768, 768], P('seq'), may hold values from -0.3125 to 0.3125
- value_weight: bfloat16 [768, 768], P('seq'), may hold values from -0.21875 to 0.21875
- output_weight: bfloat16 [768, 768], P('seq'), may hold values from -1.25 to 1.25
- second_gain: bfloat16 [768], P('seq'), may hold values from 0.099609375 to 1.8984375
- second_shift: bfloat16 [768], P('seq'), may hold values from -0.19921875 to 0.19921875
- up_weight: bfloat16 [768, 3072], P('seq'), may hold values from -0.21875 to 0.21875
- down_weight: bfloat16 [3072, 768], P('seq'), may hold values from -0.109375 to 0.109375
- lead_table: bfloat16 [40, 768], P(None, 'seq'), may hold values from -0.29882812 to 0.29882812
Outputs:
- output: bfloat16 [32, 1728, 768], P('dp', 'seq')
- input_grad: bfloat16 [32, 1728, 768], P('dp', 'seq')
- first_gain_grad: float32 [768], P('seq')
- first_shift_grad: float32 [768], P('seq')
- query_grad: float32 [768, 768], P('seq')
- key_grad: float32 [768, 768], P('seq')
- value_grad: float32 [768, 768], P('seq')
- output_weight_grad: float32 [768, 768], P('seq')
- second_gain_grad: float32 [768], P('seq')
- second_shift_grad: float32 [768], P('seq')
- up_grad: float32 [768, 3072], P('seq')
- down_grad: float32 [3072, 768], P('seq')
- lead_table_grad: float32 [40, 768], P(None, 'seq')
The draws below stay inside these ranges and needn't reach their ends.
Inputs may be any that keep to these rules, and one draw needn't show every extreme that they name: `lead_counts`: positive sample counts, in each lead larger on higher rows on the whole.
All inputs are finite; a program needn't handle non-finite values.
Results may differ from the reference program's by a relative error of at most 0.012.
The reference program's roundings to bfloat16 on the way count: a program that leaves them out, or rounds other values in their place, can miss the bound.
Values may be sent and summed in bfloat16 or wider, within the bound.
A program may use at most 256 MiB of HBM per device.

```python
import jax
import jax.numpy as jnp
from jax import lax

D = 768
HEADS = 12
HEAD_DIM = 64
FF = 3072
LEADS = 40
PATCHES = 1728
FRAMES = 32
N_DP = 16
N_SEQ = 2


def draw_lead_counts(key, part):
    key = jax.random.fold_in(key, 5)
    base_counts = jax.random.randint(key, (N_DP, LEADS), 1, 20)
    rising = (N_DP - 1 + 2 * jnp.arange(N_DP, dtype=jnp.int32))[:, None]
    return (base_counts * rising).astype(jnp.int32)


def draw_targets(key, part):
    key = jax.random.fold_in(key, 7)
    shared_key, frame_key, noise_key = jax.random.split(key, 3)
    place = (jnp.arange(PATCHES, dtype=jnp.float32) + 0.5) / PATCHES
    profile = jnp.cos(jnp.pi * place)
    noise = jax.random.normal(noise_key, (FRAMES, PATCHES, D), jnp.float32)
    amplitude = 1.2
    pattern = amplitude * jax.random.normal(shared_key, (D,), jnp.float32)[None, :] + 0.5 * jax.random.normal(frame_key, (FRAMES, D), jnp.float32)
    field = profile[None, :, None] * pattern[:, None, :]
    return jnp.clip(noise + field, -6.0, 6.0).astype(jnp.bfloat16)


def touch_ends(array, stream_key, least, high):
    shape = array.shape
    spot = [jax.random.randint(jax.random.fold_in(stream_key, axis), (), 0, shape[axis]) for axis in range(len(shape))]
    array = array.at[tuple(spot)].set(least)
    longest = shape.index(max(shape))
    spot[longest] = (spot[longest] + 1) % shape[longest]
    return array.at[tuple(spot)].set(high)


def block_scale(key, shape, shards, smallest, largest):
    level, own = 1.0, jax.random.fold_in(key, 6)
    for axis_at, parts in shards:
        draws = jnp.exp(jax.random.uniform(jax.random.fold_in(own, axis_at), (parts,), jnp.float32, smallest / len(shards), largest / len(shards)))
        level = level * jnp.repeat(draws, shape[axis_at] // parts).reshape([-1 if axis == axis_at else 1 for axis in range(len(shape))])
    return level


def centred(stream_key, shape, width, most, cuts=(), kind=jnp.bfloat16):
    drawn = jax.random.normal(stream_key, shape, jnp.float32) * width
    if len(cuts) > 0:
        drawn = block_scale(stream_key, shape, cuts, -0.22, 0.18) * drawn
    return jnp.clip(drawn, min=-most, max=most).astype(kind)


def setup_inputs(seed: int = 0) -> dict:
    arg_keys = jax.random.split(jax.random.key(seed), 16)
    return {
        "frames": centred(arg_keys[0], (FRAMES, PATCHES, D), 1.0, 6.0, ((0, 16), (1, 2))),
        "targets": draw_targets(jax.random.fold_in(arg_keys[15], 71), 0),
        "lead_index": touch_ends(jax.random.randint(arg_keys[2], (FRAMES,), 0, LEADS), jax.random.fold_in(arg_keys[2], 1), 0, LEADS - 1).astype(jnp.int32),
        "lead_counts": draw_lead_counts(jax.random.fold_in(arg_keys[15], 71), 0),
        "first_gain": jnp.clip(1.0 + 0.18 * jax.random.normal(arg_keys[4], (D,), jnp.float32), 0.099609375, 1.8984375).astype(jnp.bfloat16),
        "first_shift": centred(arg_keys[5], (D,), 0.04, 0.19921875, ((0, 2),)),
        "query_weight": centred(arg_keys[6], (D, D), (D // 2) ** -0.5, 0.3125, ((0, 2),)),
        "key_weight": centred(arg_keys[7], (D, D), (D // 2) ** -0.5, 0.3125, ((0, 2),)),
        "value_weight": centred(arg_keys[8], (D, D), D ** -0.5, 0.21875, ((0, 2),)),
        "output_weight": centred(arg_keys[9], (D, D), (max(1, min(D, 55 * D // PATCHES))) ** -0.5, 1.25, ((0, 2),)),
        "second_gain": jnp.clip(1.0 + 0.18 * jax.random.normal(arg_keys[10], (D,), jnp.float32), 0.099609375, 1.8984375).astype(jnp.bfloat16),
        "second_shift": centred(arg_keys[11], (D,), 0.04, 0.19921875, ((0, 2),)),
        "up_weight": centred(arg_keys[12], (D, FF), D ** -0.5, 0.21875, ((0, 2),)),
        "down_weight": centred(arg_keys[13], (FF, D), FF ** -0.5, 0.109375, ((0, 2),)),
        "lead_table": centred(arg_keys[14], (LEADS, D), 0.06, 0.29882812, ((1, 2),)),
    }


@jax.custom_vjp
def low(v):
    return lax.optimization_barrier(v.astype(jnp.bfloat16)).astype(jnp.float32)

@jax.custom_vjp
def low_back(v):
    return v

def low_keep(v):
    return (low(v), None)

def low_pass(kept, grad):
    return (grad,)

def back_keep(v):
    return (v, None)

def back_low(kept, grad):
    return (low(grad),)
low.defvjp(low_keep, low_pass)
low_back.defvjp(back_keep, back_low)

def product(left_side, right_side):
    return jnp.dot(left_side, right_side, precision=lax.Precision.HIGHEST)

def layer_norm(hidden, gain_row, shift_row):
    center = hidden - lax.optimization_barrier(jnp.mean(hidden, axis=-1, keepdims=True))
    inv_std = lax.rsqrt(lax.optimization_barrier(jnp.mean(jnp.square(center), axis=-1, keepdims=True)) + 1e-06)
    return center * inv_std * gain_row + shift_row

def score_block(query_block, key_heads, value_heads):
    scores = low_back(jnp.einsum('qhd,khd->hqk', query_block, key_heads, precision=lax.Precision.HIGHEST) * HEAD_DIM ** (-0.5))
    softmaxed = low(jax.nn.softmax(scores, axis=-1))
    return jnp.einsum('hqk,khd->qhd', softmaxed, value_heads, precision=lax.Precision.HIGHEST)

def frame_forward(params, frame_in, target, lead_number, weight):
    first_gain, first_shift, query_weight, key_weight, value_weight, output_weight, second_gain, second_shift, up_weight, down_weight, lead_table = params
    hidden0 = frame_in + lax.dynamic_index_in_dim(lead_table, lead_number, 0, keepdims=False)
    first_in = low(layer_norm(hidden0, first_gain, first_shift))
    queries = low(low_back(product(first_in, query_weight)))
    keys = low(low_back(product(first_in, key_weight)))
    values = low(low_back(product(first_in, value_weight)))
    key_heads = keys.reshape(PATCHES, HEADS, HEAD_DIM)
    value_heads = values.reshape(PATCHES, HEADS, HEAD_DIM)
    query_blocks = queries.reshape(N_SEQ, PATCHES // N_SEQ, HEADS, HEAD_DIM)
    kept_block = jax.checkpoint(score_block)
    mixed_rows = lax.map(lambda block_rows: kept_block(block_rows, key_heads, value_heads), query_blocks)
    attended = low(low_back(mixed_rows.reshape(PATCHES, D)))
    hidden1 = hidden0 + low_back(product(attended, output_weight))
    second_in = low(layer_norm(hidden1, second_gain, second_shift))
    pre_act = low_back(product(second_in, up_weight))
    activated = low(jax.nn.gelu(pre_act, approximate=False))
    result = hidden1 + low_back(product(activated, down_weight))
    frame_loss = weight * 0.5 * jnp.sum(jnp.square(result - target))
    return (frame_loss, result)

def reference(frames, targets, lead_index, lead_counts, first_gain, first_shift, query_weight, key_weight, value_weight, output_weight, second_gain, second_shift, up_weight, down_weight, lead_table):
    totals = lax.optimization_barrier(jnp.sum(lead_counts.astype(jnp.float32), axis=0))
    lead_weight = jnp.mean(totals) / totals
    frame_weights = lead_weight[lead_index]
    params = tuple((piece.astype(jnp.float32) for piece in (first_gain, first_shift, query_weight, key_weight, value_weight, output_weight, second_gain, second_shift, up_weight, down_weight, lead_table)))
    inputs = frames.astype(jnp.float32)
    targets_wide = targets.astype(jnp.float32)
    kept_frame = jax.checkpoint(frame_forward)

    def total_loss(params_in, inputs_in):

        def add_frame(loss_sum, pieces):
            frame_in, target, lead_number, weight = pieces
            frame_loss, result = kept_frame(params_in, frame_in, target, lead_number, weight)
            return (loss_sum + frame_loss, result)
        loss_sum, results = lax.scan(add_frame, jnp.zeros((), jnp.float32), (inputs_in, targets_wide, lead_index, frame_weights))
        return (loss_sum, results)
    loss_sum, vjp_fn, results = jax.vjp(total_loss, params, inputs, has_aux=True)
    param_grads, input_grads = vjp_fn(jnp.ones((), jnp.float32))
    return (results.astype(jnp.bfloat16), input_grads.astype(jnp.bfloat16), param_grads[0], param_grads[1], param_grads[2], param_grads[3], param_grads[4], param_grads[5], param_grads[6], param_grads[7], param_grads[8], param_grads[9], param_grads[10])
```

```python
import functools

import jax
import jax.numpy as jnp
from jax import lax
from jax.experimental import pallas as pl
from jax.experimental.pallas import tpu as pltpu
from jax.sharding import PartitionSpec as P

HEAD_DIM = 64
PAIR = 128
EPSILON = 1e-06
LOG2E = 1.4426950408889634
SCORE_SCALE = HEAD_DIM**-0.5
EXP2_SCALE = SCORE_SCALE * LOG2E
BF = jnp.bfloat16
F32 = jnp.float32
VMEM_BYTES = 61 * 2**20
SAFE_LOG2 = 100.0


def dot(left, right):
    return jnp.dot(left, right, preferred_element_type=F32)


def dot_t(left, right):
    return lax.dot_general(left, right, (((1,), (1,)), ((), ())), preferred_element_type=F32)


def dot_l(left, right):
    return lax.dot_general(left, right, (((0,), (0,)), ((), ())), preferred_element_type=F32)


def row_mean(x):
    return jnp.mean(x, axis=1, keepdims=True)


def norm_rows(hidden):
    center = hidden - row_mean(hidden)
    inv_std = lax.rsqrt(row_mean(center * center) + EPSILON)
    return center * inv_std, inv_std


def norm_rows_back(grad_out, normed, inv_std, gain):
    scaled = grad_out * gain
    return inv_std * (scaled - row_mean(scaled) - normed * row_mean(scaled * normed))


def gelu_pair(u):
    z = jnp.abs(u) * 0.7071067811865476
    t = 1.0 / (1.0 + 0.3275911 * z)
    e = jnp.exp2(u * u * (-0.5 * LOG2E))
    poly = t * (
        0.127414796
        + t * (-0.142248368 + t * (0.7107068705 + t * (-0.7265760135 + t * 0.5307027145)))
    )
    tail = poly * e
    cdf = jnp.where(u >= 0, 1.0 - tail, tail)
    return u * cdf, cdf + u * (e * 0.3989422804014327)


def params(limit=VMEM_BYTES):
    return pltpu.CompilerParams(vmem_limit_bytes=limit)


def qkv_kernel(
    seq_axis, frame_ref, emb_ref, gain_ref, shift_ref, *rest
):
    own, other = rest[0:3], rest[3:6]
    outs = rest[6:9]
    weights, sems = rest[9:11]
    seq = lax.axis_index(seq_axis)
    half = own[0].shape[0]

    @pl.when(pl.program_id(0) == 0)
    def _():
        copies = []
        for n in range(3):
            for m, (src, place) in enumerate(((own[n], seq), (other[n], 1 - seq))):
                rows = pl.ds(pl.multiple_of(place * half, 128), half)
                copies.append(pltpu.make_async_copy(src, weights.at[n, rows, :], sems.at[n, m]))
        for copy in copies:
            copy.start()
        for copy in copies:
            copy.wait()

    hidden = frame_ref[...].astype(F32) + emb_ref[...]
    normed, _ = norm_rows(hidden)
    first_in = (normed * gain_ref[...] + shift_ref[...]).astype(BF)
    for n in range(3):
        outs[n][...] = dot(first_in, weights[n]).astype(BF)


def qkv_call(frame, emb, gain, shift, own, other, block):
    rows, width = frame.shape
    tile = pl.BlockSpec((block, width), lambda i: (i, 0))
    vec = pl.BlockSpec((1, width), lambda i: (0, 0))
    anys = pl.BlockSpec(memory_space=pl.ANY)
    return pl.pallas_call(
        functools.partial(qkv_kernel, "seq"),
        grid=(rows // block,),
        in_specs=[tile, vec, vec, vec] + [anys] * 6,
        out_specs=[tile] * 3,
        out_shape=[jax.ShapeDtypeStruct((rows, width), BF)] * 3,
        scratch_shapes=[
            pltpu.VMEM((3, width, width), BF),
            pltpu.SemaphoreType.DMA((3, 2)),
        ],
        compiler_params=params(),
    )(frame, emb, gain, shift, *own, *other)


def attend_kernel(block, q_ref, k_ref, v_ref, o_ref, l_ref, keys, values):
    rows = q_ref.shape[0]
    low = lax.broadcasted_iota(jnp.int32, (rows, PAIR), 1) < HEAD_DIM
    k = k_ref[...]
    v = v_ref[...]
    keys[0] = jnp.where(low, k, 0).astype(BF)
    keys[1] = jnp.where(low, 0, k).astype(BF)
    values[0] = jnp.where(low, v, 1).astype(BF)
    values[1] = jnp.where(low, 1, v).astype(BF)

    def longest(x):
        square = x.astype(F32) * x.astype(F32)
        first = jnp.max(jnp.sum(jnp.where(low, square, 0.0), axis=1, keepdims=True))
        second = jnp.max(jnp.sum(jnp.where(low, 0.0, square), axis=1, keepdims=True))
        return jnp.maximum(first, second)

    bound = longest(q_ref[...]) * longest(k)
    fast = bound <= (SAFE_LOG2 / EXP2_SCALE) ** 2
    low_block = lax.broadcasted_iota(jnp.int32, (block, PAIR), 1) < HEAD_DIM

    def run(shifted):
        def body(i, _):
            here = pl.ds(pl.multiple_of(i * block, block), block)
            query = q_ref[here, :]
            mixed, logs = [], []
            for h in range(2):
                scores = dot_t(query, keys[h])
                if shifted:
                    peak = jnp.max(scores, axis=1, keepdims=True)
                    scores = scores - peak
                weight = jnp.exp2(scores * EXP2_SCALE).astype(BF)
                total = dot(weight, values[h])
                turned = pltpu.roll(total, HEAD_DIM, 1)
                mixed.append(total / turned)
                log = jnp.log2(turned) * (1.0 / EXP2_SCALE)
                logs.append(log + peak if shifted else log)
            o_ref[here, :] = jnp.where(low_block, mixed[0], mixed[1]).astype(BF)
            l_ref[here, :] = jnp.where(low_block, logs[0], logs[1])
            return 0

        lax.fori_loop(0, rows // block, body, 0)

    @pl.when(fast)
    def _():
        run(False)

    @pl.when(jnp.logical_not(fast))
    def _():
        run(True)


def attend_call(queries, keys, values, block):
    rows, width = queries.shape
    tile = pl.BlockSpec((rows, PAIR), lambda i: (0, i))
    return pl.pallas_call(
        functools.partial(attend_kernel, block),
        grid=(width // PAIR,),
        in_specs=[tile] * 3,
        out_specs=[tile] * 2,
        out_shape=[
            jax.ShapeDtypeStruct((rows, width), BF),
            jax.ShapeDtypeStruct((rows, width), F32),
        ],
        scratch_shapes=[pltpu.VMEM((2, rows, PAIR), BF)] * 2,
        compiler_params=params(),
    )(queries, keys, values)


def feed_kernel(
    block, steps, seq_axis,
    frame_ref, o_ref, o_full, target_ref, emb_ref, gain_ref, shift_ref, weight_ref,
    wo_own, wo_other, wu_own, wu_other, wd_own, wd_other,
    y_ref, gh_ref, go_ref, sg_ref, ss_ref, grads,
    wo, wu, wd, act, slope, second_in, result_grad, hidden_grad, normed_s, hidden_s, acc, stage,
    sems, out_sems,
):
    i = pl.program_id(0)
    seq = lax.axis_index(seq_axis)
    width = wo.shape[0]
    half = width // 2
    chunks = act.shape[0]

    @pl.when(i == 0)
    def _():
        copies = []
        for m, (place, wo_h, wu_h, wd_h) in enumerate(
            ((seq, wo_own, wu_own, wd_own), (1 - seq, wo_other, wu_other, wd_other))
        ):
            rows = pl.ds(pl.multiple_of(place * half, 128), half)
            copies.append(pltpu.make_async_copy(wo_h, wo.at[rows, :], sems.at[m, 0]))
            for c in range(chunks):
                copies.append(
                    pltpu.make_async_copy(
                        wu_h.at[:, pl.ds(c * width, width)], wu.at[c, rows, :], sems.at[m, 1 + c]
                    )
                )
            for c in range(chunks // 2):
                copies.append(
                    pltpu.make_async_copy(
                        wd_h.at[pl.ds(c * width, width), :],
                        wd.at[place * (chunks // 2) + c],
                        sems.at[m, 1 + chunks + c],
                    )
                )
        for copy in copies:
            copy.start()
        for copy in copies:
            copy.wait()
        sg_ref[...] = jnp.zeros_like(sg_ref)
        ss_ref[...] = jnp.zeros_like(ss_ref)

    @pl.when(i < steps)
    def _():
        rows = pl.ds(pl.multiple_of(i * block, block), block)
        hidden = frame_ref[...].astype(F32) + emb_ref[...] + dot(o_ref[...], wo[...])
        normed, inv_std = norm_rows(hidden)
        normed_s[...] = normed
        second_in[rows, :] = (normed * gain_ref[...] + shift_ref[...]).astype(BF)
        acc[...] = hidden

        def forward(c, _):
            a, s = gelu_pair(dot(second_in[rows, :], wu[c]))
            a = a.astype(BF)
            act[c, rows, :] = a
            slope[c, rows, :] = s.astype(BF)
            acc[...] += dot(a, wd[c])
            return 0

        lax.fori_loop(0, chunks, forward, 0)
        result = acc[...]
        y_ref[...] = result.astype(BF)
        grad = weight_ref[0, 0] * (result - target_ref[...].astype(F32))
        result_grad[rows, :] = grad.astype(BF)
        hidden_s[...] = grad
        acc[...] = jnp.zeros_like(acc)

        def backward(c, _):
            back = dot_t(result_grad[rows, :], wd[c])
            back = (back * slope[c, rows, :].astype(F32)).astype(BF)
            slope[c, rows, :] = back
            acc[...] += dot_t(back, wu[c])
            return 0

        lax.fori_loop(0, chunks, backward, 0)
        grad = acc[...]
        normed = normed_s[...]
        ss_ref[...] += jnp.sum(grad, axis=0, keepdims=True)
        sg_ref[...] += jnp.sum(grad * normed, axis=0, keepdims=True)
        grad = hidden_s[...] + norm_rows_back(grad, normed, inv_std, gain_ref[...])
        gh_ref[...] = grad
        grad = grad.astype(BF)
        hidden_grad[rows, :] = grad
        go_ref[...] = dot_t(grad, wo[...]).astype(BF)

    def out_copies(n):
        slot = n % 2
        if n < chunks:
            at = grads.at[n // (chunks // 2), pl.ds((n % (chunks // 2)) * width, width), :]
            return [pltpu.make_async_copy(stage.at[slot], at, out_sems.at[slot, 0])]
        base = (chunks // 2) * width + (n - chunks) * half
        return [
            pltpu.make_async_copy(
                stage.at[slot, pl.ds(h * half, half), :],
                grads.at[h, pl.ds(base, half), :],
                out_sems.at[slot, h],
            )
            for h in range(2)
        ]

    last = 2 * chunks
    for n in range(last + 1):

        @pl.when(i == steps + n)
        def _():
            if n >= 2:
                for copy in out_copies(n - 2):
                    copy.wait()
            if n < chunks:
                term = dot_l(act[n], result_grad[...])
            elif n < last:
                term = dot_l(second_in[...], slope[n - chunks])
            else:
                term = dot_l(o_full[...], hidden_grad[...])
            stage[n % 2] = term.astype(BF)
            for copy in out_copies(n):
                copy.start()
            if n == last:
                for m in (n - 1, n):
                    for copy in out_copies(m):
                        copy.wait()


def feed_call(frame, attended, target, emb, gain, shift, weight, halves, grad_rows, block):
    rows, width = frame.shape
    chunks = halves[2].shape[1] // width
    steps = rows // block
    tile = pl.BlockSpec((block, width), lambda i: (jnp.minimum(i, steps - 1), 0))
    whole = pl.BlockSpec((rows, width), lambda i: (0, 0))
    vec = pl.BlockSpec((1, width), lambda i: (0, 0))
    anys = pl.BlockSpec(memory_space=pl.ANY)
    return pl.pallas_call(
        functools.partial(feed_kernel, block, steps, "seq"),
        grid=(steps + 2 * chunks + 1,),
        in_specs=[tile, tile, whole, tile, vec, vec, vec, pl.BlockSpec(memory_space=pltpu.SMEM)]
        + [anys] * 6,
        out_specs=[tile, tile, tile, vec, vec, anys],
        out_shape=[
            jax.ShapeDtypeStruct((rows, width), BF),
            jax.ShapeDtypeStruct((rows, width), F32),
            jax.ShapeDtypeStruct((rows, width), BF),
            jax.ShapeDtypeStruct((1, width), F32),
            jax.ShapeDtypeStruct((1, width), F32),
            jax.ShapeDtypeStruct((2, grad_rows, width), BF),
        ],
        scratch_shapes=[
            pltpu.VMEM((width, width), BF),
            pltpu.VMEM((chunks, width, width), BF),
            pltpu.VMEM((chunks, width, width), BF),
            pltpu.VMEM((chunks, rows, width), BF),
            pltpu.VMEM((chunks, rows, width), BF),
            pltpu.VMEM((rows, width), BF),
            pltpu.VMEM((rows, width), BF),
            pltpu.VMEM((rows, width), BF),
            pltpu.VMEM((block, width), F32),
            pltpu.VMEM((block, width), F32),
            pltpu.VMEM((block, width), F32),
            pltpu.VMEM((2, width, width), BF),
            pltpu.SemaphoreType.DMA((2, 1 + chunks + chunks // 2)),
            pltpu.SemaphoreType.DMA((2, 2)),
        ],
        compiler_params=params(),
    )(frame, attended, attended, target, emb, gain, shift, weight, *halves)


def split_three(x):
    first = x.astype(BF)
    rest = x - first.astype(F32)
    second = rest.astype(BF)
    rest = rest - second.astype(F32)
    return first, second, rest.astype(BF)


def attend_back_kernel(
    block, q_ref, k_ref, v_ref, g_ref, o_ref, l_ref, gq_ref, gk_ref, gv_ref, qm, km, vm, gm, acc
):
    rows = q_ref.shape[0]
    lane = lax.broadcasted_iota(jnp.int32, (rows, PAIR), 1)
    q, k, v, g = q_ref[...], k_ref[...], v_ref[...], g_ref[...]
    product = g.astype(F32) * o_ref[...].astype(F32)
    logs = l_ref[...]
    for h in range(2):
        inside = (lane < HEAD_DIM) if h == 0 else (lane >= HEAD_DIM)
        base = HEAD_DIM * (1 - h)
        inner = -jnp.sum(jnp.where(inside, product, 0.0), axis=1, keepdims=True)
        log = -jnp.max(jnp.where(inside, logs, -jnp.inf), axis=1, keepdims=True)

        def extend(x, terms):
            tail = jnp.zeros_like(x)
            for n, term in enumerate(terms):
                tail = jnp.where(lane == base + n, term, tail)
            return jnp.where(inside, x, tail)

        ones = jnp.where((lane >= base) & (lane < base + 3), 1.0, 0.0).astype(BF)
        qm[h] = extend(q, split_three(log))
        gm[h] = extend(g, split_three(inner))
        km[h] = jnp.where(inside, k, ones)
        vm[h] = jnp.where(inside, v, ones)
    acc[...] = jnp.zeros_like(acc)
    low_block = lax.broadcasted_iota(jnp.int32, (block, PAIR), 1) < HEAD_DIM

    def body(i, _):
        here = pl.ds(pl.multiple_of(i * block, block), block)
        value_terms, key_terms = [], []
        turned = k_ref[here, :].T
        for h in range(2):
            prob = jnp.exp2(EXP2_SCALE * dot_t(km[h, here, :], qm[h]))
            score = (prob * dot_t(vm[h, here, :], gm[h])).astype(BF)
            value_terms.append(dot(prob.astype(BF), g_ref[...]))
            key_terms.append(dot(score, q_ref[...]))
            acc[h] += dot(turned, score)
        gv_ref[here, :] = jnp.where(low_block, value_terms[0], value_terms[1]).astype(BF)
        gk_ref[here, :] = (
            SCORE_SCALE * jnp.where(low_block, key_terms[0], key_terms[1])
        ).astype(BF)
        return 0

    lax.fori_loop(0, rows // block, body, 0)
    gq_ref[...] = (SCORE_SCALE * jnp.where(lane < HEAD_DIM, acc[0].T, acc[1].T)).astype(BF)


def attend_back_call(queries, keys, values, grad, attended, logs, block):
    rows, width = queries.shape
    tile = pl.BlockSpec((rows, PAIR), lambda i: (0, i))
    return pl.pallas_call(
        functools.partial(attend_back_kernel, block),
        grid=(width // PAIR,),
        in_specs=[tile] * 6,
        out_specs=[tile] * 3,
        out_shape=[jax.ShapeDtypeStruct((rows, width), BF)] * 3,
        scratch_shapes=[pltpu.VMEM((2, rows, PAIR), BF)] * 4 + [pltpu.VMEM((2, PAIR, rows), F32)],
        compiler_params=params(),
    )(queries, keys, values, grad, attended, logs)


def qkv_back_kernel(
    block, steps, seq_axis,
    frame_ref, gh_ref, gq_ref, gk_ref, gv_ref, emb_ref, gain_ref, shift_ref, *rest
):
    own, other = rest[0:3], rest[3:6]
    gi_ref, sg_ref, ss_ref, st_ref, grads = rest[6:11]
    weights, first_in, sems = rest[11:14]
    parts = (gq_ref, gk_ref, gv_ref)
    i = pl.program_id(0)
    seq = lax.axis_index(seq_axis)
    half = own[0].shape[0]

    @pl.when(i == 0)
    def _():
        copies = []
        for n in range(3):
            for m, (src, place) in enumerate(((own[n], seq), (other[n], 1 - seq))):
                rows = pl.ds(pl.multiple_of(place * half, 128), half)
                copies.append(pltpu.make_async_copy(src, weights.at[n, rows, :], sems.at[n, m]))
        for copy in copies:
            copy.start()
        for copy in copies:
            copy.wait()
        for ref in (sg_ref, ss_ref, st_ref):
            ref[...] = jnp.zeros_like(ref)

    @pl.when(i < steps)
    def _():
        rows = pl.ds(pl.multiple_of(i * block, block), block)
        hidden = frame_ref[...].astype(F32) + emb_ref[...]
        normed, inv_std = norm_rows(hidden)
        first_in[rows, :] = (normed * gain_ref[...] + shift_ref[...]).astype(BF)
        grad = dot_t(gq_ref[rows, :], weights[0])
        grad += dot_t(gk_ref[rows, :], weights[1])
        grad += dot_t(gv_ref[rows, :], weights[2])
        ss_ref[...] += jnp.sum(grad, axis=0, keepdims=True)
        sg_ref[...] += jnp.sum(grad * normed, axis=0, keepdims=True)
        grad = gh_ref[...] + norm_rows_back(grad, normed, inv_std, gain_ref[...])
        st_ref[...] += jnp.sum(grad, axis=0, keepdims=True)
        gi_ref[...] = grad.astype(BF)

    for n in range(3):

        @pl.when(i == steps + n)
        def _():
            term = dot_l(first_in[...], parts[n][...]).astype(BF)
            grads[0, pl.ds(n * half, half), :] = term[:half]
            grads[1, pl.ds(n * half, half), :] = term[half:]


def qkv_back_call(frame, hidden_grad, gq, gk, gv, emb, gain, shift, own, other, block):
    rows, width = frame.shape
    steps = rows // block
    tile = pl.BlockSpec((block, width), lambda i: (jnp.minimum(i, steps - 1), 0))
    whole = pl.BlockSpec((rows, width), lambda i: (0, 0))
    vec = pl.BlockSpec((1, width), lambda i: (0, 0))
    anys = pl.BlockSpec(memory_space=pl.ANY)
    grad_shape = (2, 3 * (width // 2), width)
    return pl.pallas_call(
        functools.partial(qkv_back_kernel, block, steps, "seq"),
        grid=(steps + 3,),
        in_specs=[tile, tile, whole, whole, whole, vec, vec, vec] + [anys] * 6,
        out_specs=[tile, vec, vec, vec, pl.BlockSpec(grad_shape, lambda i: (0, 0, 0))],
        out_shape=[jax.ShapeDtypeStruct((rows, width), BF)]
        + [jax.ShapeDtypeStruct((1, width), F32)] * 3
        + [jax.ShapeDtypeStruct(grad_shape, BF)],
        scratch_shapes=[
            pltpu.VMEM((3, width, width), BF),
            pltpu.VMEM((rows, width), BF),
            pltpu.SemaphoreType.DMA((3, 2)),
        ],
        compiler_params=params(),
    )(frame, hidden_grad, gq, gk, gv, emb, gain, shift, *own, *other)


def body(
    frames, targets, lead_index, lead_counts,
    first_gain, first_shift, query_weight, key_weight, value_weight, output_weight,
    second_gain, second_shift, up_weight, down_weight, lead_table,
):
    seq = lax.axis_index("seq")
    swap = [(0, 1), (1, 0)]

    def trade(x):
        return lax.ppermute(x, "seq", swap)

    def pick(x, which):
        return lax.dynamic_index_in_dim(x, which, 0, keepdims=False)

    def order(mine, theirs, axis):
        return jnp.where(
            seq == 0,
            jnp.concatenate([mine, theirs], axis),
            jnp.concatenate([theirs, mine], axis),
        )

    rows, width = frames.shape[1] * 2, frames.shape[2]
    half = width // 2
    rows_here = jnp.take(lead_table, lead_index, axis=0)
    vectors = jnp.stack([first_gain, first_shift, second_gain, second_shift])
    theirs = trade(jnp.concatenate([vectors, pick(rows_here, 1 - seq)[None]]))
    mine = jnp.concatenate([vectors, pick(rows_here, seq)[None]])
    table = order(mine, theirs, 1).astype(F32)
    gain1, shift1, gain2, shift2, emb = (table[n : n + 1] for n in range(5))

    early = (query_weight, key_weight, value_weight)
    late = (output_weight, up_weight, down_weight)
    early_other = tuple(trade(w) for w in early)
    frame = jnp.concatenate([pick(frames, seq), trade(pick(frames, 1 - seq))])
    late_other = tuple(trade(w) for w in late)
    target = jnp.concatenate([pick(targets, seq), trade(pick(targets, 1 - seq))])

    totals = lax.psum(lead_counts[0].astype(F32), "dp")
    lead_weight = jnp.mean(totals) / totals
    lead = pick(lead_index, seq)
    frame_weight = pick(lead_weight, lead).reshape(1, 1)

    queries, keys, values = qkv_call(frame, emb, gain1, shift1, early, early_other, rows // 4)
    attended, logs = attend_call(queries, keys, values, rows // 2)
    halves = tuple(w for pair in zip(late, late_other) for w in pair)
    result, hidden_grad, attended_grad, sg2, ss2, grads = feed_call(
        frame, attended, target, emb, gain2, shift2, frame_weight, halves, 9 * half, rows // 6
    )
    gq, gk, gv = attend_back_call(
        queries, keys, values, attended_grad, attended, logs, rows // 2
    )
    input_grad, sg1, ss1, st, grads_early = qkv_back_call(
        frame, hidden_grad, gq, gk, gv, emb, gain1, shift1, early, early_other, rows // 4
    )

    def place(x):
        mine, theirs = x[: rows // 2], trade(x[rows // 2 :])
        return jnp.where(
            seq == 0, jnp.stack([mine, theirs]), jnp.stack([theirs, mine])
        )

    def reduce(x):
        summed = pick(x, seq).astype(F32) + trade(pick(x, 1 - seq)).astype(F32)
        return lax.psum(summed.astype(BF), "dp")

    late_sum = reduce(grads).astype(F32)
    early_sum = reduce(grads_early).astype(F32)
    rows_ff = 4 * half
    down_grad = late_sum[:rows_ff]
    up_grad = late_sum[rows_ff : 2 * rows_ff].reshape(4, half, width)
    up_grad = jnp.moveaxis(up_grad, 0, 1).reshape(half, 4 * width)
    output_grad = late_sum[2 * rows_ff :]

    hot = (jnp.arange(lead_table.shape[0]) == lead).astype(F32)
    small = jnp.concatenate([sg1, ss1, sg2, ss2, hot[:, None] * st]).reshape(-1, 2, half)
    small = small.transpose(1, 0, 2)
    small = lax.psum(pick(small, seq) + trade(pick(small, 1 - seq)), "dp")
    return (
        place(result), place(input_grad), small[0], small[1],
        early_sum[:half], early_sum[half : 2 * half], early_sum[2 * half :], output_grad,
        small[2], small[3], up_grad, down_grad, small[4:],
    )


def solution(mesh):
    weight = P("seq", None)
    vector = P("seq")
    batch = P("dp", "seq", None)
    table = P(None, "seq")
    return jax.shard_map(
        body,
        mesh=mesh,
        in_specs=(
            batch, batch, P("dp"), P("dp", None), vector, vector, weight, weight, weight, weight,
            vector, vector, weight, weight, table,
        ),
        out_specs=(
            batch, batch, vector, vector, weight, weight, weight, weight, vector, vector, weight,
            weight, table,
        ),
        check_vma=False,
    )
```

```python
import functools

import jax
import jax.numpy as jnp
from jax import lax
from jax.experimental import pallas as pl
from jax.experimental.pallas import tpu as pltpu
from jax.sharding import PartitionSpec as P

HEAD_DIM = 64
PAIR = 128
EPSILON = 1e-06
LOG2E = 1.4426950408889634
SCORE_SCALE = HEAD_DIM**-0.5
EXP2_SCALE = SCORE_SCALE * LOG2E
BF = jnp.bfloat16
F32 = jnp.float32
VMEM_BYTES = 61 * 2**20
SAFE_LOG2 = 100.0


def dot(left, right):
    return jnp.dot(left, right, preferred_element_type=F32)


def dot_t(left, right):
    return lax.dot_general(left, right, (((1,), (1,)), ((), ())), preferred_element_type=F32)


def dot_l(left, right):
    return lax.dot_general(left, right, (((0,), (0,)), ((), ())), preferred_element_type=F32)


def row_mean(x):
    return jnp.mean(x, axis=1, keepdims=True)


def norm_rows(hidden):
    center = hidden - row_mean(hidden)
    inv_std = lax.rsqrt(row_mean(center * center) + EPSILON)
    return center * inv_std, inv_std


def norm_rows_back(grad_out, normed, inv_std, gain):
    scaled = grad_out * gain
    return inv_std * (scaled - row_mean(scaled) - normed * row_mean(scaled * normed))


def gelu_pair(u):
    z = jnp.abs(u) * 0.7071067811865476
    t = 1.0 / (1.0 + 0.3275911 * z)
    e = jnp.exp2(u * u * (-0.5 * LOG2E))
    poly = t * (
        0.127414796
        + t * (-0.142248368 + t * (0.7107068705 + t * (-0.7265760135 + t * 0.5307027145)))
    )
    tail = poly * e
    cdf = jnp.where(u >= 0, 1.0 - tail, tail)
    return u * cdf, cdf + u * (e * 0.3989422804014327)


def params(limit=VMEM_BYTES):
    return pltpu.CompilerParams(vmem_limit_bytes=limit)


def reduce_parts(rows, dp):
    bits = dp.bit_length() - 1
    unit = 16 * dp
    units = rows // unit
    middle = list(range(1, bits))
    orders = [["seq"] + middle, middle + ["seq"], middle[1:] + ["seq"] + middle[:1]]
    sizes = [(units + 2 - n) // 3 for n in range(3)]
    parts, base = [], 0
    for size, order in zip(sizes, orders):
        if size > 0:
            parts.append((base, size * unit, [0] + order))
            base += size * unit
    return parts


def padded_rows(rows, dp):
    unit = 16 * dp
    return -(-rows // unit) * unit


class Place:
    def __init__(self, dp):
        self.bits = dp.bit_length() - 1
        self.dp = lax.axis_index("dp")
        self.seq = lax.axis_index("seq")

    def bit(self, key):
        return self.seq if key == "seq" else (self.dp // (1 << key)) % 2

    def partner(self, key):
        if key == "seq":
            return (self.dp, 1 - self.seq)
        return (self.dp + (1 << key) * (1 - 2 * self.bit(key)), self.seq)

    def meet(self):
        barrier = pltpu.get_barrier_semaphore()
        keys = ["seq"] + list(range(self.bits))
        for key in keys:
            pl.semaphore_signal(
                barrier, inc=1, device_id=self.partner(key), device_id_type=pl.DeviceIdType.MESH
            )
        pl.semaphore_wait(barrier, len(keys))


def reduce_scratch(parts, width):
    shapes = []
    for _, rows, order in parts:
        lead, n = 2, rows // 2
        shapes += [pltpu.VMEM((2, n, width), BF), pltpu.VMEM((2, n, width), BF)]
        for key in order[1:]:
            lead, n = (1, n) if key == "seq" else (lead, n // 2)
            shapes.append(pltpu.VMEM((lead, n, width), BF))
    steps = max(len(order) for _, _, order in parts)
    shapes += [pltpu.SemaphoreType.DMA((len(parts), 2 * steps, 2))]
    shapes += [pltpu.SemaphoreType.DMA((len(parts), 2))]
    return shapes


class Reducer:
    def __init__(self, place, part, index, source, out, refs, sems, local_sems):
        self.place, self.index, self.source, self.out = place, index, source, out
        self.base, self.rows, self.order = part
        self.acc, self.landing = refs[0], refs[1:]
        self.sems, self.local = sems, local_sems
        self.copies = {}
        half = self.rows // 2
        seq = place.seq
        off, n, cut = 0, half, False
        self.plan = []
        for key in self.order[1:]:
            if key == "seq":
                leave = (pl.ds(1 - seq, 1), pl.ds(off, n))
                cut = True
                stay = (pl.ds(seq, 1), pl.ds(off, n))
            else:
                n //= 2
                bit = place.bit(key)
                lead = pl.ds(seq, 1) if cut else slice(None)
                leave = (lead, pl.ds(self.row(off + (1 - bit) * n), n))
                off = self.row(off + bit * n)
                stay = (lead, pl.ds(off, n))
            self.plan.append((key, leave, stay))
        self.final_off, self.final_rows = off, n

    @staticmethod
    def row(x):
        return x if isinstance(x, int) else pl.multiple_of(x, 16)

    def absolute(self, off):
        return pl.multiple_of(self.base + self.place.bit(0) * (self.rows // 2) + off, 16)

    def remote(self, step, src, dst, key):
        return pltpu.make_async_remote_copy(
            src_ref=src,
            dst_ref=dst,
            send_sem=self.sems.at[self.index, step, 0],
            recv_sem=self.sems.at[self.index, step, 1],
            device_id=self.place.partner(key),
            device_id_type=pl.DeviceIdType.MESH,
        )

    def scatter(self, step):
        if step == 0:
            half = self.rows // 2
            there = pl.multiple_of(self.base + (1 - self.place.bit(0)) * half, 16)
            return self.remote(0, self.source.at[:, pl.ds(there, half), :], self.landing[0], 0)
        key, leave, _ = self.plan[step - 1]
        return self.remote(step, self.acc.at[leave[0], leave[1], :], self.landing[step], key)

    def keep_copy(self):
        half = self.rows // 2
        here = pl.multiple_of(self.base + self.place.bit(0) * half, 16)
        return pltpu.make_async_copy(
            self.source.at[:, pl.ds(here, half), :], self.acc, self.local.at[self.index, 0]
        )

    def final_copy(self):
        return pltpu.make_async_copy(
            self.acc.at[self.place.seq, pl.ds(self.final_off, self.final_rows), :],
            self.out.at[pl.ds(self.absolute(self.final_off), self.final_rows), :],
            self.local.at[self.index, 1],
        )

    def gather(self, j):
        keys = [key for key in reversed(self.order) if key != "seq"]
        off, n = self.absolute(self.final_off), self.final_rows
        for key in keys[:j]:
            off = off - self.place.bit(key) * n
            n *= 2
        off = pl.multiple_of(off, 16)
        if j == 0:
            src = self.acc.at[self.place.seq, pl.ds(self.final_off, n), :]
        else:
            src = self.out.at[pl.ds(off, n), :]
        return self.remote(len(self.order) + j, src, self.out.at[pl.ds(off, n), :], keys[j])

    def add(self, step):
        landing = self.landing[step]
        if step == 0:
            lead, rows = (0, 2), pl.ds(0, self.rows // 2)
            first = 0
        else:
            _, _, stay = self.plan[step - 1]
            first = stay[0].start if isinstance(stay[0], pl.Slice) else 0
            lead, rows = (0, landing.shape[0]), stay[1]
        n = landing.shape[1]
        size = 32 if n % 32 == 0 else 16
        start = rows.start
        for m in range(lead[1]):

            def some(i, _):
                at = pl.multiple_of(i * size, size)
                here = pl.ds(pl.multiple_of(start + at, 16), size)
                self.acc[first + m, here, :] = (
                    self.acc[first + m, here, :] + landing[m, pl.ds(at, size), :]
                )
                return 0

            lax.fori_loop(0, n // size, some, 0)

    def events(self):
        steps = len(self.order)
        gathers = self.place.bits

        def begin():
            self.keep_copy().start()
            self.scatter(0).start()

        def middle(step):
            def run():
                if step == 1:
                    self.keep_copy().wait()
                self.scatter(step - 1).wait_recv()
                self.add(step - 1)
                if step < steps:
                    self.scatter(step).start()
                else:
                    self.final_copy().start()
                    self.gather(0).start()

            return run

        def onward(j):
            def run():
                if j == 1:
                    self.final_copy().wait()
                self.gather(j - 1).wait_recv()
                self.gather(j).start()

            return run

        def finish():
            self.gather(gathers - 1).wait_recv()
            for step in range(steps):
                self.scatter(step).wait_send()
            for j in range(gathers):
                self.gather(j).wait_send()

        return (
            [begin]
            + [middle(step) for step in range(1, steps + 1)]
            + [onward(j) for j in range(1, gathers)]
            + [finish]
        )


def reducers(place, parts, source, out, refs):
    sems, local_sems = refs[-2:]
    made, at = [], 0
    for index, part in enumerate(parts):
        count = 1 + len(part[2])
        made.append(Reducer(place, part, index, source, out, refs[at : at + count], sems, local_sems))
        at += count
    return made


def spread(count, slots, weights=None):
    weights = weights or [1.0] * (count - 1)
    total, at, out = sum(weights), 0.0, [0]
    for weight in weights:
        at += weight
        out.append(min(slots - 1, round(at / total * (slots - 1))))
    return out


def qkv_kernel(
    seq_axis, frame_ref, emb_ref, gain_ref, shift_ref, *rest
):
    own, other = rest[0:3], rest[3:6]
    outs = rest[6:9]
    weights, sems = rest[9:11]
    seq = lax.axis_index(seq_axis)
    half = own[0].shape[0]

    @pl.when(pl.program_id(0) == 0)
    def _():
        copies = []
        for n in range(3):
            for m, (src, place) in enumerate(((own[n], seq), (other[n], 1 - seq))):
                rows = pl.ds(pl.multiple_of(place * half, 128), half)
                copies.append(pltpu.make_async_copy(src, weights.at[n, rows, :], sems.at[n, m]))
        for copy in copies:
            copy.start()
        for copy in copies:
            copy.wait()

    hidden = frame_ref[...].astype(F32) + emb_ref[...]
    normed, _ = norm_rows(hidden)
    first_in = (normed * gain_ref[...] + shift_ref[...]).astype(BF)
    for n in range(3):
        outs[n][...] = dot(first_in, weights[n]).astype(BF)


def qkv_call(frame, emb, gain, shift, own, other, block):
    rows, width = frame.shape
    tile = pl.BlockSpec((block, width), lambda i: (i, 0))
    vec = pl.BlockSpec((1, width), lambda i: (0, 0))
    anys = pl.BlockSpec(memory_space=pl.ANY)
    return pl.pallas_call(
        functools.partial(qkv_kernel, "seq"),
        grid=(rows // block,),
        in_specs=[tile, vec, vec, vec] + [anys] * 6,
        out_specs=[tile] * 3,
        out_shape=[jax.ShapeDtypeStruct((rows, width), BF)] * 3,
        scratch_shapes=[
            pltpu.VMEM((3, width, width), BF),
            pltpu.SemaphoreType.DMA((3, 2)),
        ],
        compiler_params=params(),
    )(frame, emb, gain, shift, *own, *other)


def attend_kernel(block, q_ref, k_ref, v_ref, o_ref, l_ref, keys, values):
    rows = q_ref.shape[0]
    low = lax.broadcasted_iota(jnp.int32, (rows, PAIR), 1) < HEAD_DIM
    k = k_ref[...]
    v = v_ref[...]
    keys[0] = jnp.where(low, k, 0).astype(BF)
    keys[1] = jnp.where(low, 0, k).astype(BF)
    values[0] = jnp.where(low, v, 1).astype(BF)
    values[1] = jnp.where(low, 1, v).astype(BF)

    def longest(x):
        square = x.astype(F32) * x.astype(F32)
        first = jnp.max(jnp.sum(jnp.where(low, square, 0.0), axis=1, keepdims=True))
        second = jnp.max(jnp.sum(jnp.where(low, 0.0, square), axis=1, keepdims=True))
        return jnp.maximum(first, second)

    bound = longest(q_ref[...]) * longest(k)
    fast = bound <= (SAFE_LOG2 / EXP2_SCALE) ** 2
    low_block = lax.broadcasted_iota(jnp.int32, (block, PAIR), 1) < HEAD_DIM

    def run(shifted):
        def body(i, _):
            here = pl.ds(pl.multiple_of(i * block, block), block)
            query = q_ref[here, :]
            mixed, logs = [], []
            for h in range(2):
                scores = dot_t(query, keys[h])
                if shifted:
                    peak = jnp.max(scores, axis=1, keepdims=True)
                    scores = scores - peak
                weight = jnp.exp2(scores * EXP2_SCALE).astype(BF)
                total = dot(weight, values[h])
                turned = pltpu.roll(total, HEAD_DIM, 1)
                mixed.append(total / turned)
                log = jnp.log2(turned) * (1.0 / EXP2_SCALE)
                logs.append(log + peak if shifted else log)
            o_ref[here, :] = jnp.where(low_block, mixed[0], mixed[1]).astype(BF)
            l_ref[here, :] = jnp.where(low_block, logs[0], logs[1])
            return 0

        lax.fori_loop(0, rows // block, body, 0)

    @pl.when(fast)
    def _():
        run(False)

    @pl.when(jnp.logical_not(fast))
    def _():
        run(True)


def attend_call(queries, keys, values, block):
    rows, width = queries.shape
    tile = pl.BlockSpec((rows, PAIR), lambda i: (0, i))
    return pl.pallas_call(
        functools.partial(attend_kernel, block),
        grid=(width // PAIR,),
        in_specs=[tile] * 3,
        out_specs=[tile] * 2,
        out_shape=[
            jax.ShapeDtypeStruct((rows, width), BF),
            jax.ShapeDtypeStruct((rows, width), F32),
        ],
        scratch_shapes=[pltpu.VMEM((2, rows, PAIR), BF)] * 2,
        compiler_params=params(),
    )(queries, keys, values)


def feed_kernel(
    block, steps, seq_axis,
    frame_ref, o_ref, o_full, target_ref, emb_ref, gain_ref, shift_ref, weight_ref,
    wo_own, wo_other, wu_own, wu_other, wd_own, wd_other,
    y_ref, gh_ref, go_ref, sg_ref, ss_ref, grads,
    wo, wu, wd, act, slope, second_in, result_grad, hidden_grad, normed_s, hidden_s, acc, stage,
    sems, out_sems,
):
    i = pl.program_id(0)
    seq = lax.axis_index(seq_axis)
    width = wo.shape[0]
    half = width // 2
    chunks = act.shape[0]

    @pl.when(i == 0)
    def _():
        copies = []
        for m, (place, wo_h, wu_h, wd_h) in enumerate(
            ((seq, wo_own, wu_own, wd_own), (1 - seq, wo_other, wu_other, wd_other))
        ):
            rows = pl.ds(pl.multiple_of(place * half, 128), half)
            copies.append(pltpu.make_async_copy(wo_h, wo.at[rows, :], sems.at[m, 0]))
            for c in range(chunks):
                copies.append(
                    pltpu.make_async_copy(
                        wu_h.at[:, pl.ds(c * width, width)], wu.at[c, rows, :], sems.at[m, 1 + c]
                    )
                )
            for c in range(chunks // 2):
                copies.append(
                    pltpu.make_async_copy(
                        wd_h.at[pl.ds(c * width, width), :],
                        wd.at[place * (chunks // 2) + c],
                        sems.at[m, 1 + chunks + c],
                    )
                )
        for copy in copies:
            copy.start()
        for copy in copies:
            copy.wait()
        sg_ref[...] = jnp.zeros_like(sg_ref)
        ss_ref[...] = jnp.zeros_like(ss_ref)
        spare = grads.shape[1] - (2 * chunks + 1) * half
        if spare > 0:
            stage[0] = jnp.zeros_like(stage[0])
            fills = [
                pltpu.make_async_copy(
                    stage.at[0, pl.ds(0, spare), :],
                    grads.at[h, pl.ds((2 * chunks + 1) * half, spare), :],
                    out_sems.at[0, h],
                )
                for h in range(2)
            ]
            for fill in fills:
                fill.start()
            for fill in fills:
                fill.wait()

    @pl.when(i < steps)
    def _():
        rows = pl.ds(pl.multiple_of(i * block, block), block)
        hidden = frame_ref[...].astype(F32) + emb_ref[...] + dot(o_ref[...], wo[...])
        normed, inv_std = norm_rows(hidden)
        normed_s[...] = normed
        second_in[rows, :] = (normed * gain_ref[...] + shift_ref[...]).astype(BF)
        acc[...] = hidden

        def forward(c, _):
            a, s = gelu_pair(dot(second_in[rows, :], wu[c]))
            a = a.astype(BF)
            act[c, rows, :] = a
            slope[c, rows, :] = s.astype(BF)
            acc[...] += dot(a, wd[c])
            return 0

        lax.fori_loop(0, chunks, forward, 0)
        result = acc[...]
        y_ref[...] = result.astype(BF)
        grad = weight_ref[0, 0] * (result - target_ref[...].astype(F32))
        result_grad[rows, :] = grad.astype(BF)
        hidden_s[...] = grad
        acc[...] = jnp.zeros_like(acc)

        def backward(c, _):
            back = dot_t(result_grad[rows, :], wd[c])
            back = (back * slope[c, rows, :].astype(F32)).astype(BF)
            slope[c, rows, :] = back
            acc[...] += dot_t(back, wu[c])
            return 0

        lax.fori_loop(0, chunks, backward, 0)
        grad = acc[...]
        normed = normed_s[...]
        ss_ref[...] += jnp.sum(grad, axis=0, keepdims=True)
        sg_ref[...] += jnp.sum(grad * normed, axis=0, keepdims=True)
        grad = hidden_s[...] + norm_rows_back(grad, normed, inv_std, gain_ref[...])
        gh_ref[...] = grad
        grad = grad.astype(BF)
        hidden_grad[rows, :] = grad
        go_ref[...] = dot_t(grad, wo[...]).astype(BF)

    def out_copies(n):
        slot = n % 2
        if n < chunks:
            at = grads.at[n // (chunks // 2), pl.ds((n % (chunks // 2)) * width, width), :]
            return [pltpu.make_async_copy(stage.at[slot], at, out_sems.at[slot, 0])]
        base = (chunks // 2) * width + (n - chunks) * half
        return [
            pltpu.make_async_copy(
                stage.at[slot, pl.ds(h * half, half), :],
                grads.at[h, pl.ds(base, half), :],
                out_sems.at[slot, h],
            )
            for h in range(2)
        ]

    last = 2 * chunks
    for n in range(last + 1):

        @pl.when(i == steps + n)
        def _():
            if n >= 2:
                for copy in out_copies(n - 2):
                    copy.wait()
            if n < chunks:
                term = dot_l(act[n], result_grad[...])
            elif n < last:
                term = dot_l(second_in[...], slope[n - chunks])
            else:
                term = dot_l(o_full[...], hidden_grad[...])
            stage[n % 2] = term.astype(BF)
            for copy in out_copies(n):
                copy.start()
            if n == last:
                for m in (n - 1, n):
                    for copy in out_copies(m):
                        copy.wait()


def feed_call(frame, attended, target, emb, gain, shift, weight, halves, grad_rows, block):
    rows, width = frame.shape
    chunks = halves[2].shape[1] // width
    steps = rows // block
    tile = pl.BlockSpec((block, width), lambda i: (jnp.minimum(i, steps - 1), 0))
    whole = pl.BlockSpec((rows, width), lambda i: (0, 0))
    vec = pl.BlockSpec((1, width), lambda i: (0, 0))
    anys = pl.BlockSpec(memory_space=pl.ANY)
    return pl.pallas_call(
        functools.partial(feed_kernel, block, steps, "seq"),
        grid=(steps + 2 * chunks + 1,),
        in_specs=[tile, tile, whole, tile, vec, vec, vec, pl.BlockSpec(memory_space=pltpu.SMEM)]
        + [anys] * 6,
        out_specs=[tile, tile, tile, vec, vec, anys],
        out_shape=[
            jax.ShapeDtypeStruct((rows, width), BF),
            jax.ShapeDtypeStruct((rows, width), F32),
            jax.ShapeDtypeStruct((rows, width), BF),
            jax.ShapeDtypeStruct((1, width), F32),
            jax.ShapeDtypeStruct((1, width), F32),
            jax.ShapeDtypeStruct((2, grad_rows, width), BF),
        ],
        scratch_shapes=[
            pltpu.VMEM((width, width), BF),
            pltpu.VMEM((chunks, width, width), BF),
            pltpu.VMEM((chunks, width, width), BF),
            pltpu.VMEM((chunks, rows, width), BF),
            pltpu.VMEM((chunks, rows, width), BF),
            pltpu.VMEM((rows, width), BF),
            pltpu.VMEM((rows, width), BF),
            pltpu.VMEM((rows, width), BF),
            pltpu.VMEM((block, width), F32),
            pltpu.VMEM((block, width), F32),
            pltpu.VMEM((block, width), F32),
            pltpu.VMEM((2, width, width), BF),
            pltpu.SemaphoreType.DMA((2, 1 + chunks + chunks // 2)),
            pltpu.SemaphoreType.DMA((2, 2)),
        ],
        compiler_params=params(),
    )(frame, attended, attended, target, emb, gain, shift, weight, *halves)


def split_three(x):
    first = x.astype(BF)
    rest = x - first.astype(F32)
    second = rest.astype(BF)
    rest = rest - second.astype(F32)
    return first, second, rest.astype(BF)


def attend_back_kernel(
    dp, parts, q_ref, k_ref, v_ref, g_ref, o_ref, l_ref, source, gq_ref, gk_ref, gv_ref, out,
    qm, km, vm, gm, acc, *refs
):
    rows = q_ref.shape[0]
    pair, i = pl.program_id(0), pl.program_id(1)
    pairs, blocks = pl.num_programs(0), pl.num_programs(1)
    block = gv_ref.shape[0]
    slot = pair * blocks + i
    slots = 6 * (rows // block)
    place = Place(dp)

    @pl.when(slot == 0)
    def _():
        place.meet()

    for reducer in reducers(place, parts, source, out, refs):
        events = reducer.events()
        for at, event in zip(spread(len(events), slots, REDUCE_WEIGHTS(len(events))), events):
            pl.when(slot == at)(event)

    lane = lax.broadcasted_iota(jnp.int32, (rows, PAIR), 1)

    @pl.when(i == 0)
    def _():
        q, k, v, g = q_ref[...], k_ref[...], v_ref[...], g_ref[...]
        product = g.astype(F32) * o_ref[...].astype(F32)
        logs = l_ref[...]
        for h in range(2):
            inside = (lane < HEAD_DIM) if h == 0 else (lane >= HEAD_DIM)
            base = HEAD_DIM * (1 - h)
            inner = -jnp.sum(jnp.where(inside, product, 0.0), axis=1, keepdims=True)
            log = -jnp.max(jnp.where(inside, logs, -jnp.inf), axis=1, keepdims=True)

            def extend(x, terms):
                tail = jnp.zeros_like(x)
                for n, term in enumerate(terms):
                    tail = jnp.where(lane == base + n, term, tail)
                return jnp.where(inside, x, tail)

            ones = jnp.where((lane >= base) & (lane < base + 3), 1.0, 0.0).astype(BF)
            qm[h] = extend(q, split_three(log))
            gm[h] = extend(g, split_three(inner))
            km[h] = jnp.where(inside, k, ones)
            vm[h] = jnp.where(inside, v, ones)
        acc[...] = jnp.zeros_like(acc)

    low_block = lax.broadcasted_iota(jnp.int32, (block, PAIR), 1) < HEAD_DIM
    here = pl.ds(pl.multiple_of(i * block, block), block)
    value_terms, key_terms = [], []
    turned = k_ref[here, :].T
    for h in range(2):
        prob = jnp.exp2(EXP2_SCALE * dot_t(km[h, here, :], qm[h]))
        score = (prob * dot_t(vm[h, here, :], gm[h])).astype(BF)
        value_terms.append(dot(prob.astype(BF), g_ref[...]))
        key_terms.append(dot(score, q_ref[...]))
        acc[h] += dot(turned, score)
    gv_ref[...] = jnp.where(low_block, value_terms[0], value_terms[1]).astype(BF)
    gk_ref[...] = (SCORE_SCALE * jnp.where(low_block, key_terms[0], key_terms[1])).astype(BF)

    @pl.when(i == blocks - 1)
    def _():
        gq_ref[...] = (SCORE_SCALE * jnp.where(lane < HEAD_DIM, acc[0].T, acc[1].T)).astype(BF)


def REDUCE_WEIGHTS(count):
    known = [1, 5, 3, 2, 2, 2, 2, 3, 2]
    return known if count == len(known) + 1 else None


def attend_back_call(queries, keys, values, grad, attended, logs, source, dp, block):
    rows, width = queries.shape
    tile = pl.BlockSpec((rows, PAIR), lambda i, j: (0, i))
    part_tile = pl.BlockSpec((block, PAIR), lambda i, j: (j, i))
    anys = pl.BlockSpec(memory_space=pl.ANY)
    parts = reduce_parts(source.shape[1], dp)
    return pl.pallas_call(
        functools.partial(attend_back_kernel, dp, parts),
        grid=(width // PAIR, rows // block),
        in_specs=[tile] * 6 + [anys],
        out_specs=[tile, part_tile, part_tile, anys],
        out_shape=[jax.ShapeDtypeStruct((rows, width), BF)] * 3
        + [jax.ShapeDtypeStruct(source.shape[1:], BF)],
        scratch_shapes=[pltpu.VMEM((2, rows, PAIR), BF)] * 4
        + [pltpu.VMEM((2, PAIR, rows), F32)]
        + reduce_scratch(parts, width),
        compiler_params=pltpu.CompilerParams(
            vmem_limit_bytes=VMEM_BYTES, collective_id=1, has_side_effects=True
        ),
    )(queries, keys, values, grad, attended, logs, source)


def qkv_back_kernel(
    block, steps, seq_axis,
    frame_ref, gh_ref, gq_ref, gk_ref, gv_ref, emb_ref, gain_ref, shift_ref, *rest
):
    own, other = rest[0:3], rest[3:6]
    gi_ref, sg_ref, ss_ref, st_ref, grads = rest[6:11]
    weights, first_in, sems = rest[11:14]
    parts = (gq_ref, gk_ref, gv_ref)
    i = pl.program_id(0)
    seq = lax.axis_index(seq_axis)
    half = own[0].shape[0]

    @pl.when(i == 0)
    def _():
        copies = []
        for n in range(3):
            for m, (src, place) in enumerate(((own[n], seq), (other[n], 1 - seq))):
                rows = pl.ds(pl.multiple_of(place * half, 128), half)
                copies.append(pltpu.make_async_copy(src, weights.at[n, rows, :], sems.at[n, m]))
        for copy in copies:
            copy.start()
        for copy in copies:
            copy.wait()
        for ref in (sg_ref, ss_ref, st_ref):
            ref[...] = jnp.zeros_like(ref)

    @pl.when(i < steps)
    def _():
        rows = pl.ds(pl.multiple_of(i * block, block), block)
        hidden = frame_ref[...].astype(F32) + emb_ref[...]
        normed, inv_std = norm_rows(hidden)
        first_in[rows, :] = (normed * gain_ref[...] + shift_ref[...]).astype(BF)
        grad = dot_t(gq_ref[rows, :], weights[0])
        grad += dot_t(gk_ref[rows, :], weights[1])
        grad += dot_t(gv_ref[rows, :], weights[2])
        ss_ref[...] += jnp.sum(grad, axis=0, keepdims=True)
        sg_ref[...] += jnp.sum(grad * normed, axis=0, keepdims=True)
        grad = gh_ref[...] + norm_rows_back(grad, normed, inv_std, gain_ref[...])
        st_ref[...] += jnp.sum(grad, axis=0, keepdims=True)
        gi_ref[...] = grad.astype(BF)

    for n in range(3):

        @pl.when(i == steps + n)
        def _():
            term = dot_l(first_in[...], parts[n][...]).astype(BF)
            grads[0, pl.ds(n * half, half), :] = term[:half]
            grads[1, pl.ds(n * half, half), :] = term[half:]


def qkv_back_call(frame, hidden_grad, gq, gk, gv, emb, gain, shift, own, other, block):
    rows, width = frame.shape
    steps = rows // block
    tile = pl.BlockSpec((block, width), lambda i: (jnp.minimum(i, steps - 1), 0))
    whole = pl.BlockSpec((rows, width), lambda i: (0, 0))
    vec = pl.BlockSpec((1, width), lambda i: (0, 0))
    anys = pl.BlockSpec(memory_space=pl.ANY)
    grad_shape = (2, 3 * (width // 2), width)
    return pl.pallas_call(
        functools.partial(qkv_back_kernel, block, steps, "seq"),
        grid=(steps + 3,),
        in_specs=[tile, tile, whole, whole, whole, vec, vec, vec] + [anys] * 6,
        out_specs=[tile, vec, vec, vec, pl.BlockSpec(grad_shape, lambda i: (0, 0, 0))],
        out_shape=[jax.ShapeDtypeStruct((rows, width), BF)]
        + [jax.ShapeDtypeStruct((1, width), F32)] * 3
        + [jax.ShapeDtypeStruct(grad_shape, BF)],
        scratch_shapes=[
            pltpu.VMEM((3, width, width), BF),
            pltpu.VMEM((rows, width), BF),
            pltpu.SemaphoreType.DMA((3, 2)),
        ],
        compiler_params=params(),
    )(frame, hidden_grad, gq, gk, gv, emb, gain, shift, *own, *other)


def body(
    frames, targets, lead_index, lead_counts,
    first_gain, first_shift, query_weight, key_weight, value_weight, output_weight,
    second_gain, second_shift, up_weight, down_weight, lead_table,
):
    seq = lax.axis_index("seq")
    dp = lax.axis_size("dp")
    swap = [(0, 1), (1, 0)]

    def trade(x):
        return lax.ppermute(x, "seq", swap)

    def pick(x, which):
        return lax.dynamic_index_in_dim(x, which, 0, keepdims=False)

    def order(mine, theirs, axis):
        return jnp.where(
            seq == 0,
            jnp.concatenate([mine, theirs], axis),
            jnp.concatenate([theirs, mine], axis),
        )

    rows, width = frames.shape[1] * 2, frames.shape[2]
    half = width // 2
    rows_here = jnp.take(lead_table, lead_index, axis=0)
    vectors = jnp.stack([first_gain, first_shift, second_gain, second_shift])
    theirs = trade(jnp.concatenate([vectors, pick(rows_here, 1 - seq)[None]]))
    mine = jnp.concatenate([vectors, pick(rows_here, seq)[None]])
    table = order(mine, theirs, 1).astype(F32)
    gain1, shift1, gain2, shift2, emb = (table[n : n + 1] for n in range(5))

    early = (query_weight, key_weight, value_weight)
    late = (output_weight, up_weight, down_weight)
    early_other = tuple(trade(w) for w in early)
    frame = jnp.concatenate([pick(frames, seq), trade(pick(frames, 1 - seq))])
    late_other = tuple(trade(w) for w in late)
    target = jnp.concatenate([pick(targets, seq), trade(pick(targets, 1 - seq))])

    totals = lax.psum(lead_counts[0].astype(F32), "dp")
    lead_weight = jnp.mean(totals) / totals
    lead = pick(lead_index, seq)
    frame_weight = pick(lead_weight, lead).reshape(1, 1)

    queries, keys, values = qkv_call(frame, emb, gain1, shift1, early, early_other, rows // 4)
    attended, logs = attend_call(queries, keys, values, rows // 2)
    halves = tuple(w for pair in zip(late, late_other) for w in pair)
    result, hidden_grad, attended_grad, sg2, ss2, grads = feed_call(
        frame, attended, target, emb, gain2, shift2, frame_weight, halves, padded_rows(9 * half, dp), rows // 6
    )
    gq, gk, gv, late_sum = attend_back_call(
        queries, keys, values, attended_grad, attended, logs, grads, dp, rows // 4
    )
    input_grad, sg1, ss1, st, grads_early = qkv_back_call(
        frame, hidden_grad, gq, gk, gv, emb, gain1, shift1, early, early_other, rows // 4
    )

    def place(x):
        mine, theirs = x[: rows // 2], trade(x[rows // 2 :])
        return jnp.where(
            seq == 0, jnp.stack([mine, theirs]), jnp.stack([theirs, mine])
        )

    def reduce(x):
        summed = pick(x, seq).astype(F32) + trade(pick(x, 1 - seq)).astype(F32)
        return lax.psum(summed.astype(BF), "dp")

    late_sum = late_sum.astype(F32)
    early_sum = reduce(grads_early).astype(F32)
    rows_ff = 4 * half
    down_grad = late_sum[:rows_ff]
    up_grad = late_sum[rows_ff : 2 * rows_ff].reshape(4, half, width)
    up_grad = jnp.moveaxis(up_grad, 0, 1).reshape(half, 4 * width)
    output_grad = late_sum[2 * rows_ff : 2 * rows_ff + half]

    hot = (jnp.arange(lead_table.shape[0]) == lead).astype(F32)
    small = jnp.concatenate([sg1, ss1, sg2, ss2, hot[:, None] * st]).reshape(-1, 2, half)
    small = small.transpose(1, 0, 2)
    small = lax.psum(pick(small, seq) + trade(pick(small, 1 - seq)), "dp")
    return (
        place(result), place(input_grad), small[0], small[1],
        early_sum[:half], early_sum[half : 2 * half], early_sum[2 * half :], output_grad,
        small[2], small[3], up_grad, down_grad, small[4:],
    )


def solution(mesh):
    weight = P("seq", None)
    vector = P("seq")
    batch = P("dp", "seq", None)
    table = P(None, "seq")
    return jax.shard_map(
        body,
        mesh=mesh,
        in_specs=(
            batch, batch, P("dp"), P("dp", None), vector, vector, weight, weight, weight, weight,
            vector, vector, weight, weight, table,
        ),
        out_specs=(
            batch, batch, vector, vector, weight, weight, weight, weight, vector, vector, weight,
            weight, table,
        ),
        check_vma=False,
    )
```

```python
import functools

import jax
import jax.numpy as jnp
from jax import lax
from jax.experimental import pallas as pl
from jax.experimental.pallas import tpu as pltpu
from jax.sharding import PartitionSpec as P

HEAD_DIM = 64
PAIR = 128
EPSILON = 1e-06
LOG2E = 1.4426950408889634
SCORE_SCALE = HEAD_DIM**-0.5
EXP2_SCALE = SCORE_SCALE * LOG2E
BF = jnp.bfloat16
F32 = jnp.float32
VMEM_BYTES = 61 * 2**20
SAFE_LOG2 = 100.0


def dot(left, right):
    return jnp.dot(left, right, preferred_element_type=F32)


def dot_t(left, right):
    return lax.dot_general(left, right, (((1,), (1,)), ((), ())), preferred_element_type=F32)


def dot_l(left, right):
    return lax.dot_general(left, right, (((0,), (0,)), ((), ())), preferred_element_type=F32)


def row_mean(x):
    return jnp.mean(x, axis=1, keepdims=True)


def norm_rows(hidden):
    center = hidden - row_mean(hidden)
    inv_std = lax.rsqrt(row_mean(center * center) + EPSILON)
    return center * inv_std, inv_std


def norm_rows_back(grad_out, normed, inv_std, gain):
    scaled = grad_out * gain
    return inv_std * (scaled - row_mean(scaled) - normed * row_mean(scaled * normed))


def gelu_pair(u):
    z = jnp.abs(u) * 0.7071067811865476
    t = 1.0 / (1.0 + 0.3275911 * z)
    e = jnp.exp2(u * u * (-0.5 * LOG2E))
    poly = t * (
        0.127414796
        + t * (-0.142248368 + t * (0.7107068705 + t * (-0.7265760135 + t * 0.5307027145)))
    )
    tail = poly * e
    cdf = jnp.where(u >= 0, 1.0 - tail, tail)
    return u * cdf, cdf + u * (e * 0.3989422804014327)


def params(limit=VMEM_BYTES):
    return pltpu.CompilerParams(vmem_limit_bytes=limit)


def reduce_parts(rows, dp):
    bits = dp.bit_length() - 1
    unit = 16 * dp
    units = rows // unit
    middle = list(range(1, bits))
    orders = [["seq"] + middle, middle + ["seq"], middle[1:] + ["seq"] + middle[:1]]
    sizes = [(units + 2 - n) // 3 for n in range(3)]
    parts, base = [], 0
    for size, order in zip(sizes, orders):
        if size > 0:
            parts.append((base, size * unit, [0] + order))
            base += size * unit
    return parts


def padded_rows(rows, dp):
    unit = 16 * dp
    return -(-rows // unit) * unit


class Place:
    def __init__(self, dp):
        self.bits = dp.bit_length() - 1
        self.dp = lax.axis_index("dp")
        self.seq = lax.axis_index("seq")

    def bit(self, key):
        return self.seq if key == "seq" else (self.dp // (1 << key)) % 2

    def partner(self, key):
        if key == "seq":
            return (self.dp, 1 - self.seq)
        return (self.dp + (1 << key) * (1 - 2 * self.bit(key)), self.seq)

    def meet(self, keys=None):
        barrier = pltpu.get_barrier_semaphore()
        keys = keys or ["seq"] + list(range(self.bits))
        for key in keys:
            pl.semaphore_signal(
                barrier, inc=1, device_id=self.partner(key), device_id_type=pl.DeviceIdType.MESH
            )
        pl.semaphore_wait(barrier, len(keys))


def send(place, key, src, dst, sems):
    return pltpu.make_async_remote_copy(
        src_ref=src,
        dst_ref=dst,
        send_sem=sems.at[0],
        recv_sem=sems.at[1],
        device_id=place.partner(key),
        device_id_type=pl.DeviceIdType.MESH,
    )


def fetch_other(place, own, full, base, sems):
    quarter = own.shape[0] // 4
    mine, theirs = base
    b0, b1 = place.bit(0), place.bit(1)
    at = (b0 * 2 + b1) * quarter

    def rows(start, n):
        return pl.ds(pl.multiple_of(start, 16), n)

    there = full.at[rows(theirs + at, quarter), :]
    pair = full.at[rows(theirs + b0 * 2 * quarter, 2 * quarter), :]
    return (
        send(place, "seq", own.at[rows(at, quarter), :], full.at[rows(mine + at, quarter), :], sems.at[0]),
        send(place, 1, there, there, sems.at[1]),
        send(place, 0, pair, pair, sems.at[2]),
    )


def reduce_scratch(parts, width):
    shapes = []
    for _, rows, order in parts:
        lead, n = 2, rows // 2
        shapes += [pltpu.VMEM((2, n, width), BF), pltpu.VMEM((2, n, width), BF)]
        for key in order[1:]:
            lead, n = (1, n) if key == "seq" else (lead, n // 2)
            shapes.append(pltpu.VMEM((lead, n, width), BF))
    steps = max(len(order) for _, _, order in parts)
    shapes += [pltpu.SemaphoreType.DMA((len(parts), 2 * steps, 2))]
    shapes += [pltpu.SemaphoreType.DMA((len(parts), 2))]
    return shapes


class Reducer:
    def __init__(self, place, part, index, source, out, refs, sems, local_sems):
        self.place, self.index, self.source, self.out = place, index, source, out
        self.base, self.rows, self.order = part
        self.acc, self.landing = refs[0], refs[1:]
        self.sems, self.local = sems, local_sems
        self.copies = {}
        half = self.rows // 2
        seq = place.seq
        off, n, cut = 0, half, False
        self.plan = []
        for key in self.order[1:]:
            if key == "seq":
                leave = (pl.ds(1 - seq, 1), pl.ds(off, n))
                cut = True
                stay = (pl.ds(seq, 1), pl.ds(off, n))
            else:
                n //= 2
                bit = place.bit(key)
                lead = pl.ds(seq, 1) if cut else slice(None)
                leave = (lead, pl.ds(self.row(off + (1 - bit) * n), n))
                off = self.row(off + bit * n)
                stay = (lead, pl.ds(off, n))
            self.plan.append((key, leave, stay))
        self.final_off, self.final_rows = off, n

    @staticmethod
    def row(x):
        return x if isinstance(x, int) else pl.multiple_of(x, 16)

    def absolute(self, off):
        return pl.multiple_of(self.base + self.place.bit(0) * (self.rows // 2) + off, 16)

    def remote(self, step, src, dst, key):
        return pltpu.make_async_remote_copy(
            src_ref=src,
            dst_ref=dst,
            send_sem=self.sems.at[self.index, step, 0],
            recv_sem=self.sems.at[self.index, step, 1],
            device_id=self.place.partner(key),
            device_id_type=pl.DeviceIdType.MESH,
        )

    def scatter(self, step):
        if step == 0:
            half = self.rows // 2
            there = pl.multiple_of(self.base + (1 - self.place.bit(0)) * half, 16)
            return self.remote(0, self.source.at[:, pl.ds(there, half), :], self.landing[0], 0)
        key, leave, _ = self.plan[step - 1]
        return self.remote(step, self.acc.at[leave[0], leave[1], :], self.landing[step], key)

    def keep_copy(self):
        half = self.rows // 2
        here = pl.multiple_of(self.base + self.place.bit(0) * half, 16)
        return pltpu.make_async_copy(
            self.source.at[:, pl.ds(here, half), :], self.acc, self.local.at[self.index, 0]
        )

    def final_copy(self):
        return pltpu.make_async_copy(
            self.acc.at[self.place.seq, pl.ds(self.final_off, self.final_rows), :],
            self.out.at[pl.ds(self.absolute(self.final_off), self.final_rows), :],
            self.local.at[self.index, 1],
        )

    def gather(self, j):
        keys = [key for key in reversed(self.order) if key != "seq"]
        off, n = self.absolute(self.final_off), self.final_rows
        for key in keys[:j]:
            off = off - self.place.bit(key) * n
            n *= 2
        off = pl.multiple_of(off, 16)
        if j == 0:
            src = self.acc.at[self.place.seq, pl.ds(self.final_off, n), :]
        else:
            src = self.out.at[pl.ds(off, n), :]
        return self.remote(len(self.order) + j, src, self.out.at[pl.ds(off, n), :], keys[j])

    def add(self, step):
        landing = self.landing[step]
        if step == 0:
            lead, rows = (0, 2), pl.ds(0, self.rows // 2)
            first = 0
        else:
            _, _, stay = self.plan[step - 1]
            first = stay[0].start if isinstance(stay[0], pl.Slice) else 0
            lead, rows = (0, landing.shape[0]), stay[1]
        n = landing.shape[1]
        size = 32 if n % 32 == 0 else 16
        start = rows.start
        for m in range(lead[1]):

            def some(i, _):
                at = pl.multiple_of(i * size, size)
                here = pl.ds(pl.multiple_of(start + at, 16), size)
                self.acc[first + m, here, :] = (
                    self.acc[first + m, here, :] + landing[m, pl.ds(at, size), :]
                )
                return 0

            lax.fori_loop(0, n // size, some, 0)

    def events(self):
        steps = len(self.order)
        gathers = self.place.bits

        def begin():
            self.keep_copy().start()
            self.scatter(0).start()

        def middle(step):
            def run():
                if step == 1:
                    self.keep_copy().wait()
                self.scatter(step - 1).wait_recv()
                self.add(step - 1)
                if step < steps:
                    self.scatter(step).start()
                else:
                    self.final_copy().start()
                    self.gather(0).start()

            return run

        def onward(j):
            def run():
                if j == 1:
                    self.final_copy().wait()
                self.gather(j - 1).wait_recv()
                self.gather(j).start()

            return run

        def finish():
            self.gather(gathers - 1).wait_recv()
            for step in range(steps):
                self.scatter(step).wait_send()
            for j in range(gathers):
                self.gather(j).wait_send()

        return (
            [begin]
            + [middle(step) for step in range(1, steps + 1)]
            + [onward(j) for j in range(1, gathers)]
            + [finish]
        )


def reducers(place, parts, source, out, refs):
    sems, local_sems = refs[-2:]
    made, at = [], 0
    for index, part in enumerate(parts):
        count = 1 + len(part[2])
        made.append(Reducer(place, part, index, source, out, refs[at : at + count], sems, local_sems))
        at += count
    return made


def spread(count, slots, weights=None):
    weights = weights or [1.0] * (count - 1)
    total, at, out = sum(weights), 0.0, [0]
    for weight in weights:
        at += weight
        out.append(min(slots - 1, round(at / total * (slots - 1))))
    return out


def start_kernel(
    dp, frames, pack_ref, wq, wk, wv,
    q_ref, k_ref, v_ref, frame_out, weight_out, table_ref,
    weights, frame, pack_in, weight_sems, frame_sems, pack_sems, local_sems,
):
    i = pl.program_id(0)
    steps = pl.num_programs(0)
    place = Place(dp)
    seq = place.seq
    rows = frame.shape[0] // 2
    half = wq.shape[0]
    block = q_ref.shape[0]
    pieces = rows // block
    own = (wq, wk, wv)
    chains = [
        fetch_other(place, own[n], weights.at[n], (seq * half, (1 - seq) * half), weight_sems.at[n])
        for n in range(3)
    ]
    pack_copy = send(place, "seq", pack_ref, pack_in, pack_sems)
    frame_copies = [
        send(
            place, "seq",
            frames.at[1 - seq, pl.ds(c * block, block), :],
            frame.at[pl.ds(rows + c * block, block), :],
            frame_sems.at[c],
        )
        for c in range(pieces)
    ]
    keep = [
        pltpu.make_async_copy(
            own[n], weights.at[n, pl.ds(pl.multiple_of(seq * half, 128), half), :], local_sems.at[n]
        )
        for n in range(3)
    ] + [pltpu.make_async_copy(frames.at[seq], frame.at[pl.ds(0, rows), :], local_sems.at[3])]
    weights_back = pltpu.make_async_copy(weights, weight_out, local_sems.at[4])
    frame_back = pltpu.make_async_copy(frame, frame_out, local_sems.at[5])

    @pl.when(i == 0)
    def _():
        place.meet(["seq", 0, 1])
        pack_copy.start()
        for chain in chains:
            chain[0].start()
        for copy in frame_copies:
            copy.start()
        for copy in keep:
            copy.start()
        for step in range(2):
            for chain in chains:
                chain[step].wait_recv()
                chain[step + 1].start()
        pack_copy.wait()
        here = pl.ds(pl.multiple_of(seq * half, 128), half)
        there = pl.ds(pl.multiple_of((1 - seq) * half, 128), half)
        table_ref[:, here] = pack_ref[...]
        table_ref[:, there] = pack_in[...]
        table_ref[4:5, there] = pack_in[5:6, :]
        for copy in keep:
            copy.wait()
        for chain in chains:
            chain[2].wait_recv()
            for step in range(3):
                chain[step].wait_send()
        weights_back.start()

    for c in range(pieces):

        @pl.when(i == pieces + c)
        def _():
            frame_copies[c].wait()

    @pl.when(i == steps - 1)
    def _():
        frame_back.start()

    hidden = frame[pl.ds(pl.multiple_of(i * block, block), block), :].astype(F32)
    normed, _ = norm_rows(hidden + table_ref[4:5, :])
    first_in = (normed * table_ref[0:1, :] + table_ref[1:2, :]).astype(BF)
    for n, ref in enumerate((q_ref, k_ref, v_ref)):
        ref[...] = dot(first_in, weights[n]).astype(BF)

    @pl.when(i == steps - 1)
    def _():
        weights_back.wait()
        frame_back.wait()


def start_call(frames, pack, own, dp, block):
    rows, width = 2 * frames.shape[1], frames.shape[2]
    pieces = frames.shape[1] // block
    tile = pl.BlockSpec((block, width), lambda i: (i, 0))
    anys = pl.BlockSpec(memory_space=pl.ANY)
    return pl.pallas_call(
        functools.partial(start_kernel, dp),
        grid=(rows // block,),
        in_specs=[anys, pl.BlockSpec(memory_space=pltpu.VMEM)] + [anys] * 3,
        out_specs=[tile] * 3 + [anys, anys, pl.BlockSpec((8, width), lambda i: (0, 0))],
        out_shape=[jax.ShapeDtypeStruct((rows, width), BF)] * 4
        + [
            jax.ShapeDtypeStruct((3, width, width), BF),
            jax.ShapeDtypeStruct((8, width), F32),
        ],
        scratch_shapes=[
            pltpu.VMEM((3, width, width), BF),
            pltpu.VMEM((rows, width), BF),
            pltpu.VMEM((8, width // 2), F32),
            pltpu.SemaphoreType.DMA((3, 3, 2)),
            pltpu.SemaphoreType.DMA((pieces, 2)),
            pltpu.SemaphoreType.DMA((2,)),
            pltpu.SemaphoreType.DMA((6,)),
        ],
        compiler_params=pltpu.CompilerParams(
            vmem_limit_bytes=VMEM_BYTES, collective_id=2, has_side_effects=True
        ),
    )(frames, pack, *own)


def masked_pair(k, v):
    low = lax.broadcasted_iota(jnp.int32, k.shape, 1) < HEAD_DIM
    return (
        (jnp.where(low, k, 0).astype(BF), jnp.where(low, 0, k).astype(BF)),
        (jnp.where(low, v, 1).astype(BF), jnp.where(low, 1, v).astype(BF)),
    )


def attend_rows(query, keys, values, shifted):
    mixed, logs = [], []
    for h in range(2):
        scores = dot_t(query, keys[h])
        if shifted:
            peak = jnp.max(scores, axis=1, keepdims=True)
            scores = scores - peak
        weight = jnp.exp2(scores * EXP2_SCALE).astype(BF)
        total = dot(weight, values[h])
        turned = pltpu.roll(total, HEAD_DIM, 1)
        mixed.append(total / turned)
        log = jnp.log2(turned) * (1.0 / EXP2_SCALE)
        logs.append(log + peak if shifted else log)
    low = lax.broadcasted_iota(jnp.int32, mixed[0].shape, 1) < HEAD_DIM
    return jnp.where(low, mixed[0], mixed[1]).astype(BF), jnp.where(low, logs[0], logs[1])


def longest(x):
    square = x.astype(F32) * x.astype(F32)
    low = lax.broadcasted_iota(jnp.int32, x.shape, 1) < HEAD_DIM
    first = jnp.sum(jnp.where(low, square, 0.0), axis=1, keepdims=True)
    second = jnp.sum(jnp.where(low, 0.0, square), axis=1, keepdims=True)
    return jnp.max(jnp.maximum(first, second), axis=0, keepdims=True)


def attend_kernel(
    dp, q_ref, k_ref, v_ref, targets, wu_own, wd_own, wo_own,
    o_ref, l_ref, bound_ref, target, wu_other, wd_other, wo_other,
    keys, values, chain_sems, target_sems, local_sem,
):
    pair, i = pl.program_id(0), pl.program_id(1)
    pairs, blocks = pl.num_programs(0), pl.num_programs(1)
    slot = pair * blocks + i
    rows, block = k_ref.shape[0], q_ref.shape[0]
    slots = 6 * (rows // block)
    place = Place(dp)
    wu, wd, wo = (
        fetch_other(place, own, other, (0, 0), chain_sems.at[n])
        for n, (own, other) in enumerate(((wu_own, wu_other), (wd_own, wd_other), (wo_own, wo_other)))
    )
    near = targets.shape[1]
    trade = send(
        place, "seq", targets.at[1 - place.seq], target.at[pl.ds(near, near), :], target_sems
    )
    keep = pltpu.make_async_copy(targets.at[place.seq], target.at[pl.ds(0, near), :], local_sem)

    def begin():
        place.meet(["seq", 0, 1])
        wu[0].start()
        wd[0].start()
        keep.start()

    def step_on(chain, step):
        chain[step].wait_recv()
        chain[step + 1].start()

    def third():
        step_on(wu, 0)
        wo[0].start()
        trade.start()

    def last_step():
        step_on(wd, 1)
        step_on(wo, 1)

    def end():
        for chain in (wu, wd, wo):
            chain[2].wait_recv()
            for copy in chain:
                copy.wait_send()
        trade.wait()
        keep.wait()

    events = [
        (0, begin),
        (3, third),
        (5, lambda: step_on(wd, 0)),
        (6, lambda: step_on(wu, 1)),
        (7, lambda: step_on(wo, 0)),
        (9, last_step),
    ]
    for at, event in events:
        pl.when(slot == (at * slots) // 12)(event)

    @pl.when(i == 0)
    def _():
        ks, vs = masked_pair(k_ref[...], v_ref[...])
        for h in range(2):
            keys[h] = ks[h]
            values[h] = vs[h]

    @pl.when(slot == 0)
    def _():
        bound_ref[...] = jnp.zeros_like(bound_ref)

    query = q_ref[...]
    bound = longest(query) * longest(k_ref[...])
    bound_ref[...] = jnp.maximum(bound_ref[...], bound)
    o_ref[...], l_ref[...] = attend_rows(query, keys, values, False)

    pl.when(slot == slots - 1)(end)


def attend_call(queries, keys, values, targets, late, dp, block):
    rows, width = queries.shape
    tile = pl.BlockSpec((block, PAIR), lambda i, j: (j, i))
    whole = pl.BlockSpec((rows, PAIR), lambda i, j: (0, i))
    anys = pl.BlockSpec(memory_space=pl.ANY)
    wo, wu, wd = late
    return pl.pallas_call(
        functools.partial(attend_kernel, dp),
        grid=(width // PAIR, rows // block),
        in_specs=[tile, whole, whole] + [anys] * 4,
        out_specs=[tile] * 2 + [pl.BlockSpec((1, PAIR), lambda i, j: (0, 0))] + [anys] * 4,
        out_shape=[
            jax.ShapeDtypeStruct((rows, width), BF),
            jax.ShapeDtypeStruct((rows, width), F32),
            jax.ShapeDtypeStruct((1, PAIR), F32),
            jax.ShapeDtypeStruct((rows, width), BF),
        ]
        + [jax.ShapeDtypeStruct(w.shape, BF) for w in (wu, wd, wo)],
        scratch_shapes=[pltpu.VMEM((2, rows, PAIR), BF)] * 2
        + [
            pltpu.SemaphoreType.DMA((3, 3, 2)),
            pltpu.SemaphoreType.DMA((2,)),
            pltpu.SemaphoreType.DMA,
        ],
        compiler_params=pltpu.CompilerParams(
            vmem_limit_bytes=VMEM_BYTES, collective_id=3, has_side_effects=True
        ),
    )(queries, keys, values, targets, wu, wd, wo)


def shifted_kernel(block, bound_ref, q_ref, k_ref, v_ref, o_in, l_in, o_ref, l_ref, q, k, v, o, log):
    @pl.when(jnp.logical_not(bound_ref[0, 0] <= (SAFE_LOG2 / EXP2_SCALE) ** 2))
    def _():
        rows, width = q_ref.shape

        def one_pair(n, _):
            columns = pl.ds(pl.multiple_of(n * PAIR, PAIR), PAIR)
            for src, dst in ((q_ref, q), (k_ref, k), (v_ref, v)):
                pltpu.sync_copy(src.at[:, columns], dst)
            keys, values = masked_pair(k[...], v[...])

            def some(i, _):
                here = pl.ds(pl.multiple_of(i * block, block), block)
                o[here, :], log[here, :] = attend_rows(q[here, :], keys, values, True)
                return 0

            lax.fori_loop(0, rows // block, some, 0)
            pltpu.sync_copy(o, o_ref.at[:, columns])
            pltpu.sync_copy(log, l_ref.at[:, columns])
            return 0

        lax.fori_loop(0, width // PAIR, one_pair, 0)


def shifted_call(bound, queries, keys, values, attended, logs, block):
    rows, width = queries.shape
    anys = pl.BlockSpec(memory_space=pl.ANY)
    return pl.pallas_call(
        functools.partial(shifted_kernel, block),
        in_specs=[pl.BlockSpec(memory_space=pltpu.SMEM)] + [anys] * 5,
        out_specs=[anys] * 2,
        out_shape=[
            jax.ShapeDtypeStruct((rows, width), BF),
            jax.ShapeDtypeStruct((rows, width), F32),
        ],
        input_output_aliases={4: 0, 5: 1},
        scratch_shapes=[pltpu.VMEM((rows, PAIR), BF)] * 4 + [pltpu.VMEM((rows, PAIR), F32)],
        compiler_params=params(),
    )(bound, queries, keys, values, attended, logs)


def feed_kernel(
    block, steps, seq_axis,
    frame_ref, o_ref, o_full, target_ref, emb_ref, gain_ref, shift_ref, weight_ref,
    wo_own, wo_other, wu_own, wu_other, wd_own, wd_other,
    y_ref, gh_ref, go_ref, sg_ref, ss_ref, grads,
    wo, wu, wd, act, slope, second_in, result_grad, hidden_grad, normed_s, hidden_s, acc, stage,
    sems, out_sems,
):
    i = pl.program_id(0)
    seq = lax.axis_index(seq_axis)
    width = wo.shape[0]
    half = width // 2
    chunks = act.shape[0]

    @pl.when(i == 0)
    def _():
        copies = []
        for m, (place, wo_h, wu_h, wd_h) in enumerate(
            ((seq, wo_own, wu_own, wd_own), (1 - seq, wo_other, wu_other, wd_other))
        ):
            rows = pl.ds(pl.multiple_of(place * half, 128), half)
            copies.append(pltpu.make_async_copy(wo_h, wo.at[rows, :], sems.at[m, 0]))
            for c in range(chunks):
                copies.append(
                    pltpu.make_async_copy(
                        wu_h.at[:, pl.ds(c * width, width)], wu.at[c, rows, :], sems.at[m, 1 + c]
                    )
                )
            for c in range(chunks // 2):
                copies.append(
                    pltpu.make_async_copy(
                        wd_h.at[pl.ds(c * width, width), :],
                        wd.at[place * (chunks // 2) + c],
                        sems.at[m, 1 + chunks + c],
                    )
                )
        for copy in copies:
            copy.start()
        for copy in copies:
            copy.wait()
        sg_ref[...] = jnp.zeros_like(sg_ref)
        ss_ref[...] = jnp.zeros_like(ss_ref)
        spare = grads.shape[1] - (2 * chunks + 1) * half
        if spare > 0:
            stage[0] = jnp.zeros_like(stage[0])
            fills = [
                pltpu.make_async_copy(
                    stage.at[0, pl.ds(0, spare), :],
                    grads.at[h, pl.ds((2 * chunks + 1) * half, spare), :],
                    out_sems.at[0, h],
                )
                for h in range(2)
            ]
            for fill in fills:
                fill.start()
            for fill in fills:
                fill.wait()

    @pl.when(i < steps)
    def _():
        rows = pl.ds(pl.multiple_of(i * block, block), block)
        hidden = frame_ref[...].astype(F32) + emb_ref[...] + dot(o_ref[...], wo[...])
        normed, inv_std = norm_rows(hidden)
        normed_s[...] = normed
        second_in[rows, :] = (normed * gain_ref[...] + shift_ref[...]).astype(BF)
        acc[...] = hidden

        def forward(c, _):
            a, s = gelu_pair(dot(second_in[rows, :], wu[c]))
            a = a.astype(BF)
            act[c, rows, :] = a
            slope[c, rows, :] = s.astype(BF)
            acc[...] += dot(a, wd[c])
            return 0

        lax.fori_loop(0, chunks, forward, 0)
        result = acc[...]
        y_ref[...] = result.astype(BF)
        grad = weight_ref[0, 0] * (result - target_ref[...].astype(F32))
        result_grad[rows, :] = grad.astype(BF)
        hidden_s[...] = grad
        acc[...] = jnp.zeros_like(acc)

        def backward(c, _):
            back = dot_t(result_grad[rows, :], wd[c])
            back = (back * slope[c, rows, :].astype(F32)).astype(BF)
            slope[c, rows, :] = back
            acc[...] += dot_t(back, wu[c])
            return 0

        lax.fori_loop(0, chunks, backward, 0)
        grad = acc[...]
        normed = normed_s[...]
        ss_ref[...] += jnp.sum(grad, axis=0, keepdims=True)
        sg_ref[...] += jnp.sum(grad * normed, axis=0, keepdims=True)
        grad = hidden_s[...] + norm_rows_back(grad, normed, inv_std, gain_ref[...])
        gh_ref[...] = grad
        grad = grad.astype(BF)
        hidden_grad[rows, :] = grad
        go_ref[...] = dot_t(grad, wo[...]).astype(BF)

    def out_copies(n):
        slot = n % 2
        if n < chunks:
            at = grads.at[n // (chunks // 2), pl.ds((n % (chunks // 2)) * width, width), :]
            return [pltpu.make_async_copy(stage.at[slot], at, out_sems.at[slot, 0])]
        base = (chunks // 2) * width + (n - chunks) * half
        return [
            pltpu.make_async_copy(
                stage.at[slot, pl.ds(h * half, half), :],
                grads.at[h, pl.ds(base, half), :],
                out_sems.at[slot, h],
            )
            for h in range(2)
        ]

    last = 2 * chunks
    for n in range(last + 1):

        @pl.when(i == steps + n)
        def _():
            if n >= 2:
                for copy in out_copies(n - 2):
                    copy.wait()
            if n < chunks:
                term = dot_l(act[n], result_grad[...])
            elif n < last:
                term = dot_l(second_in[...], slope[n - chunks])
            else:
                term = dot_l(o_full[...], hidden_grad[...])
            stage[n % 2] = term.astype(BF)
            for copy in out_copies(n):
                copy.start()
            if n == last:
                for m in (n - 1, n):
                    for copy in out_copies(m):
                        copy.wait()


def feed_call(frame, attended, target, emb, gain, shift, weight, halves, grad_rows, block):
    rows, width = frame.shape
    chunks = halves[2].shape[1] // width
    steps = rows // block
    tile = pl.BlockSpec((block, width), lambda i: (jnp.minimum(i, steps - 1), 0))
    whole = pl.BlockSpec((rows, width), lambda i: (0, 0))
    vec = pl.BlockSpec((1, width), lambda i: (0, 0))
    anys = pl.BlockSpec(memory_space=pl.ANY)
    return pl.pallas_call(
        functools.partial(feed_kernel, block, steps, "seq"),
        grid=(steps + 2 * chunks + 1,),
        in_specs=[tile, tile, whole, tile, vec, vec, vec, pl.BlockSpec(memory_space=pltpu.SMEM)]
        + [anys] * 6,
        out_specs=[tile, tile, tile, vec, vec, anys],
        out_shape=[
            jax.ShapeDtypeStruct((rows, width), BF),
            jax.ShapeDtypeStruct((rows, width), F32),
            jax.ShapeDtypeStruct((rows, width), BF),
            jax.ShapeDtypeStruct((1, width), F32),
            jax.ShapeDtypeStruct((1, width), F32),
            jax.ShapeDtypeStruct((2, grad_rows, width), BF),
        ],
        scratch_shapes=[
            pltpu.VMEM((width, width), BF),
            pltpu.VMEM((chunks, width, width), BF),
            pltpu.VMEM((chunks, width, width), BF),
            pltpu.VMEM((chunks, rows, width), BF),
            pltpu.VMEM((chunks, rows, width), BF),
            pltpu.VMEM((rows, width), BF),
            pltpu.VMEM((rows, width), BF),
            pltpu.VMEM((rows, width), BF),
            pltpu.VMEM((block, width), F32),
            pltpu.VMEM((block, width), F32),
            pltpu.VMEM((block, width), F32),
            pltpu.VMEM((2, width, width), BF),
            pltpu.SemaphoreType.DMA((2, 1 + chunks + chunks // 2)),
            pltpu.SemaphoreType.DMA((2, 2)),
        ],
        compiler_params=params(),
    )(frame, attended, attended, target, emb, gain, shift, weight, *halves)


def split_three(x):
    first = x.astype(BF)
    rest = x - first.astype(F32)
    second = rest.astype(BF)
    rest = rest - second.astype(F32)
    return first, second, rest.astype(BF)


def attend_back_kernel(
    dp, parts, q_ref, k_ref, v_ref, g_ref, o_ref, l_ref, source, result,
    gq_ref, gk_ref, gv_ref, out, result_out,
    qm, km, vm, gm, acc, trade_sems, *refs
):
    rows = q_ref.shape[0]
    pair, i = pl.program_id(0), pl.program_id(1)
    pairs, blocks = pl.num_programs(0), pl.num_programs(1)
    block = gv_ref.shape[0]
    slot = pair * blocks + i
    slots = 6 * (rows // block)
    place = Place(dp)

    near = result_out.shape[1]
    seq = place.seq
    trade = send(
        place, "seq", result.at[pl.ds(near, near), :], result_out.at[seq], trade_sems
    )
    keep = pltpu.make_async_copy(
        result.at[pl.ds(0, near), :], result_out.at[seq], trade_sems.at[2]
    )

    @pl.when(slot == 0)
    def _():
        place.meet()
        keep.start()

    @pl.when(slot == slots // 2)
    def _():
        trade.start()

    @pl.when(slot == slots - 1)
    def _():
        trade.wait()
        keep.wait()

    for reducer in reducers(place, parts, source, out, refs):
        events = reducer.events()
        for at, event in zip(spread(len(events), slots, REDUCE_WEIGHTS(len(events))), events):
            pl.when(slot == at)(event)

    lane = lax.broadcasted_iota(jnp.int32, (rows, PAIR), 1)

    @pl.when(i == 0)
    def _():
        q, k, v, g = q_ref[...], k_ref[...], v_ref[...], g_ref[...]
        product = g.astype(F32) * o_ref[...].astype(F32)
        logs = l_ref[...]
        for h in range(2):
            inside = (lane < HEAD_DIM) if h == 0 else (lane >= HEAD_DIM)
            base = HEAD_DIM * (1 - h)
            inner = -jnp.sum(jnp.where(inside, product, 0.0), axis=1, keepdims=True)
            log = -jnp.max(jnp.where(inside, logs, -jnp.inf), axis=1, keepdims=True)

            def extend(x, terms):
                tail = jnp.zeros_like(x)
                for n, term in enumerate(terms):
                    tail = jnp.where(lane == base + n, term, tail)
                return jnp.where(inside, x, tail)

            ones = jnp.where((lane >= base) & (lane < base + 3), 1.0, 0.0).astype(BF)
            qm[h] = extend(q, split_three(log))
            gm[h] = extend(g, split_three(inner))
            km[h] = jnp.where(inside, k, ones)
            vm[h] = jnp.where(inside, v, ones)
        acc[...] = jnp.zeros_like(acc)

    low_block = lax.broadcasted_iota(jnp.int32, (block, PAIR), 1) < HEAD_DIM
    here = pl.ds(pl.multiple_of(i * block, block), block)
    value_terms, key_terms = [], []
    turned = k_ref[here, :].T
    for h in range(2):
        prob = jnp.exp2(EXP2_SCALE * dot_t(km[h, here, :], qm[h]))
        score = (prob * dot_t(vm[h, here, :], gm[h])).astype(BF)
        value_terms.append(dot(prob.astype(BF), g_ref[...]))
        key_terms.append(dot(score, q_ref[...]))
        acc[h] += dot(turned, score)
    gv_ref[...] = jnp.where(low_block, value_terms[0], value_terms[1]).astype(BF)
    gk_ref[...] = (SCORE_SCALE * jnp.where(low_block, key_terms[0], key_terms[1])).astype(BF)

    @pl.when(i == blocks - 1)
    def _():
        gq_ref[...] = (SCORE_SCALE * jnp.where(lane < HEAD_DIM, acc[0].T, acc[1].T)).astype(BF)


def REDUCE_WEIGHTS(count):
    known = [1, 5, 3, 2, 2, 2, 2, 3, 2]
    return known if count == len(known) + 1 else None


def attend_back_call(queries, keys, values, grad, attended, logs, source, result, dp, block):
    rows, width = queries.shape
    tile = pl.BlockSpec((rows, PAIR), lambda i, j: (0, i))
    part_tile = pl.BlockSpec((block, PAIR), lambda i, j: (j, i))
    anys = pl.BlockSpec(memory_space=pl.ANY)
    parts = reduce_parts(source.shape[1], dp)
    return pl.pallas_call(
        functools.partial(attend_back_kernel, dp, parts),
        grid=(width // PAIR, rows // block),
        in_specs=[tile] * 6 + [anys] * 2,
        out_specs=[tile, part_tile, part_tile, anys, anys],
        out_shape=[jax.ShapeDtypeStruct((rows, width), BF)] * 3
        + [
            jax.ShapeDtypeStruct(source.shape[1:], BF),
            jax.ShapeDtypeStruct((2, rows // 2, width), BF),
        ],
        scratch_shapes=[pltpu.VMEM((2, rows, PAIR), BF)] * 4
        + [pltpu.VMEM((2, PAIR, rows), F32), pltpu.SemaphoreType.DMA((3,))]
        + reduce_scratch(parts, width),
        compiler_params=pltpu.CompilerParams(
            vmem_limit_bytes=VMEM_BYTES, collective_id=1, has_side_effects=True
        ),
    )(queries, keys, values, grad, attended, logs, source, result)


def last_kernel(
    dp, parts, block, count,
    frame_ref, gh_ref, gq_ref, gk_ref, gv_ref, table_ref, sg2_ref, ss2_ref, leads_ref, weight_ref,
    out, gi_out, small_ref, lead_ref,
    weights, first_in, source, gi, sums, trade, gathered, weight_sem, gi_sems, keep_sems, small_sems,
    *refs,
):
    parts_in = (gq_ref, gk_ref, gv_ref)
    i = pl.program_id(0)
    place = Place(dp)
    seq = place.seq
    rows, width = gq_ref.shape
    half = width // 2
    near = rows // 2
    steps = rows // block
    pieces = near // block
    emb, gain, shift = table_ref[4:5, :], table_ref[0:1, :], table_ref[1:2, :]
    fetch = pltpu.make_async_copy(weight_ref, weights, weight_sem)
    made = [r.events() for r in reducers(place, parts, source, out, refs)]

    def normed_rows(at):
        hidden = frame_ref[pl.ds(at, block), :].astype(F32) + emb
        return norm_rows(hidden)

    @pl.when(i == 0)
    def _():
        place.meet()
        fetch.start()
        sums[...] = jnp.zeros_like(sums)
        if source.shape[1] > 3 * width:
            source[...] = jnp.zeros_like(source)

        def some(n, _):
            at = pl.multiple_of(n * block, block)
            normed, _ = normed_rows(at)
            first_in[pl.ds(at, block), :] = (normed * gain + shift).astype(BF)
            return 0

        lax.fori_loop(0, steps, some, 0)

    for n in range(3):

        @pl.when(i == 1 + n)
        def _():
            term = dot_l(first_in[...], parts_in[n][...]).astype(BF)
            base = parts[n][0]
            for h in range(2):
                for m in range(2):
                    source[h, pl.ds(base + m * half, half), :] = term[
                        h * half : (h + 1) * half, m * half : (m + 1) * half
                    ]
            made[n][0]()

    def gi_copies(n):
        if n < pieces:
            src = gi.at[pl.ds(n * block, block), :]
            return send(place, "seq", src, gi_out.at[seq, pl.ds(n * block, block), :], gi_sems.at[n])
        n -= pieces
        return pltpu.make_async_copy(
            gi.at[pl.ds(near + n * block, block), :],
            gi_out.at[seq, pl.ds(n * block, block), :],
            keep_sems.at[n],
        )

    first = 4
    for n in range(steps):

        @pl.when(i == first + n)
        def _():
            if n == 0:
                fetch.wait()
            at = n * block + (near if n < pieces else -near)
            here = pl.ds(at, block)
            grad = dot_t(gq_ref[here, :], weights[0])
            grad += dot_t(gk_ref[here, :], weights[1])
            grad += dot_t(gv_ref[here, :], weights[2])
            normed, inv_std = normed_rows(at)
            sums[1:2, :] += jnp.sum(grad, axis=0, keepdims=True)
            sums[0:1, :] += jnp.sum(grad * normed, axis=0, keepdims=True)
            grad = gh_ref[...] + norm_rows_back(grad, normed, inv_std, gain)
            sums[4:5, :] += jnp.sum(grad, axis=0, keepdims=True)
            gi[pl.ds(n * block, block), :] = grad.astype(BF)
            gi_copies(n).start()
            if 0 < n:
                for events in made:
                    events[n]()

    def small_copy(step):
        if step == 0:
            return send(place, "seq", trade.at[0], trade.at[1], small_sems.at[0])
        b = step - 1
        start = (place.dp // (1 << b)) * (1 << b)
        group = gathered.at[pl.ds(start, 1 << b)]
        return send(place, b, group, group, small_sems.at[step])

    @pl.when(i == first + steps)
    def _():
        sums[2:3, :] = sg2_ref[...]
        sums[3:4, :] = ss2_ref[...]
        here = pl.ds(pl.multiple_of(seq * half, 128), half)
        there = pl.ds(pl.multiple_of((1 - seq) * half, 128), half)
        trade[0] = sums[:, there]
        small_copy(0).start()
        left = [events[steps:] for events in made]
        todo = [events[n] for n in range(len(left[0])) for events in left]
        share = -(-len(todo) // (place.bits + 2))
        for event in todo[:share]:
            event()
        small_copy(0).wait()
        mine, theirs = sums[:, here], trade[1]
        line = lax.broadcasted_iota(jnp.int32, (8, half), 0)
        turned = jnp.broadcast_to(theirs[4:5, :], (8, half))
        value = jnp.where(line < 4, mine + theirs, jnp.where(line == 4, mine, turned))
        value = jnp.where(line == 6, leads_ref[0:1, :], value)
        value = jnp.where(line == 7, leads_ref[1:2, :], value)
        gathered[place.dp] = value
        for step in range(1, place.bits + 1):
            small_copy(step).start()
            for event in todo[step * share : (step + 1) * share]:
                event()
            small_copy(step).wait()
        for event in todo[(place.bits + 1) * share :]:
            event()
        index = lax.broadcasted_iota(jnp.int32, lead_ref.shape, 0).astype(F32)
        small_ref[...] = jnp.zeros_like(small_ref)
        lead_ref[...] = jnp.zeros_like(lead_ref)

        def add_device(d, _):
            value = gathered[d]
            small_ref[...] += value
            lead_ref[...] += jnp.where(index == value[6:7, :], value[4:5, :], 0.0) + jnp.where(
                index == value[7:8, :], value[5:6, :], 0.0
            )
            return 0

        lax.fori_loop(0, dp, add_device, 0)
        for n in range(steps):
            gi_copies(n).wait()


def last_call(
    frame, hidden_grad, gq, gk, gv, table, sg2, ss2, leads, weights, dp, lead_count, block
):
    rows, width = frame.shape
    half = width // 2
    steps = rows // block
    pieces = steps // 2
    size = padded_rows(width, dp)
    bits = dp.bit_length() - 1
    middle = list(range(1, bits))
    orders = [["seq"] + middle, middle + ["seq"], middle[1:] + ["seq"] + middle[:1]]
    parts = [(n * size, size, [0] + order) for n, order in enumerate(orders)]
    whole = pl.BlockSpec((rows, width), lambda i: (0, 0))

    def turn(i):
        n = jnp.clip(i - 4, 0, steps - 1)
        return (jnp.where(n < pieces, n + pieces, n - pieces), 0)

    def fixed(*shape):
        return pl.BlockSpec(shape, lambda i: (0,) * len(shape))

    vec = fixed(1, width)
    anys = pl.BlockSpec(memory_space=pl.ANY)
    return pl.pallas_call(
        functools.partial(last_kernel, dp, parts, block, lead_count),
        grid=(5 + steps,),
        in_specs=[whole, pl.BlockSpec((block, width), turn), whole, whole, whole]
        + [fixed(8, width), vec, vec, fixed(2, half), anys],
        out_specs=[anys, anys, fixed(8, half), fixed(lead_count, half)],
        out_shape=[
            jax.ShapeDtypeStruct((3 * size, half), BF),
            jax.ShapeDtypeStruct((2, rows // 2, width), BF),
            jax.ShapeDtypeStruct((8, half), F32),
            jax.ShapeDtypeStruct((lead_count, half), F32),
        ],
        scratch_shapes=[
            pltpu.VMEM((3, width, width), BF),
            pltpu.VMEM((rows, width), BF),
            pltpu.VMEM((2, 3 * size, half), BF),
            pltpu.VMEM((rows, width), BF),
            pltpu.VMEM((8, width), F32),
            pltpu.VMEM((2, 8, half), F32),
            pltpu.VMEM((dp, 8, half), F32),
            pltpu.SemaphoreType.DMA,
            pltpu.SemaphoreType.DMA((pieces, 2)),
            pltpu.SemaphoreType.DMA((pieces,)),
            pltpu.SemaphoreType.DMA((bits + 1, 2)),
        ]
        + reduce_scratch(parts, half),
        compiler_params=pltpu.CompilerParams(
            vmem_limit_bytes=VMEM_BYTES, collective_id=4, has_side_effects=True
        ),
    )(frame, hidden_grad, gq, gk, gv, table, sg2, ss2, leads, weights)


def body(
    frames, targets, lead_index, lead_counts,
    first_gain, first_shift, query_weight, key_weight, value_weight, output_weight,
    second_gain, second_shift, up_weight, down_weight, lead_table,
):
    seq = lax.axis_index("seq")
    dp = lax.axis_size("dp")

    def pick(x, which):
        return lax.dynamic_index_in_dim(x, which, 0, keepdims=False)

    rows, width = frames.shape[1] * 2, frames.shape[2]
    half = width // 2
    lead_rows = jnp.take(lead_table, lead_index, axis=0)
    pack = jnp.stack(
        [
            first_gain, first_shift, second_gain, second_shift,
            pick(lead_rows, seq), pick(lead_rows, 1 - seq), first_gain, first_gain,
        ]
    ).astype(F32)

    totals = lax.psum(lead_counts[0].astype(F32), "dp")
    lead_weight = jnp.mean(totals) / totals
    lead = pick(lead_index, seq)
    frame_weight = pick(lead_weight, lead).reshape(1, 1)
    leads = jnp.stack([lead, pick(lead_index, 1 - seq)]).astype(F32)
    leads = jnp.broadcast_to(leads[:, None], (2, half))

    early = (query_weight, key_weight, value_weight)
    late = (output_weight, up_weight, down_weight)
    queries, keys, values, frame, weights, table = start_call(frames, pack, early, dp, rows // 4)
    gain2, shift2, emb = (table[n : n + 1] for n in (2, 3, 4))
    attended, logs, bound, target, wu_other, wd_other, wo_other = attend_call(
        queries, keys, values, targets, late, dp, rows // 2
    )
    attended, logs = shifted_call(bound, queries, keys, values, attended, logs, rows // 4)
    halves = (output_weight, wo_other, up_weight, wu_other, down_weight, wd_other)
    result, hidden_grad, attended_grad, sg2, ss2, grads = feed_call(
        frame, attended, target, emb, gain2, shift2, frame_weight, halves,
        padded_rows(9 * half, dp), rows // 6,
    )
    gq, gk, gv, late_sum, output = attend_back_call(
        queries, keys, values, attended_grad, attended, logs, grads, result, dp, rows // 4
    )
    early_sum, input_grad, small, lead_grad = last_call(
        frame, hidden_grad, gq, gk, gv, table, sg2, ss2, leads, weights, dp,
        lead_table.shape[0], rows // 6,
    )

    rows_ff = 4 * half
    late_sum = late_sum.astype(F32)
    down_grad = late_sum[:rows_ff]
    up_grad = late_sum[rows_ff : 2 * rows_ff].reshape(4, half, width)
    up_grad = jnp.moveaxis(up_grad, 0, 1).reshape(half, 4 * width)
    output_grad = late_sum[2 * rows_ff : 2 * rows_ff + half]
    size = early_sum.shape[0] // 3
    early_grads = [
        jnp.concatenate([early_sum[at : at + half], early_sum[at + half : at + 2 * half]], 1).astype(F32)
        for at in (0, size, 2 * size)
    ]
    return (
        output, input_grad, small[0], small[1], *early_grads, output_grad,
        small[2], small[3], up_grad, down_grad, lead_grad,
    )


def solution(mesh):
    weight = P("seq", None)
    vector = P("seq")
    batch = P("dp", "seq", None)
    table = P(None, "seq")
    return jax.shard_map(
        body,
        mesh=mesh,
        in_specs=(
            batch, batch, P("dp"), P("dp", None), vector, vector, weight, weight, weight, weight,
            vector, vector, weight, weight, table,
        ),
        out_specs=(
            batch, batch, vector, vector, weight, weight, weight, weight, vector, vector, weight,
            weight, table,
        ),
        check_vma=False,
    )
```

```python
import functools

import jax
import jax.numpy as jnp
from jax import lax
from jax.experimental import pallas as pl
from jax.experimental.pallas import tpu as pltpu
from jax.sharding import PartitionSpec as P

HEAD_DIM = 64
PAIR = 128
EPSILON = 1e-06
LOG2E = 1.4426950408889634
SCORE_SCALE = HEAD_DIM**-0.5
EXP2_SCALE = SCORE_SCALE * LOG2E
BF = jnp.bfloat16
F32 = jnp.float32
VMEM_BYTES = 61 * 2**20
SAFE_LOG2 = 100.0


def dot(left, right):
    return jnp.dot(left, right, preferred_element_type=F32)


def dot_t(left, right):
    return lax.dot_general(left, right, (((1,), (1,)), ((), ())), preferred_element_type=F32)


def dot_l(left, right):
    return lax.dot_general(left, right, (((0,), (0,)), ((), ())), preferred_element_type=F32)


def row_mean(x):
    return jnp.mean(x, axis=1, keepdims=True)


def norm_rows(hidden):
    center = hidden - row_mean(hidden)
    inv_std = lax.rsqrt(row_mean(center * center) + EPSILON)
    return center * inv_std, inv_std


def norm_rows_back(grad_out, normed, inv_std, gain):
    scaled = grad_out * gain
    return inv_std * (scaled - row_mean(scaled) - normed * row_mean(scaled * normed))


def gelu_pair(u):
    z = jnp.abs(u) * 0.7071067811865476
    d = 1.0 + 0.3275911 * z
    t = pl.reciprocal(d, approx=True)
    t = t * (2.0 - d * t)
    e = jnp.exp2(u * u * (-0.5 * LOG2E))
    poly = t * (
        0.127414796
        + t * (-0.142248368 + t * (0.7107068705 + t * (-0.7265760135 + t * 0.5307027145)))
    )
    tail = poly * e
    cdf = jnp.where(u >= 0, 1.0 - tail, tail)
    return u * cdf, cdf + u * (e * 0.3989422804014327)


def params(limit=VMEM_BYTES):
    return pltpu.CompilerParams(vmem_limit_bytes=limit)


def reduce_parts(rows, dp):
    bits = dp.bit_length() - 1
    unit = 16 * dp
    units = rows // unit
    middle = list(range(1, bits))
    orders = [["seq"] + middle, middle + ["seq"]] * 2
    sizes = [(units + 3 - n) // 4 for n in range(4)]
    parts, base = [], 0
    for size, order in zip(sizes, orders):
        if size > 0:
            parts.append((base, size * unit, [0] + order))
            base += size * unit
    return parts


def padded_rows(rows, dp):
    unit = 16 * dp
    return -(-rows // unit) * unit


class Place:
    def __init__(self, dp):
        self.bits = dp.bit_length() - 1
        self.dp = lax.axis_index("dp")
        self.seq = lax.axis_index("seq")

    def bit(self, key):
        return self.seq if key == "seq" else (self.dp // (1 << key)) % 2

    def partner(self, key):
        if key == "seq":
            return (self.dp, 1 - self.seq)
        return (self.dp + (1 << key) * (1 - 2 * self.bit(key)), self.seq)

    def meet(self, keys=None):
        barrier = pltpu.get_barrier_semaphore()
        keys = keys or ["seq"] + list(range(self.bits))
        for key in keys:
            pl.semaphore_signal(
                barrier, inc=1, device_id=self.partner(key), device_id_type=pl.DeviceIdType.MESH
            )
        pl.semaphore_wait(barrier, len(keys))


def send(place, key, src, dst, sems):
    return pltpu.make_async_remote_copy(
        src_ref=src,
        dst_ref=dst,
        send_sem=sems.at[0],
        recv_sem=sems.at[1],
        device_id=place.partner(key),
        device_id_type=pl.DeviceIdType.MESH,
    )


def fetch_other(place, own, full, base, sems):
    quarter = own.shape[0] // 4
    mine, theirs = base
    b0, b1 = place.bit(0), place.bit(1)
    at = (b0 * 2 + b1) * quarter

    def rows(start, n):
        return pl.ds(pl.multiple_of(start, 16), n)

    there = full.at[rows(theirs + at, quarter), :]
    pair = full.at[rows(theirs + b0 * 2 * quarter, 2 * quarter), :]
    return (
        send(place, "seq", own.at[rows(at, quarter), :], full.at[rows(mine + at, quarter), :], sems.at[0]),
        send(place, 1, there, there, sems.at[1]),
        send(place, 0, pair, pair, sems.at[2]),
    )


def reduce_scratch(parts, width):
    shapes = []
    for _, rows, order in parts:
        lead, n = 2, rows // 2
        shapes += [pltpu.VMEM((2, n, width), BF), pltpu.VMEM((2, n, width), BF)]
        for key in order[1:]:
            lead, n = (1, n) if key == "seq" else (lead, n // 2)
            shapes.append(pltpu.VMEM((lead, n, width), BF))
    steps = max(len(order) for _, _, order in parts)
    shapes += [pltpu.SemaphoreType.DMA((len(parts), 2 * steps, 2))]
    shapes += [pltpu.SemaphoreType.DMA((len(parts), 2))]
    return shapes


class Reducer:
    def __init__(self, place, part, index, source, out, refs, sems, local_sems):
        self.place, self.index, self.source, self.out = place, index, source, out
        self.base, self.rows, self.order = part
        self.acc, self.landing = refs[0], refs[1:]
        self.sems, self.local = sems, local_sems
        self.copies = {}
        half = self.rows // 2
        seq = place.seq
        off, n, cut = 0, half, False
        self.plan = []
        for key in self.order[1:]:
            if key == "seq":
                leave = (pl.ds(1 - seq, 1), pl.ds(off, n))
                cut = True
                stay = (pl.ds(seq, 1), pl.ds(off, n))
            else:
                n //= 2
                bit = place.bit(key)
                lead = pl.ds(seq, 1) if cut else slice(None)
                leave = (lead, pl.ds(self.row(off + (1 - bit) * n), n))
                off = self.row(off + bit * n)
                stay = (lead, pl.ds(off, n))
            self.plan.append((key, leave, stay))
        self.final_off, self.final_rows = off, n

    @staticmethod
    def row(x):
        return x if isinstance(x, int) else pl.multiple_of(x, 16)

    def absolute(self, off):
        return pl.multiple_of(self.base + self.place.bit(0) * (self.rows // 2) + off, 16)

    def remote(self, step, src, dst, key):
        return pltpu.make_async_remote_copy(
            src_ref=src,
            dst_ref=dst,
            send_sem=self.sems.at[self.index, step, 0],
            recv_sem=self.sems.at[self.index, step, 1],
            device_id=self.place.partner(key),
            device_id_type=pl.DeviceIdType.MESH,
        )

    def scatter(self, step):
        if step == 0:
            half = self.rows // 2
            there = pl.multiple_of(self.base + (1 - self.place.bit(0)) * half, 16)
            return self.remote(0, self.source.at[:, pl.ds(there, half), :], self.landing[0], 0)
        key, leave, _ = self.plan[step - 1]
        return self.remote(step, self.acc.at[leave[0], leave[1], :], self.landing[step], key)

    def keep_copy(self):
        half = self.rows // 2
        here = pl.multiple_of(self.base + self.place.bit(0) * half, 16)
        return pltpu.make_async_copy(
            self.source.at[:, pl.ds(here, half), :], self.acc, self.local.at[self.index, 0]
        )

    def final_copy(self):
        return pltpu.make_async_copy(
            self.acc.at[self.place.seq, pl.ds(self.final_off, self.final_rows), :],
            self.out.at[pl.ds(self.absolute(self.final_off), self.final_rows), :],
            self.local.at[self.index, 1],
        )

    def gather(self, j):
        keys = [key for key in reversed(self.order) if key != "seq"]
        off, n = self.absolute(self.final_off), self.final_rows
        for key in keys[:j]:
            off = off - self.place.bit(key) * n
            n *= 2
        off = pl.multiple_of(off, 16)
        if j == 0:
            src = self.acc.at[self.place.seq, pl.ds(self.final_off, n), :]
        else:
            src = self.out.at[pl.ds(off, n), :]
        return self.remote(len(self.order) + j, src, self.out.at[pl.ds(off, n), :], keys[j])

    def add(self, step):
        landing = self.landing[step]
        if step == 0:
            lead, rows = (0, 2), pl.ds(0, self.rows // 2)
            first = 0
        else:
            _, _, stay = self.plan[step - 1]
            first = stay[0].start if isinstance(stay[0], pl.Slice) else 0
            lead, rows = (0, landing.shape[0]), stay[1]
        n = landing.shape[1]
        size = 32 if n % 32 == 0 else 16
        start = rows.start
        for m in range(lead[1]):

            def some(i, _):
                at = pl.multiple_of(i * size, size)
                here = pl.ds(pl.multiple_of(start + at, 16), size)
                self.acc[first + m, here, :] = (
                    self.acc[first + m, here, :] + landing[m, pl.ds(at, size), :]
                )
                return 0

            lax.fori_loop(0, n // size, some, 0)

    def events(self):
        steps = len(self.order)
        gathers = self.place.bits

        def begin():
            self.keep_copy().start()
            self.scatter(0).start()

        def middle(step):
            def run():
                if step == 1:
                    self.keep_copy().wait()
                self.scatter(step - 1).wait_recv()
                self.add(step - 1)
                if step < steps:
                    self.scatter(step).start()
                else:
                    self.final_copy().start()
                    self.gather(0).start()

            return run

        def onward(j):
            def run():
                if j == 1:
                    self.final_copy().wait()
                self.gather(j - 1).wait_recv()
                self.gather(j).start()

            return run

        def finish():
            self.gather(gathers - 1).wait_recv()
            for step in range(steps):
                self.scatter(step).wait_send()
            for j in range(gathers):
                self.gather(j).wait_send()

        return (
            [begin]
            + [middle(step) for step in range(1, steps + 1)]
            + [onward(j) for j in range(1, gathers)]
            + [finish]
        )


def reducers(place, parts, source, out, refs):
    sems, local_sems = refs[-2:]
    made, at = [], 0
    for index, part in enumerate(parts):
        count = 1 + len(part[2])
        made.append(Reducer(place, part, index, source, out, refs[at : at + count], sems, local_sems))
        at += count
    return made


def start_kernel(
    dp, frames, leads_ref, counts_ref, vectors_ref, lead_table, wq, wk, wv,
    q_ref, k_ref, v_ref, frame_out, weight_out, table_ref,
    weights, frame, pack, pack_in, counts, counts_in,
    weight_sems, frame_sems, pack_sems, count_sems, local_sems,
):
    i = pl.program_id(0)
    steps = pl.num_programs(0)
    place = Place(dp)
    seq = place.seq
    rows = frame.shape[0] // 2
    half = wq.shape[0]
    block = q_ref.shape[0]
    pieces = rows // block
    own = (wq, wk, wv)
    chains = [
        fetch_other(place, own[n], weights.at[n], (seq * half, (1 - seq) * half), weight_sems.at[n])
        for n in range(3)
    ]
    pack_copy = send(place, "seq", pack, pack_in, pack_sems)
    count_copies = [
        send(place, b, counts.at[b], counts_in.at[b], count_sems.at[b]) for b in range(place.bits)
    ]

    def count_on(b):
        if b > 0:
            count_copies[b - 1].wait()
            counts[b] = counts[b - 1] + counts_in[b - 1]
        if b < place.bits:
            count_copies[b].start()
    frame_copies = [
        send(
            place, "seq",
            frames.at[1 - seq, pl.ds(c * block, block), :],
            frame.at[pl.ds(rows + c * block, block), :],
            frame_sems.at[c],
        )
        for c in range(pieces)
    ]
    keep = [
        pltpu.make_async_copy(
            own[n], weights.at[n, pl.ds(pl.multiple_of(seq * half, 128), half), :], local_sems.at[n]
        )
        for n in range(3)
    ] + [pltpu.make_async_copy(frames.at[seq], frame.at[pl.ds(0, rows), :], local_sems.at[3])]
    weights_back = pltpu.make_async_copy(weights, weight_out, local_sems.at[4])
    frame_back = pltpu.make_async_copy(frame, frame_out, local_sems.at[5])

    @pl.when(i == 0)
    def _():
        lead, other = leads_ref[seq], leads_ref[1 - seq]
        leads = lead_table.shape[0]
        line = lax.broadcasted_iota(jnp.int32, (8, leads), 0)
        index = lax.broadcasted_iota(jnp.int32, (8, leads), 1)
        hot = jnp.where(line == 4, lead, jnp.where(line == 5, other, -1)) == index
        pack[...] = dot(jnp.where(hot, 1.0, 0.0).astype(BF), lead_table[...])
        pack[0:4, :] = vectors_ref[...].astype(F32)
        counts[0] = jnp.zeros_like(counts[0])
        counts[0, 0:1, 0:leads] = counts_ref[...].astype(F32)
        place.meet()
        pack_copy.start()
        for chain in chains:
            chain[0].start()
        for copy in frame_copies:
            copy.start()
        for copy in keep:
            copy.start()
        count_on(0)
        for step in range(2):
            for chain in chains:
                chain[step].wait_recv()
                chain[step + 1].start()
            count_on(step + 1)
        pack_copy.wait()
        here = pl.ds(pl.multiple_of(seq * half, 128), half)
        there = pl.ds(pl.multiple_of((1 - seq) * half, 128), half)
        table_ref[:, here] = pack[...]
        table_ref[:, there] = pack_in[...]
        table_ref[4:5, there] = pack_in[5:6, :]
        table_ref[6:7, :] = jnp.full((1, 2 * half), lead.astype(F32))
        table_ref[7:8, :] = jnp.full((1, 2 * half), other.astype(F32))
        for copy in keep:
            copy.wait()
        for chain in chains:
            chain[2].wait_recv()
            for step in range(3):
                chain[step].wait_send()
        weights_back.start()

    for c in range(pieces):

        @pl.when(i == pieces + c)
        def _():
            frame_copies[c].wait()

    @pl.when(i == steps - 1)
    def _():
        frame_back.start()
        for b in range(3, place.bits + 1):
            count_on(b)
        totals = counts[place.bits, 0:1, :]
        lane = lax.broadcasted_iota(jnp.int32, totals.shape, 1)
        leads = lead_table.shape[0]
        mean = jnp.sum(jnp.where(lane < leads, totals, 0.0), axis=1, keepdims=True) / leads
        share = mean / jnp.where(lane < leads, totals, 1.0)
        weight = jnp.sum(jnp.where(lane == leads_ref[seq], share, 0.0), axis=1, keepdims=True)
        table_ref[5:6, :] = jnp.broadcast_to(weight, (1, 2 * half))

    hidden = frame[pl.ds(pl.multiple_of(i * block, block), block), :].astype(F32)
    normed, _ = norm_rows(hidden + table_ref[4:5, :])
    first_in = (normed * table_ref[0:1, :] + table_ref[1:2, :]).astype(BF)
    for n, ref in enumerate((q_ref, k_ref, v_ref)):
        ref[...] = dot(first_in, weights[n]).astype(BF)

    @pl.when(i == steps - 1)
    def _():
        weights_back.wait()
        frame_back.wait()


def start_call(frames, lead_index, lead_counts, vectors, lead_table, own, dp, block):
    rows, width = 2 * frames.shape[1], frames.shape[2]
    pieces = frames.shape[1] // block
    bits = dp.bit_length() - 1
    tile = pl.BlockSpec((block, width), lambda i: (i, 0))
    anys = pl.BlockSpec(memory_space=pl.ANY)
    return pl.pallas_call(
        functools.partial(start_kernel, dp),
        grid=(rows // block,),
        in_specs=[anys, pl.BlockSpec(memory_space=pltpu.SMEM)]
        + [pl.BlockSpec(memory_space=pltpu.VMEM)] * 3
        + [anys] * 3,
        out_specs=[tile] * 3 + [anys, anys, pl.BlockSpec((8, width), lambda i: (0, 0))],
        out_shape=[jax.ShapeDtypeStruct((rows, width), BF)] * 4
        + [
            jax.ShapeDtypeStruct((3, width, width), BF),
            jax.ShapeDtypeStruct((8, width), F32),
        ],
        scratch_shapes=[
            pltpu.VMEM((3, width, width), BF),
            pltpu.VMEM((rows, width), BF),
            pltpu.VMEM((8, width // 2), F32),
            pltpu.VMEM((8, width // 2), F32),
            pltpu.VMEM((bits + 1, 8, PAIR), F32),
            pltpu.VMEM((bits, 8, PAIR), F32),
            pltpu.SemaphoreType.DMA((3, 3, 2)),
            pltpu.SemaphoreType.DMA((pieces, 2)),
            pltpu.SemaphoreType.DMA((2,)),
            pltpu.SemaphoreType.DMA((bits, 2)),
            pltpu.SemaphoreType.DMA((6,)),
        ],
        compiler_params=pltpu.CompilerParams(
            vmem_limit_bytes=VMEM_BYTES, collective_id=2, has_side_effects=True
        ),
    )(frames, lead_index, lead_counts, vectors, lead_table, *own)


def masked_pair(k, v):
    low = lax.broadcasted_iota(jnp.int32, k.shape, 1) < HEAD_DIM
    return (
        (jnp.where(low, k, 0).astype(BF), jnp.where(low, 0, k).astype(BF)),
        (jnp.where(low, v, 1).astype(BF), jnp.where(low, 1, v).astype(BF)),
    )


def attend_rows(query, keys, values, shifted):
    mixed, logs = [], []
    for h in range(2):
        scores = dot_t(query, keys[h])
        if shifted:
            peak = jnp.max(scores, axis=1, keepdims=True)
            scores = scores - peak
        weight = jnp.exp2(scores * EXP2_SCALE).astype(BF)
        total = dot(weight, values[h])
        turned = pltpu.roll(total, HEAD_DIM, 1)
        mixed.append(total / turned)
        log = jnp.log2(turned) * (1.0 / EXP2_SCALE)
        logs.append(log + peak if shifted else log)
    low = lax.broadcasted_iota(jnp.int32, mixed[0].shape, 1) < HEAD_DIM
    return jnp.where(low, mixed[0], mixed[1]).astype(BF), jnp.where(low, logs[0], logs[1])


def longest(x):
    square = x.astype(F32) * x.astype(F32)
    low = lax.broadcasted_iota(jnp.int32, x.shape, 1) < HEAD_DIM
    first = jnp.sum(jnp.where(low, square, 0.0), axis=1, keepdims=True)
    second = jnp.sum(jnp.where(low, 0.0, square), axis=1, keepdims=True)
    return jnp.max(jnp.maximum(first, second), axis=0, keepdims=True)


def attend_kernel(
    dp, q_ref, k_ref, v_ref, targets, wu_own, wd_own, wo_own,
    o_ref, l_ref, bound_ref, target, wu_other, wd_other, wo_other,
    keys, values, chain_sems, target_sems, local_sem,
):
    pair, i = pl.program_id(0), pl.program_id(1)
    pairs, blocks = pl.num_programs(0), pl.num_programs(1)
    slot = pair * blocks + i
    rows, block = k_ref.shape[0], q_ref.shape[0]
    slots = 6 * (rows // block)
    place = Place(dp)
    wu, wd, wo = (
        fetch_other(place, own, other, (0, 0), chain_sems.at[n])
        for n, (own, other) in enumerate(((wu_own, wu_other), (wd_own, wd_other), (wo_own, wo_other)))
    )
    near = targets.shape[1]
    trade = send(
        place, "seq", targets.at[1 - place.seq], target.at[pl.ds(near, near), :], target_sems
    )
    keep = pltpu.make_async_copy(targets.at[place.seq], target.at[pl.ds(0, near), :], local_sem)

    def begin():
        place.meet(["seq", 0, 1])
        wu[0].start()
        wd[0].start()
        keep.start()

    def step_on(chain, step):
        chain[step].wait_recv()
        chain[step + 1].start()

    def third():
        step_on(wu, 0)
        wo[0].start()
        trade.start()

    def last_step():
        step_on(wd, 1)
        step_on(wo, 1)

    def end():
        for chain in (wu, wd, wo):
            chain[2].wait_recv()
            for copy in chain:
                copy.wait_send()
        trade.wait()
        keep.wait()

    events = [
        (0, begin),
        (3, third),
        (5, lambda: step_on(wd, 0)),
        (6, lambda: step_on(wu, 1)),
        (7, lambda: step_on(wo, 0)),
        (9, last_step),
    ]
    for at, event in events:
        pl.when(slot == (at * slots) // 12)(event)

    @pl.when(i == 0)
    def _():
        ks, vs = masked_pair(k_ref[...], v_ref[...])
        for h in range(2):
            keys[h] = ks[h]
            values[h] = vs[h]

    @pl.when(slot == 0)
    def _():
        bound_ref[...] = jnp.zeros_like(bound_ref)

    query = q_ref[...]
    bound = longest(query) * longest(k_ref[...])
    bound_ref[...] = jnp.maximum(bound_ref[...], bound)
    o_ref[...], l_ref[...] = attend_rows(query, keys, values, False)

    pl.when(slot == slots - 1)(end)


def attend_call(queries, keys, values, targets, late, dp, block):
    rows, width = queries.shape
    tile = pl.BlockSpec((block, PAIR), lambda i, j: (j, i))
    whole = pl.BlockSpec((rows, PAIR), lambda i, j: (0, i))
    anys = pl.BlockSpec(memory_space=pl.ANY)
    wo, wu, wd = late
    return pl.pallas_call(
        functools.partial(attend_kernel, dp),
        grid=(width // PAIR, rows // block),
        in_specs=[tile, whole, whole] + [anys] * 4,
        out_specs=[tile] * 2 + [pl.BlockSpec((1, PAIR), lambda i, j: (0, 0))] + [anys] * 4,
        out_shape=[
            jax.ShapeDtypeStruct((rows, width), BF),
            jax.ShapeDtypeStruct((rows, width), F32),
            jax.ShapeDtypeStruct((1, PAIR), F32),
            jax.ShapeDtypeStruct((rows, width), BF),
        ]
        + [jax.ShapeDtypeStruct(w.shape, BF) for w in (wu, wd, wo)],
        scratch_shapes=[pltpu.VMEM((2, rows, PAIR), BF)] * 2
        + [
            pltpu.SemaphoreType.DMA((3, 3, 2)),
            pltpu.SemaphoreType.DMA((2,)),
            pltpu.SemaphoreType.DMA,
        ],
        compiler_params=pltpu.CompilerParams(
            vmem_limit_bytes=VMEM_BYTES, collective_id=3, has_side_effects=True
        ),
    )(queries, keys, values, targets, wu, wd, wo)


def shifted_kernel(block, bound_ref, q_ref, k_ref, v_ref, o_in, l_in, o_ref, l_ref, q, k, v, o, log):
    @pl.when(jnp.logical_not(bound_ref[0, 0] <= (SAFE_LOG2 / EXP2_SCALE) ** 2))
    def _():
        rows, width = q_ref.shape

        def one_pair(n, _):
            columns = pl.ds(pl.multiple_of(n * PAIR, PAIR), PAIR)
            for src, dst in ((q_ref, q), (k_ref, k), (v_ref, v)):
                pltpu.sync_copy(src.at[:, columns], dst)
            keys, values = masked_pair(k[...], v[...])

            def some(i, _):
                here = pl.ds(pl.multiple_of(i * block, block), block)
                o[here, :], log[here, :] = attend_rows(q[here, :], keys, values, True)
                return 0

            lax.fori_loop(0, rows // block, some, 0)
            pltpu.sync_copy(o, o_ref.at[:, columns])
            pltpu.sync_copy(log, l_ref.at[:, columns])
            return 0

        lax.fori_loop(0, width // PAIR, one_pair, 0)


def shifted_call(bound, queries, keys, values, attended, logs, block):
    rows, width = queries.shape
    anys = pl.BlockSpec(memory_space=pl.ANY)
    return pl.pallas_call(
        functools.partial(shifted_kernel, block),
        in_specs=[pl.BlockSpec(memory_space=pltpu.SMEM)] + [anys] * 5,
        out_specs=[anys] * 2,
        out_shape=[
            jax.ShapeDtypeStruct((rows, width), BF),
            jax.ShapeDtypeStruct((rows, width), F32),
        ],
        input_output_aliases={4: 0, 5: 1},
        scratch_shapes=[pltpu.VMEM((rows, PAIR), BF)] * 4 + [pltpu.VMEM((rows, PAIR), F32)],
        compiler_params=params(),
    )(bound, queries, keys, values, attended, logs)


def feed_kernel(
    block, steps, seq_axis,
    frame_ref, o_ref, o_full, target_ref, emb_ref, gain_ref, shift_ref, weight_ref,
    wo_own, wo_other, wu_own, wu_other, wd_own, wd_other,
    y_ref, gh_ref, go_ref, sg_ref, ss_ref, grads,
    wo, wu, wd, act, slope, second_in, result_grad, hidden_grad, normed_s, hidden_s, acc, stage,
    sems, out_sems,
):
    i = pl.program_id(0)
    seq = lax.axis_index(seq_axis)
    width = wo.shape[0]
    half = width // 2
    chunks = act.shape[0]

    @pl.when(i == 0)
    def _():
        copies = []
        for m, (place, wo_h, wu_h, wd_h) in enumerate(
            ((seq, wo_own, wu_own, wd_own), (1 - seq, wo_other, wu_other, wd_other))
        ):
            rows = pl.ds(pl.multiple_of(place * half, 128), half)
            copies.append(pltpu.make_async_copy(wo_h, wo.at[rows, :], sems.at[m, 0]))
            for c in range(chunks):
                copies.append(
                    pltpu.make_async_copy(
                        wu_h.at[:, pl.ds(c * width, width)], wu.at[c, rows, :], sems.at[m, 1 + c]
                    )
                )
            for c in range(chunks // 2):
                copies.append(
                    pltpu.make_async_copy(
                        wd_h.at[pl.ds(c * width, width), :],
                        wd.at[place * (chunks // 2) + c],
                        sems.at[m, 1 + chunks + c],
                    )
                )
        for copy in copies:
            copy.start()
        for copy in copies:
            copy.wait()
        sg_ref[...] = jnp.zeros_like(sg_ref)
        ss_ref[...] = jnp.zeros_like(ss_ref)
        spare = grads.shape[1] - (2 * chunks + 1) * half
        if spare > 0:
            stage[0] = jnp.zeros_like(stage[0])
            fills = [
                pltpu.make_async_copy(
                    stage.at[0, pl.ds(0, spare), :],
                    grads.at[h, pl.ds((2 * chunks + 1) * half, spare), :],
                    out_sems.at[0, h],
                )
                for h in range(2)
            ]
            for fill in fills:
                fill.start()
            for fill in fills:
                fill.wait()

    @pl.when(i < steps)
    def _():
        rows = pl.ds(pl.multiple_of(i * block, block), block)
        hidden = frame_ref[...].astype(F32) + emb_ref[...] + dot(o_ref[...], wo[...])
        normed, inv_std = norm_rows(hidden)
        normed_s[...] = normed
        second_in[rows, :] = (normed * gain_ref[...] + shift_ref[...]).astype(BF)
        acc[...] = hidden

        u = dot(second_in[rows, :], wu[0])
        for c in range(chunks):
            later = dot(second_in[rows, :], wu[c + 1]) if c + 1 < chunks else None
            a, s = gelu_pair(u)
            a = a.astype(BF)
            act[c, rows, :] = a
            slope[c, rows, :] = s.astype(BF)
            acc[...] += dot(a, wd[c])
            u = later
        result = acc[...]
        y_ref[...] = result.astype(BF)
        grad = weight_ref[...] * (result - target_ref[...].astype(F32))
        result_grad[rows, :] = grad.astype(BF)
        hidden_s[...] = grad
        acc[...] = jnp.zeros_like(acc)

        back = dot_t(result_grad[rows, :], wd[0])
        for c in range(chunks):
            later = dot_t(result_grad[rows, :], wd[c + 1]) if c + 1 < chunks else None
            back = (back * slope[c, rows, :].astype(F32)).astype(BF)
            slope[c, rows, :] = back
            acc[...] += dot_t(back, wu[c])
            back = later
        grad = acc[...]
        normed = normed_s[...]
        ss_ref[...] += jnp.sum(grad, axis=0, keepdims=True)
        sg_ref[...] += jnp.sum(grad * normed, axis=0, keepdims=True)
        grad = hidden_s[...] + norm_rows_back(grad, normed, inv_std, gain_ref[...])
        gh_ref[...] = grad
        grad = grad.astype(BF)
        hidden_grad[rows, :] = grad
        go_ref[...] = dot_t(grad, wo[...]).astype(BF)

    def out_copies(n):
        slot = n % 2
        if n < chunks:
            at = grads.at[n // (chunks // 2), pl.ds((n % (chunks // 2)) * width, width), :]
            return [pltpu.make_async_copy(stage.at[slot], at, out_sems.at[slot, 0])]
        base = (chunks // 2) * width + (n - chunks) * half
        return [
            pltpu.make_async_copy(
                stage.at[slot, pl.ds(h * half, half), :],
                grads.at[h, pl.ds(base, half), :],
                out_sems.at[slot, h],
            )
            for h in range(2)
        ]

    last = 2 * chunks
    for n in range(last + 1):

        @pl.when(i == steps + n)
        def _():
            if n >= 2:
                for copy in out_copies(n - 2):
                    copy.wait()
            if n < chunks:
                term = dot_l(act[n], result_grad[...])
            elif n < last:
                term = dot_l(second_in[...], slope[n - chunks])
            else:
                term = dot_l(o_full[...], hidden_grad[...])
            stage[n % 2] = term.astype(BF)
            for copy in out_copies(n):
                copy.start()
            if n == last:
                for m in (n - 1, n):
                    for copy in out_copies(m):
                        copy.wait()


def feed_call(frame, attended, target, emb, gain, shift, weight, halves, grad_rows, block):
    rows, width = frame.shape
    chunks = halves[2].shape[1] // width
    steps = rows // block
    tile = pl.BlockSpec((block, width), lambda i: (jnp.minimum(i, steps - 1), 0))
    whole = pl.BlockSpec((rows, width), lambda i: (0, 0), pipeline_mode=pl.Buffered(1))
    vec = pl.BlockSpec((1, width), lambda i: (0, 0))
    anys = pl.BlockSpec(memory_space=pl.ANY)
    return pl.pallas_call(
        functools.partial(feed_kernel, block, steps, "seq"),
        grid=(steps + 2 * chunks + 1,),
        in_specs=[tile, tile, whole, tile, vec, vec, vec, vec]
        + [anys] * 6,
        out_specs=[tile, tile, tile, vec, vec, anys],
        out_shape=[
            jax.ShapeDtypeStruct((rows, width), BF),
            jax.ShapeDtypeStruct((rows, width), F32),
            jax.ShapeDtypeStruct((rows, width), BF),
            jax.ShapeDtypeStruct((1, width), F32),
            jax.ShapeDtypeStruct((1, width), F32),
            jax.ShapeDtypeStruct((2, grad_rows, width), BF),
        ],
        scratch_shapes=[
            pltpu.VMEM((width, width), BF),
            pltpu.VMEM((chunks, width, width), BF),
            pltpu.VMEM((chunks, width, width), BF),
            pltpu.VMEM((chunks, rows, width), BF),
            pltpu.VMEM((chunks, rows, width), BF),
            pltpu.VMEM((rows, width), BF),
            pltpu.VMEM((rows, width), BF),
            pltpu.VMEM((rows, width), BF),
            pltpu.VMEM((block, width), F32),
            pltpu.VMEM((block, width), F32),
            pltpu.VMEM((block, width), F32),
            pltpu.VMEM((2, width, width), BF),
            pltpu.SemaphoreType.DMA((2, 1 + chunks + chunks // 2)),
            pltpu.SemaphoreType.DMA((2, 2)),
        ],
        compiler_params=params(),
    )(frame, attended, attended, target, emb, gain, shift, weight, *halves)


def split_three(x):
    first = x.astype(BF)
    rest = x - first.astype(F32)
    second = rest.astype(BF)
    rest = rest - second.astype(F32)
    return first, second, rest.astype(BF)


def attend_back_kernel(
    dp, parts, q_ref, k_ref, v_ref, g_ref, o_ref, l_ref, source, result,
    gq_ref, gk_ref, gv_ref, out, result_out,
    qm, km, vm, gm, acc, trade_sems, *refs
):
    rows = q_ref.shape[0]
    pair, i = pl.program_id(0), pl.program_id(1)
    pairs, blocks = pl.num_programs(0), pl.num_programs(1)
    block = gv_ref.shape[0]
    slot = pair * blocks + i
    slots = 6 * (rows // block)
    place = Place(dp)

    near = result_out.shape[1]
    seq = place.seq
    trade = send(
        place, "seq", result.at[pl.ds(near, near), :], result_out.at[seq], trade_sems
    )
    keep = pltpu.make_async_copy(
        result.at[pl.ds(0, near), :], result_out.at[seq], trade_sems.at[2]
    )

    @pl.when(slot == 0)
    def _():
        place.meet()
        keep.start()

    @pl.when(slot == slots // 2)
    def _():
        trade.start()

    @pl.when(slot == slots - 1)
    def _():
        trade.wait()
        keep.wait()

    for n, reducer in enumerate(reducers(place, parts, source, out, refs)):
        events = reducer.events()
        for at, event in zip(reduce_slots(len(events), slots, n), events):
            pl.when(slot == at)(event)

    lane = lax.broadcasted_iota(jnp.int32, (rows, PAIR), 1)

    @pl.when(i == 0)
    def _():
        q, k, v, g = q_ref[...], k_ref[...], v_ref[...], g_ref[...]
        product = g.astype(F32) * o_ref[...].astype(F32)
        logs = l_ref[...]
        for h in range(2):
            inside = (lane < HEAD_DIM) if h == 0 else (lane >= HEAD_DIM)
            base = HEAD_DIM * (1 - h)
            inner = -jnp.sum(jnp.where(inside, product, 0.0), axis=1, keepdims=True)
            log = -jnp.max(jnp.where(inside, logs, -jnp.inf), axis=1, keepdims=True)

            def extend(x, terms):
                tail = jnp.zeros_like(x)
                for n, term in enumerate(terms):
                    tail = jnp.where(lane == base + n, term, tail)
                return jnp.where(inside, x, tail)

            ones = jnp.where((lane >= base) & (lane < base + 3), 1.0, 0.0).astype(BF)
            qm[h] = extend(q, split_three(log))
            gm[h] = extend(g, split_three(inner))
            km[h] = jnp.where(inside, k, ones)
            vm[h] = jnp.where(inside, v, ones)
        acc[...] = jnp.zeros_like(acc)

    low_block = lax.broadcasted_iota(jnp.int32, (block, PAIR), 1) < HEAD_DIM
    here = pl.ds(pl.multiple_of(i * block, block), block)
    value_terms, key_terms = [], []
    turned = k_ref[here, :].T
    for h in range(2):
        prob = jnp.exp2(EXP2_SCALE * dot_t(km[h, here, :], qm[h]))
        score = (prob * dot_t(vm[h, here, :], gm[h])).astype(BF)
        value_terms.append(dot(prob.astype(BF), g_ref[...]))
        key_terms.append(dot(score, q_ref[...]))
        acc[h] += dot(turned, score)
    gv_ref[...] = jnp.where(low_block, value_terms[0], value_terms[1]).astype(BF)
    gk_ref[...] = (SCORE_SCALE * jnp.where(low_block, key_terms[0], key_terms[1])).astype(BF)

    @pl.when(i == blocks - 1)
    def _():
        gq_ref[...] = (SCORE_SCALE * jnp.where(lane < HEAD_DIM, acc[0].T, acc[1].T)).astype(BF)


REDUCE_SLOTS = (
    (0, 1, 5, 8, 10, 12, 14, 16, 19, 21),
    (0, 1, 5, 8, 10, 12, 14, 16, 19, 21),
    (3, 5, 9, 11, 13, 15, 17, 19, 21, 23),
    (3, 5, 9, 11, 13, 15, 17, 19, 21, 23),
)


def reduce_slots(count, slots, part):
    known = REDUCE_SLOTS[part]
    if len(known) == count:
        return [at * (slots - 1) // known[-1] if slots != 24 else at for at in known]
    return [n * (slots - 1) // (count - 1) for n in range(count)]


def attend_back_call(queries, keys, values, grad, attended, logs, source, result, dp, block):
    rows, width = queries.shape
    tile = pl.BlockSpec((rows, PAIR), lambda i, j: (0, i))
    part_tile = pl.BlockSpec((block, PAIR), lambda i, j: (j, i))
    anys = pl.BlockSpec(memory_space=pl.ANY)
    parts = reduce_parts(source.shape[1], dp)
    return pl.pallas_call(
        functools.partial(attend_back_kernel, dp, parts),
        grid=(width // PAIR, rows // block),
        in_specs=[tile] * 6 + [anys] * 2,
        out_specs=[tile, part_tile, part_tile, anys, anys],
        out_shape=[jax.ShapeDtypeStruct((rows, width), BF)] * 3
        + [
            jax.ShapeDtypeStruct(source.shape[1:], BF),
            jax.ShapeDtypeStruct((2, rows // 2, width), BF),
        ],
        scratch_shapes=[pltpu.VMEM((2, rows, PAIR), BF)] * 4
        + [pltpu.VMEM((2, PAIR, rows), F32), pltpu.SemaphoreType.DMA((3,))]
        + reduce_scratch(parts, width),
        compiler_params=pltpu.CompilerParams(
            vmem_limit_bytes=VMEM_BYTES, collective_id=1, has_side_effects=True
        ),
    )(queries, keys, values, grad, attended, logs, source, result)


def last_kernel(
    dp, parts, block, count,
    frame_ref, gh_ref, gq_ref, gk_ref, gv_ref, table_ref, sg2_ref, ss2_ref, weight_ref,
    out, gi_out, small_ref, lead_ref,
    weights, first_in, source, gi, sums, trade, gathered, weight_sem, gi_sems, keep_sems, small_sems,
    *refs,
):
    parts_in = (gq_ref, gk_ref, gv_ref)
    i = pl.program_id(0)
    place = Place(dp)
    seq = place.seq
    rows, width = gq_ref.shape
    half = width // 2
    near = rows // 2
    steps = rows // block
    pieces = near // block
    emb, gain, shift = table_ref[4:5, :], table_ref[0:1, :], table_ref[1:2, :]
    fetch = pltpu.make_async_copy(weight_ref, weights, weight_sem)
    made = [r.events() for r in reducers(place, parts, source, out, refs)]

    def normed_rows(at):
        hidden = frame_ref[pl.ds(at, block), :].astype(F32) + emb
        return norm_rows(hidden)

    @pl.when(i == 0)
    def _():
        place.meet()
        fetch.start()
        sums[...] = jnp.zeros_like(sums)
        if source.shape[1] > 3 * width:
            source[...] = jnp.zeros_like(source)

        def some(n, _):
            at = pl.multiple_of(n * block, block)
            normed, _ = normed_rows(at)
            first_in[pl.ds(at, block), :] = (normed * gain + shift).astype(BF)
            return 0

        lax.fori_loop(0, steps, some, 0)

    for n in range(3):

        @pl.when(i == 1 + n)
        def _():
            term = dot_l(first_in[...], parts_in[n][...]).astype(BF)
            base = parts[n][0]
            for h in range(2):
                for m in range(2):
                    source[h, pl.ds(base + m * half, half), :] = term[
                        h * half : (h + 1) * half, m * half : (m + 1) * half
                    ]
            made[n][0]()

    def gi_copies(n):
        if n < pieces:
            src = gi.at[pl.ds(n * block, block), :]
            return send(place, "seq", src, gi_out.at[seq, pl.ds(n * block, block), :], gi_sems.at[n])
        n -= pieces
        return pltpu.make_async_copy(
            gi.at[pl.ds(near + n * block, block), :],
            gi_out.at[seq, pl.ds(n * block, block), :],
            keep_sems.at[n],
        )

    first = 4
    for n in range(steps):

        @pl.when(i == first + n)
        def _():
            if n == 0:
                fetch.wait()
            at = n * block + (near if n < pieces else -near)
            here = pl.ds(at, block)
            grad = dot_t(gq_ref[here, :], weights[0])
            grad += dot_t(gk_ref[here, :], weights[1])
            grad += dot_t(gv_ref[here, :], weights[2])
            normed, inv_std = normed_rows(at)
            sums[1:2, :] += jnp.sum(grad, axis=0, keepdims=True)
            sums[0:1, :] += jnp.sum(grad * normed, axis=0, keepdims=True)
            grad = gh_ref[...] + norm_rows_back(grad, normed, inv_std, gain)
            sums[4:5, :] += jnp.sum(grad, axis=0, keepdims=True)
            gi[pl.ds(n * block, block), :] = grad.astype(BF)
            gi_copies(n).start()
            if 0 < n:
                for events in made:
                    events[n]()

    def small_copy(step):
        if step == 0:
            return send(place, "seq", trade.at[0], trade.at[1], small_sems.at[0])
        b = step - 1
        start = (place.dp // (1 << b)) * (1 << b)
        group = gathered.at[pl.ds(start, 1 << b)]
        return send(place, b, group, group, small_sems.at[step])

    @pl.when(i == first + steps)
    def _():
        sums[2:3, :] = sg2_ref[...]
        sums[3:4, :] = ss2_ref[...]
        here = pl.ds(pl.multiple_of(seq * half, 128), half)
        there = pl.ds(pl.multiple_of((1 - seq) * half, 128), half)
        trade[0] = sums[:, there]
        small_copy(0).start()
        left = [events[steps:] for events in made]
        todo = [events[n] for n in range(len(left[0])) for events in left]
        share = -(-len(todo) // (place.bits + 2))
        for event in todo[:share]:
            event()
        small_copy(0).wait()
        mine, theirs = sums[:, here], trade[1]
        line = lax.broadcasted_iota(jnp.int32, (8, half), 0)
        turned = jnp.broadcast_to(theirs[4:5, :], (8, half))
        value = jnp.where(line < 4, mine + theirs, jnp.where(line == 4, mine, turned))
        value = jnp.where(line == 6, table_ref[6:7, 0:half], value)
        value = jnp.where(line == 7, table_ref[7:8, 0:half], value)
        gathered[place.dp] = value
        for step in range(1, place.bits + 1):
            small_copy(step).start()
            for event in todo[step * share : (step + 1) * share]:
                event()
            small_copy(step).wait()
        for event in todo[(place.bits + 1) * share :]:
            event()
        index = lax.broadcasted_iota(jnp.int32, lead_ref.shape, 0).astype(F32)
        small_ref[...] = jnp.zeros_like(small_ref)
        lead_ref[...] = jnp.zeros_like(lead_ref)

        def add_device(d, _):
            value = gathered[d]
            small_ref[...] += value
            lead_ref[...] += jnp.where(index == value[6:7, :], value[4:5, :], 0.0) + jnp.where(
                index == value[7:8, :], value[5:6, :], 0.0
            )
            return 0

        lax.fori_loop(0, dp, add_device, 0)
        for n in range(steps):
            gi_copies(n).wait()


def last_call(
    frame, hidden_grad, gq, gk, gv, table, sg2, ss2, weights, dp, lead_count, block
):
    rows, width = frame.shape
    half = width // 2
    steps = rows // block
    pieces = steps // 2
    size = padded_rows(width, dp)
    bits = dp.bit_length() - 1
    middle = list(range(1, bits))
    orders = [["seq"] + middle, middle + ["seq"], middle[1:] + ["seq"] + middle[:1]]
    parts = [(n * size, size, [0] + order) for n, order in enumerate(orders)]
    whole = pl.BlockSpec((rows, width), lambda i: (0, 0))

    def turn(i):
        n = jnp.clip(i - 4, 0, steps - 1)
        return (jnp.where(n < pieces, n + pieces, n - pieces), 0)

    def fixed(*shape):
        return pl.BlockSpec(shape, lambda i: (0,) * len(shape))

    vec = fixed(1, width)
    anys = pl.BlockSpec(memory_space=pl.ANY)
    return pl.pallas_call(
        functools.partial(last_kernel, dp, parts, block, lead_count),
        grid=(5 + steps,),
        in_specs=[whole, pl.BlockSpec((block, width), turn), whole, whole, whole]
        + [fixed(8, width), vec, vec, anys],
        out_specs=[anys, anys, fixed(8, half), fixed(lead_count, half)],
        out_shape=[
            jax.ShapeDtypeStruct((3 * size, half), BF),
            jax.ShapeDtypeStruct((2, rows // 2, width), BF),
            jax.ShapeDtypeStruct((8, half), F32),
            jax.ShapeDtypeStruct((lead_count, half), F32),
        ],
        scratch_shapes=[
            pltpu.VMEM((3, width, width), BF),
            pltpu.VMEM((rows, width), BF),
            pltpu.VMEM((2, 3 * size, half), BF),
            pltpu.VMEM((rows, width), BF),
            pltpu.VMEM((8, width), F32),
            pltpu.VMEM((2, 8, half), F32),
            pltpu.VMEM((dp, 8, half), F32),
            pltpu.SemaphoreType.DMA,
            pltpu.SemaphoreType.DMA((pieces, 2)),
            pltpu.SemaphoreType.DMA((pieces,)),
            pltpu.SemaphoreType.DMA((bits + 1, 2)),
        ]
        + reduce_scratch(parts, half),
        compiler_params=pltpu.CompilerParams(
            vmem_limit_bytes=VMEM_BYTES, collective_id=4, has_side_effects=True
        ),
    )(frame, hidden_grad, gq, gk, gv, table, sg2, ss2, weights)


def body(
    frames, targets, lead_index, lead_counts,
    first_gain, first_shift, query_weight, key_weight, value_weight, output_weight,
    second_gain, second_shift, up_weight, down_weight, lead_table,
):
    dp = lax.axis_size("dp")
    rows, width = frames.shape[1] * 2, frames.shape[2]
    half = width // 2
    vectors = jnp.concatenate([first_gain, first_shift, second_gain, second_shift]).reshape(4, half)

    early = (query_weight, key_weight, value_weight)
    late = (output_weight, up_weight, down_weight)
    queries, keys, values, frame, weights, table = start_call(
        frames, lead_index, lead_counts, vectors, lead_table, early, dp, rows // 4
    )
    gain2, shift2, emb, frame_weight = (table[n : n + 1] for n in (2, 3, 4, 5))
    attended, logs, bound, target, wu_other, wd_other, wo_other = attend_call(
        queries, keys, values, targets, late, dp, rows // 2
    )
    attended, logs = shifted_call(bound, queries, keys, values, attended, logs, rows // 4)
    halves = (output_weight, wo_other, up_weight, wu_other, down_weight, wd_other)
    result, hidden_grad, attended_grad, sg2, ss2, grads = feed_call(
        frame, attended, target, emb, gain2, shift2, frame_weight, halves,
        padded_rows(9 * half, dp), rows // 6,
    )
    gq, gk, gv, late_sum, output = attend_back_call(
        queries, keys, values, attended_grad, attended, logs, grads, result, dp, rows // 4
    )
    early_sum, input_grad, small, lead_grad = last_call(
        frame, hidden_grad, gq, gk, gv, table, sg2, ss2, weights, dp,
        lead_table.shape[0], rows // 6,
    )

    rows_ff = 4 * half
    late_sum = late_sum.astype(F32)
    down_grad = late_sum[:rows_ff]
    up_grad = late_sum[rows_ff : 2 * rows_ff].reshape(4, half, width)
    up_grad = jnp.moveaxis(up_grad, 0, 1).reshape(half, 4 * width)
    output_grad = late_sum[2 * rows_ff : 2 * rows_ff + half]
    size = early_sum.shape[0] // 3
    early_grads = [
        jnp.concatenate([early_sum[at : at + half], early_sum[at + half : at + 2 * half]], 1).astype(F32)
        for at in (0, size, 2 * size)
    ]
    return (
        output, input_grad, small[0], small[1], *early_grads, output_grad,
        small[2], small[3], up_grad, down_grad, lead_grad,
    )


def solution(mesh):
    weight = P("seq", None)
    vector = P("seq")
    batch = P("dp", "seq", None)
    table = P(None, "seq")
    return jax.shard_map(
        body,
        mesh=mesh,
        in_specs=(
            batch, batch, P("dp"), P("dp", None), vector, vector, weight, weight, weight, weight,
            vector, vector, weight, weight, table,
        ),
        out_specs=(
            batch, batch, vector, vector, weight, weight, weight, weight, vector, vector, weight,
            weight, table,
        ),
        check_vma=False,
    )
```

```python
import functools

import jax
import jax.numpy as jnp
from jax import lax
from jax.experimental import pallas as pl
from jax.experimental.pallas import tpu as pltpu
from jax.sharding import PartitionSpec as P

HEAD_DIM = 64
PAIR = 128
EPSILON = 1e-06
LOG2E = 1.4426950408889634
SCORE_SCALE = HEAD_DIM**-0.5
EXP2_SCALE = SCORE_SCALE * LOG2E
BF = jnp.bfloat16
F32 = jnp.float32
VMEM_BYTES = 61 * 2**20
SAFE_LOG2 = 100.0


def dot(left, right):
    return jnp.dot(left, right, preferred_element_type=F32)


def dot_t(left, right):
    return lax.dot_general(left, right, (((1,), (1,)), ((), ())), preferred_element_type=F32)


def dot_l(left, right):
    return lax.dot_general(left, right, (((0,), (0,)), ((), ())), preferred_element_type=F32)


def row_mean(x):
    return jnp.mean(x, axis=1, keepdims=True)


def norm_rows(hidden):
    center = hidden - row_mean(hidden)
    inv_std = lax.rsqrt(row_mean(center * center) + EPSILON)
    return center * inv_std, inv_std


def norm_rows_back(grad_out, normed, inv_std, gain):
    scaled = grad_out * gain
    return inv_std * (scaled - row_mean(scaled) - normed * row_mean(scaled * normed))


def gelu_pair(u):
    z = jnp.abs(u) * 0.7071067811865476
    d = 1.0 + 0.3275911 * z
    t = pl.reciprocal(d, approx=True)
    t = t * (2.0 - d * t)
    e = jnp.exp2(u * u * (-0.5 * LOG2E))
    poly = t * (
        0.127414796
        + t * (-0.142248368 + t * (0.7107068705 + t * (-0.7265760135 + t * 0.5307027145)))
    )
    tail = poly * e
    cdf = jnp.where(u >= 0, 1.0 - tail, tail)
    return u * cdf, cdf + u * (e * 0.3989422804014327)


def params(limit=VMEM_BYTES):
    return pltpu.CompilerParams(vmem_limit_bytes=limit)


def reduce_parts(rows, dp):
    bits = dp.bit_length() - 1
    unit = 16 * dp
    units = rows // unit
    middle = list(range(1, bits))
    orders = [["seq"] + middle, middle + ["seq"]] * 2
    sizes = [(units + 3 - n) // 4 for n in range(4)]
    parts, base = [], 0
    for size, order in zip(sizes, orders):
        if size > 0:
            parts.append((base, size * unit, [0] + order))
            base += size * unit
    return parts


def padded_rows(rows, dp):
    unit = 16 * dp
    return -(-rows // unit) * unit


class Place:
    def __init__(self, dp):
        self.bits = dp.bit_length() - 1
        self.dp = lax.axis_index("dp")
        self.seq = lax.axis_index("seq")

    def bit(self, key):
        return self.seq if key == "seq" else (self.dp // (1 << key)) % 2

    def partner(self, key):
        if key == "seq":
            return (self.dp, 1 - self.seq)
        return (self.dp + (1 << key) * (1 - 2 * self.bit(key)), self.seq)

    def meet(self, keys=None):
        barrier = pltpu.get_barrier_semaphore()
        keys = keys or ["seq"] + list(range(self.bits))
        for key in keys:
            pl.semaphore_signal(
                barrier, inc=1, device_id=self.partner(key), device_id_type=pl.DeviceIdType.MESH
            )
        pl.semaphore_wait(barrier, len(keys))


def send(place, key, src, dst, sems):
    return pltpu.make_async_remote_copy(
        src_ref=src,
        dst_ref=dst,
        send_sem=sems.at[0],
        recv_sem=sems.at[1],
        device_id=place.partner(key),
        device_id_type=pl.DeviceIdType.MESH,
    )


def fetch_other(place, own, full, base, sems):
    eighth = own.shape[0] // 8
    mine, theirs = base
    at = [0]
    for b in range(3):
        at.append(at[-1] + place.bit(b) * (4 * eighth // (1 << b)))

    def rows(start, n):
        return pl.ds(pl.multiple_of(start, 16), n)

    copies = [
        send(
            place, "seq", own.at[rows(at[3], eighth), :], full.at[rows(mine + at[3], eighth), :],
            sems.at[0],
        )
    ]
    for n, b in enumerate((2, 1, 0)):
        there = full.at[rows(theirs + at[b + 1], eighth << n), :]
        copies.append(send(place, b, there, there, sems.at[1 + n]))
    return copies


def reduce_scratch(parts, width):
    shapes = []
    for _, rows, order in parts:
        lead, n = 2, rows // 2
        shapes += [pltpu.VMEM((2, n, width), BF), pltpu.VMEM((2, n, width), BF)]
        for key in order[1:]:
            lead, n = (1, n) if key == "seq" else (lead, n // 2)
            shapes.append(pltpu.VMEM((lead, n, width), BF))
    steps = max(len(order) for _, _, order in parts)
    shapes += [pltpu.SemaphoreType.DMA((len(parts), 2 * steps, 2))]
    shapes += [pltpu.SemaphoreType.DMA((len(parts), 2))]
    return shapes


class Reducer:
    def __init__(self, place, part, index, source, out, refs, sems, local_sems):
        self.place, self.index, self.source, self.out = place, index, source, out
        self.base, self.rows, self.order = part
        self.acc, self.landing = (refs[0], refs[1:]) if refs else (None, None)
        self.sems, self.local = sems, local_sems
        self.copies = {}
        half = self.rows // 2
        seq = place.seq
        off, n, cut = 0, half, False
        self.plan = []
        for key in self.order[1:]:
            if key == "seq":
                leave = (pl.ds(1 - seq, 1), pl.ds(off, n))
                cut = True
                stay = (pl.ds(seq, 1), pl.ds(off, n))
            else:
                n //= 2
                bit = place.bit(key)
                lead = pl.ds(seq, 1) if cut else slice(None)
                leave = (lead, pl.ds(self.row(off + (1 - bit) * n), n))
                off = self.row(off + bit * n)
                stay = (lead, pl.ds(off, n))
            self.plan.append((key, leave, stay))
        self.final_off, self.final_rows = off, n

    @staticmethod
    def row(x):
        return x if isinstance(x, int) else pl.multiple_of(x, 16)

    def absolute(self, off):
        return pl.multiple_of(self.base + self.place.bit(0) * (self.rows // 2) + off, 16)

    def remote(self, step, src, dst, key):
        return pltpu.make_async_remote_copy(
            src_ref=src,
            dst_ref=dst,
            send_sem=self.sems.at[self.index, step, 0],
            recv_sem=self.sems.at[self.index, step, 1],
            device_id=self.place.partner(key),
            device_id_type=pl.DeviceIdType.MESH,
        )

    def scatter(self, step):
        if step == 0:
            half = self.rows // 2
            there = pl.multiple_of(self.base + (1 - self.place.bit(0)) * half, 16)
            return self.remote(0, self.source.at[:, pl.ds(there, half), :], self.landing[0], 0)
        key, leave, _ = self.plan[step - 1]
        return self.remote(step, self.acc.at[leave[0], leave[1], :], self.landing[step], key)

    def keep_copy(self):
        half = self.rows // 2
        here = pl.multiple_of(self.base + self.place.bit(0) * half, 16)
        return pltpu.make_async_copy(
            self.source.at[:, pl.ds(here, half), :], self.acc, self.local.at[self.index, 0]
        )

    def final_copy(self):
        return pltpu.make_async_copy(
            self.acc.at[self.place.seq, pl.ds(self.final_off, self.final_rows), :],
            self.out.at[pl.ds(self.absolute(self.final_off), self.final_rows), :],
            self.local.at[self.index, 1],
        )

    def gather(self, j):
        keys = [key for key in reversed(self.order) if key != "seq"]
        off, n = self.absolute(self.final_off), self.final_rows
        for key in keys[:j]:
            off = off - self.place.bit(key) * n
            n *= 2
        off = pl.multiple_of(off, 16)
        here = self.out.at[pl.ds(off, n), :]
        src = here
        if j == 0 and self.acc is not None:
            src = self.acc.at[self.place.seq, pl.ds(self.final_off, n), :]
        return self.remote(len(self.order) + j, src, here, keys[j])

    def add(self, step):
        landing = self.landing[step]
        if step == 0:
            lead, rows = (0, 2), pl.ds(0, self.rows // 2)
            first = 0
        else:
            _, _, stay = self.plan[step - 1]
            first = stay[0].start if isinstance(stay[0], pl.Slice) else 0
            lead, rows = (0, landing.shape[0]), stay[1]
        n = landing.shape[1]
        size = 32 if n % 32 == 0 else 16
        start = rows.start
        for m in range(lead[1]):

            def some(i, _):
                at = pl.multiple_of(i * size, size)
                here = pl.ds(pl.multiple_of(start + at, 16), size)
                self.acc[first + m, here, :] = (
                    self.acc[first + m, here, :] + landing[m, pl.ds(at, size), :]
                )
                return 0

            lax.fori_loop(0, n // size, some, 0)

    def gather_events(self):
        last = self.place.bits - 1

        def onward(j):
            def run():
                if j > 0:
                    self.gather(j - 1).wait_recv()
                self.gather(j).start()

            return run

        def finish():
            self.gather(last).wait_recv()
            for j in range(last + 1):
                self.gather(j).wait_send()

        return [onward(j) for j in range(last + 1)] + [finish]

    def events(self, gathered=True):
        steps = len(self.order)
        gathers = self.place.bits

        def begin():
            self.keep_copy().start()
            self.scatter(0).start()

        def middle(step):
            def run():
                if step == 1:
                    self.keep_copy().wait()
                self.scatter(step - 1).wait_recv()
                self.add(step - 1)
                if step < steps:
                    self.scatter(step).start()
                else:
                    self.final_copy().start()
                    if gathered:
                        self.gather(0).start()

            return run

        def end_scatter():
            self.final_copy().wait()
            for step in range(steps):
                self.scatter(step).wait_send()

        def onward(j):
            def run():
                if j == 1:
                    self.final_copy().wait()
                self.gather(j - 1).wait_recv()
                self.gather(j).start()

            return run

        def finish():
            self.gather(gathers - 1).wait_recv()
            for step in range(steps):
                self.scatter(step).wait_send()
            for j in range(gathers):
                self.gather(j).wait_send()

        if not gathered:
            return [begin] + [middle(step) for step in range(1, steps + 1)] + [end_scatter]
        return (
            [begin]
            + [middle(step) for step in range(1, steps + 1)]
            + [onward(j) for j in range(1, gathers)]
            + [finish]
        )


def reducers(place, parts, source, out, refs):
    sems, local_sems = refs[-2:]
    made, at = [], 0
    for index, part in enumerate(parts):
        count = 1 + len(part[2])
        made.append(Reducer(place, part, index, source, out, refs[at : at + count], sems, local_sems))
        at += count
    return made


def start_kernel(
    dp, frames, leads_ref, counts_ref, vectors_ref, lead_table, wq, wk, wv,
    q_ref, k_ref, v_ref, frame_out, weight_out, table_ref, bound_ref,
    weights, frame, longest, pack, pack_in, counts, counts_in,
    weight_sems, frame_sems, pack_sems, count_sems, local_sems,
):
    i = pl.program_id(0)
    steps = pl.num_programs(0)
    place = Place(dp)
    seq = place.seq
    rows = frame.shape[0] // 2
    half = wq.shape[0]
    block = q_ref.shape[0]
    pieces = rows // block
    own = (wq, wk, wv)
    chains = [
        fetch_other(place, own[n], weights.at[n], (seq * half, (1 - seq) * half), weight_sems.at[n])
        for n in range(3)
    ]
    pack_copy = send(place, "seq", pack, pack_in, pack_sems)
    count_copies = [
        send(place, b, counts.at[b], counts_in.at[b], count_sems.at[b]) for b in range(place.bits)
    ]

    def count_on(b):
        if b > 0:
            count_copies[b - 1].wait()
            counts[b] = counts[b - 1] + counts_in[b - 1]
        if b < place.bits:
            count_copies[b].start()
    frame_copies = [
        send(
            place, "seq",
            frames.at[1 - seq, pl.ds(c * block, block), :],
            frame.at[pl.ds(rows + c * block, block), :],
            frame_sems.at[c],
        )
        for c in range(pieces)
    ]
    keep = [
        pltpu.make_async_copy(
            own[n], weights.at[n, pl.ds(pl.multiple_of(seq * half, 128), half), :], local_sems.at[n]
        )
        for n in range(3)
    ] + [pltpu.make_async_copy(frames.at[seq], frame.at[pl.ds(0, rows), :], local_sems.at[3])]
    weights_back = pltpu.make_async_copy(weights, weight_out, local_sems.at[4])
    frame_back = pltpu.make_async_copy(frame, frame_out, local_sems.at[5])

    @pl.when(i == 0)
    def _():
        longest[...] = jnp.zeros_like(longest)
        lead, other = leads_ref[seq], leads_ref[1 - seq]
        leads = lead_table.shape[0]
        line = lax.broadcasted_iota(jnp.int32, (8, leads), 0)
        index = lax.broadcasted_iota(jnp.int32, (8, leads), 1)
        hot = jnp.where(line == 4, lead, jnp.where(line == 5, other, -1)) == index
        pack[...] = dot(jnp.where(hot, 1.0, 0.0).astype(BF), lead_table[...])
        pack[0:4, :] = vectors_ref[...].astype(F32)
        counts[0] = jnp.zeros_like(counts[0])
        counts[0, 0:1, 0:leads] = counts_ref[...].astype(F32)
        place.meet()
        pack_copy.start()
        for chain in chains:
            chain[0].start()
        for copy in keep:
            copy.start()
        count_on(0)
        for step in range(3):
            for chain in chains:
                chain[step].wait_recv()
                chain[step + 1].start()
            if step < pieces:
                frame_copies[step].start()
            count_on(step + 1)
        pack_copy.wait()
        here = pl.ds(pl.multiple_of(seq * half, 128), half)
        there = pl.ds(pl.multiple_of((1 - seq) * half, 128), half)
        table_ref[:, here] = pack[...]
        table_ref[:, there] = pack_in[...]
        table_ref[4:5, there] = pack_in[5:6, :]
        table_ref[6:7, :] = jnp.full((1, 2 * half), lead.astype(F32))
        table_ref[7:8, :] = jnp.full((1, 2 * half), other.astype(F32))
        for copy in keep:
            copy.wait()
        for chain in chains:
            chain[3].wait_recv()
            for step in range(4):
                chain[step].wait_send()
        weights_back.start()
        for copy in frame_copies[3:]:
            copy.start()

    for c in range(pieces):

        @pl.when(i == pieces + c)
        def _():
            frame_copies[c].wait()

    @pl.when(i == steps - 1)
    def _():
        frame_back.start()
        for b in range(4, place.bits + 1):
            count_on(b)
        totals = counts[place.bits, 0:1, :]
        lane = lax.broadcasted_iota(jnp.int32, totals.shape, 1)
        leads = lead_table.shape[0]
        mean = jnp.sum(jnp.where(lane < leads, totals, 0.0), axis=1, keepdims=True) / leads
        share = mean / jnp.where(lane < leads, totals, 1.0)
        weight = jnp.sum(jnp.where(lane == leads_ref[seq], share, 0.0), axis=1, keepdims=True)
        table_ref[5:6, :] = jnp.broadcast_to(weight, (1, 2 * half))

    hidden = frame[pl.ds(pl.multiple_of(i * block, block), block), :].astype(F32)
    normed, _ = norm_rows(hidden + table_ref[4:5, :])
    first_in = (normed * table_ref[0:1, :] + table_ref[1:2, :]).astype(BF)
    line = lax.broadcasted_iota(jnp.int32, (2 * half, PAIR), 0)
    column = lax.broadcasted_iota(jnp.int32, (2 * half, PAIR), 1)
    heads = jnp.where(line // HEAD_DIM == column, 1.0, 0.0).astype(BF)
    for n, ref in enumerate((q_ref, k_ref, v_ref)):
        made = dot(first_in, weights[n]).astype(BF)
        ref[...] = made
        if n < 2:
            square = (made.astype(F32) * made.astype(F32)).astype(BF)
            most = jnp.max(dot(square, heads), axis=0, keepdims=True) * 1.02
            longest[n : n + 1, :] = jnp.maximum(longest[n : n + 1, :], most)

    @pl.when(i == steps - 1)
    def _():
        bound_ref[...] = jnp.max(longest[0:1, :] * longest[1:2, :], axis=1, keepdims=True)
        weights_back.wait()
        frame_back.wait()


def start_call(frames, lead_index, lead_counts, vectors, lead_table, own, dp, block):
    rows, width = 2 * frames.shape[1], frames.shape[2]
    pieces = frames.shape[1] // block
    bits = dp.bit_length() - 1
    tile = pl.BlockSpec((block, width), lambda i: (i, 0))
    anys = pl.BlockSpec(memory_space=pl.ANY)
    return pl.pallas_call(
        functools.partial(start_kernel, dp),
        grid=(rows // block,),
        in_specs=[anys, pl.BlockSpec(memory_space=pltpu.SMEM)]
        + [pl.BlockSpec(memory_space=pltpu.VMEM)] * 3
        + [anys] * 3,
        out_specs=[tile] * 3 + [
            anys, anys,
            pl.BlockSpec((8, width), lambda i: (0, 0)),
            pl.BlockSpec((1, 1), lambda i: (0, 0)),
        ],
        out_shape=[jax.ShapeDtypeStruct((rows, width), BF)] * 4
        + [
            jax.ShapeDtypeStruct((3, width, width), BF),
            jax.ShapeDtypeStruct((8, width), F32),
            jax.ShapeDtypeStruct((1, 1), F32),
        ],
        scratch_shapes=[
            pltpu.VMEM((3, width, width), BF),
            pltpu.VMEM((rows, width), BF),
            pltpu.VMEM((8, PAIR), F32),
            pltpu.VMEM((8, width // 2), F32),
            pltpu.VMEM((8, width // 2), F32),
            pltpu.VMEM((bits + 1, 8, PAIR), F32),
            pltpu.VMEM((bits, 8, PAIR), F32),
            pltpu.SemaphoreType.DMA((3, 4, 2)),
            pltpu.SemaphoreType.DMA((pieces, 2)),
            pltpu.SemaphoreType.DMA((2,)),
            pltpu.SemaphoreType.DMA((bits, 2)),
            pltpu.SemaphoreType.DMA((6,)),
        ],
        compiler_params=pltpu.CompilerParams(
            vmem_limit_bytes=VMEM_BYTES, collective_id=2, has_side_effects=True
        ),
    )(frames, lead_index, lead_counts, vectors, lead_table, *own)


def masked_pair(k, v):
    low = lax.broadcasted_iota(jnp.int32, k.shape, 1) < HEAD_DIM
    return (
        (jnp.where(low, k, 0).astype(BF), jnp.where(low, 0, k).astype(BF)),
        (jnp.where(low, v, 1).astype(BF), jnp.where(low, 1, v).astype(BF)),
    )


def attend_rows(query, keys, values, shifted):
    mixed, logs = [], []
    for h in range(2):
        scores = dot_t(query, keys[h])
        if shifted:
            peak = jnp.max(scores, axis=1, keepdims=True)
            scores = scores - peak
        weight = jnp.exp2(scores * EXP2_SCALE).astype(BF)
        total = dot(weight, values[h])
        turned = pltpu.roll(total, HEAD_DIM, 1)
        mixed.append(total / turned)
        log = jnp.log2(turned) * (1.0 / EXP2_SCALE)
        logs.append(log + peak if shifted else log)
    low = lax.broadcasted_iota(jnp.int32, mixed[0].shape, 1) < HEAD_DIM
    return jnp.where(low, mixed[0], mixed[1]).astype(BF), jnp.where(low, logs[0], logs[1])


def attend_kernel(
    dp, q_ref, k_ref, v_ref, targets, wu_own, wd_own, wo_own,
    o_ref, l_ref, target, wu_other, wd_other, wo_other,
    keys, values, chain_sems, target_sems, local_sem,
):
    pair, i = pl.program_id(0), pl.program_id(1)
    pairs, blocks = pl.num_programs(0), pl.num_programs(1)
    slot = pair * blocks + i
    rows, block = k_ref.shape[0], q_ref.shape[0]
    slots = 6 * (rows // block)
    place = Place(dp)
    wu, wd, wo = (
        fetch_other(place, own, other, (0, 0), chain_sems.at[n])
        for n, (own, other) in enumerate(((wu_own, wu_other), (wd_own, wd_other), (wo_own, wo_other)))
    )
    near = targets.shape[1]
    trade = send(
        place, "seq", targets.at[1 - place.seq], target.at[pl.ds(near, near), :], target_sems
    )
    keep = pltpu.make_async_copy(targets.at[place.seq], target.at[pl.ds(0, near), :], local_sem)

    def begin():
        place.meet(["seq", 0, 1, 2])
        wu[0].start()
        keep.start()

    def step_on(chain, step):
        chain[step].wait_recv()
        chain[step + 1].start()

    def first():
        step_on(wu, 0)
        wd[0].start()
        wo[0].start()

    def second():
        step_on(wu, 1)
        step_on(wd, 0)
        step_on(wo, 0)
        trade.start()

    def third():
        step_on(wd, 1)
        step_on(wo, 1)

    def fourth():
        step_on(wd, 2)
        step_on(wo, 2)

    def end():
        for chain in (wu, wd, wo):
            chain[3].wait_recv()
            for copy in chain:
                copy.wait_send()
        trade.wait()
        keep.wait()

    events = [
        (0, begin),
        (2, first),
        (4, second),
        (6, third),
        (8, lambda: step_on(wu, 2)),
        (11, fourth),
    ]
    for at, event in events:
        pl.when(slot == (at * slots) // 12)(event)

    @pl.when(i == 0)
    def _():
        ks, vs = masked_pair(k_ref[...], v_ref[...])
        for h in range(2):
            keys[h] = ks[h]
            values[h] = vs[h]

    o_ref[...], l_ref[...] = attend_rows(q_ref[...], keys, values, False)

    pl.when(slot == slots - 1)(end)


def attend_call(queries, keys, values, targets, late, dp, block):
    rows, width = queries.shape
    tile = pl.BlockSpec((block, PAIR), lambda i, j: (j, i))
    whole = pl.BlockSpec((rows, PAIR), lambda i, j: (0, i))
    anys = pl.BlockSpec(memory_space=pl.ANY)
    wo, wu, wd = late
    return pl.pallas_call(
        functools.partial(attend_kernel, dp),
        grid=(width // PAIR, rows // block),
        in_specs=[tile, whole, whole] + [anys] * 4,
        out_specs=[tile] * 2 + [anys] * 4,
        out_shape=[
            jax.ShapeDtypeStruct((rows, width), BF),
            jax.ShapeDtypeStruct((rows, width), F32),
            jax.ShapeDtypeStruct((rows, width), BF),
        ]
        + [jax.ShapeDtypeStruct(w.shape, BF) for w in (wu, wd, wo)],
        scratch_shapes=[pltpu.VMEM((2, rows, PAIR), BF)] * 2
        + [
            pltpu.SemaphoreType.DMA((3, 4, 2)),
            pltpu.SemaphoreType.DMA((2,)),
            pltpu.SemaphoreType.DMA,
        ],
        compiler_params=pltpu.CompilerParams(
            vmem_limit_bytes=VMEM_BYTES, collective_id=3, has_side_effects=True
        ),
    )(queries, keys, values, targets, wu, wd, wo)


def shifted_kernel(block, bound_ref, q_ref, k_ref, v_ref, o_in, l_in, o_ref, l_ref, q, k, v, o, log):
    @pl.when(jnp.logical_not(bound_ref[0, 0] <= (SAFE_LOG2 / EXP2_SCALE) ** 2))
    def _():
        rows, width = q_ref.shape

        def one_pair(n, _):
            columns = pl.ds(pl.multiple_of(n * PAIR, PAIR), PAIR)
            for src, dst in ((q_ref, q), (k_ref, k), (v_ref, v)):
                pltpu.sync_copy(src.at[:, columns], dst)
            keys, values = masked_pair(k[...], v[...])

            def some(i, _):
                here = pl.ds(pl.multiple_of(i * block, block), block)
                o[here, :], log[here, :] = attend_rows(q[here, :], keys, values, True)
                return 0

            lax.fori_loop(0, rows // block, some, 0)
            pltpu.sync_copy(o, o_ref.at[:, columns])
            pltpu.sync_copy(log, l_ref.at[:, columns])
            return 0

        lax.fori_loop(0, width // PAIR, one_pair, 0)


def shifted_call(bound, queries, keys, values, attended, logs, block):
    rows, width = queries.shape
    anys = pl.BlockSpec(memory_space=pl.ANY)
    return pl.pallas_call(
        functools.partial(shifted_kernel, block),
        in_specs=[pl.BlockSpec(memory_space=pltpu.SMEM)] + [anys] * 5,
        out_specs=[anys] * 2,
        out_shape=[
            jax.ShapeDtypeStruct((rows, width), BF),
            jax.ShapeDtypeStruct((rows, width), F32),
        ],
        input_output_aliases={4: 0, 5: 1},
        scratch_shapes=[pltpu.VMEM((rows, PAIR), BF)] * 4 + [pltpu.VMEM((rows, PAIR), F32)],
        compiler_params=params(),
    )(bound, queries, keys, values, attended, logs)


def feed_kernel(
    block, steps, seq_axis,
    frame_ref, o_ref, o_full, target_ref, emb_ref, gain_ref, shift_ref, weight_ref,
    wo_own, wo_other, wu_own, wu_other, wd_own, wd_other,
    y_ref, gh_ref, go_ref, sg_ref, ss_ref, grads,
    wo, wu, wd, act, slope, second_in, result_grad, hidden_grad, normed_s, hidden_s, acc, stage,
    sems, out_sems,
):
    i = pl.program_id(0)
    seq = lax.axis_index(seq_axis)
    width = wo.shape[0]
    half = width // 2
    chunks = act.shape[0]

    @pl.when(i == 0)
    def _():
        copies = []
        for m, (place, wo_h, wu_h, wd_h) in enumerate(
            ((seq, wo_own, wu_own, wd_own), (1 - seq, wo_other, wu_other, wd_other))
        ):
            rows = pl.ds(pl.multiple_of(place * half, 128), half)
            copies.append(pltpu.make_async_copy(wo_h, wo.at[rows, :], sems.at[m, 0]))
            for c in range(chunks):
                copies.append(
                    pltpu.make_async_copy(
                        wu_h.at[:, pl.ds(c * width, width)], wu.at[c, rows, :], sems.at[m, 1 + c]
                    )
                )
            for c in range(chunks // 2):
                copies.append(
                    pltpu.make_async_copy(
                        wd_h.at[pl.ds(c * width, width), :],
                        wd.at[place * (chunks // 2) + c],
                        sems.at[m, 1 + chunks + c],
                    )
                )
        for copy in copies:
            copy.start()
        for copy in copies:
            copy.wait()
        sg_ref[...] = jnp.zeros_like(sg_ref)
        ss_ref[...] = jnp.zeros_like(ss_ref)
        spare = grads.shape[1] - (2 * chunks + 1) * half
        if spare > 0:
            stage[0] = jnp.zeros_like(stage[0])
            fills = [
                pltpu.make_async_copy(
                    stage.at[0, pl.ds(0, spare), :],
                    grads.at[h, pl.ds((2 * chunks + 1) * half, spare), :],
                    out_sems.at[0, h],
                )
                for h in range(2)
            ]
            for fill in fills:
                fill.start()
            for fill in fills:
                fill.wait()

    @pl.when(i < steps)
    def _():
        rows = pl.ds(pl.multiple_of(i * block, block), block)
        hidden = frame_ref[...].astype(F32) + emb_ref[...] + dot(o_ref[...], wo[...])
        normed, inv_std = norm_rows(hidden)
        normed_s[...] = normed
        second_in[rows, :] = (normed * gain_ref[...] + shift_ref[...]).astype(BF)
        acc[...] = hidden

        u = dot(second_in[rows, :], wu[0])
        for c in range(chunks):
            later = dot(second_in[rows, :], wu[c + 1]) if c + 1 < chunks else None
            a, s = gelu_pair(u)
            a = a.astype(BF)
            act[c, rows, :] = a
            slope[c, rows, :] = s.astype(BF)
            acc[...] += dot(a, wd[c])
            u = later
        result = acc[...]
        y_ref[...] = result.astype(BF)
        grad = weight_ref[...] * (result - target_ref[...].astype(F32))
        result_grad[rows, :] = grad.astype(BF)
        hidden_s[...] = grad
        acc[...] = jnp.zeros_like(acc)

        back = dot_t(result_grad[rows, :], wd[0])
        for c in range(chunks):
            later = dot_t(result_grad[rows, :], wd[c + 1]) if c + 1 < chunks else None
            back = (back * slope[c, rows, :].astype(F32)).astype(BF)
            slope[c, rows, :] = back
            acc[...] += dot_t(back, wu[c])
            back = later
        grad = acc[...]
        normed = normed_s[...]
        ss_ref[...] += jnp.sum(grad, axis=0, keepdims=True)
        sg_ref[...] += jnp.sum(grad * normed, axis=0, keepdims=True)
        grad = hidden_s[...] + norm_rows_back(grad, normed, inv_std, gain_ref[...])
        gh_ref[...] = grad
        grad = grad.astype(BF)
        hidden_grad[rows, :] = grad
        go_ref[...] = dot_t(grad, wo[...]).astype(BF)

    def out_copies(n):
        slot = n % 2
        if n < chunks:
            at = grads.at[n // (chunks // 2), pl.ds((n % (chunks // 2)) * width, width), :]
            return [pltpu.make_async_copy(stage.at[slot], at, out_sems.at[slot, 0])]
        base = (chunks // 2) * width + (n - chunks) * half
        return [
            pltpu.make_async_copy(
                stage.at[slot, pl.ds(h * half, half), :],
                grads.at[h, pl.ds(base, half), :],
                out_sems.at[slot, h],
            )
            for h in range(2)
        ]

    last = 2 * chunks
    for n in range(last + 1):

        @pl.when(i == steps + n)
        def _():
            if n >= 2:
                for copy in out_copies(n - 2):
                    copy.wait()
            if n < chunks:
                term = dot_l(act[n], result_grad[...])
            elif n < last:
                term = dot_l(second_in[...], slope[n - chunks])
            else:
                term = dot_l(o_full[...], hidden_grad[...])
            stage[n % 2] = term.astype(BF)
            for copy in out_copies(n):
                copy.start()
            if n == last:
                for m in (n - 1, n):
                    for copy in out_copies(m):
                        copy.wait()


def feed_call(frame, attended, target, emb, gain, shift, weight, halves, grad_rows, block):
    rows, width = frame.shape
    chunks = halves[2].shape[1] // width
    steps = rows // block
    tile = pl.BlockSpec((block, width), lambda i: (jnp.minimum(i, steps - 1), 0))
    whole = pl.BlockSpec((rows, width), lambda i: (0, 0), pipeline_mode=pl.Buffered(1))
    vec = pl.BlockSpec((1, width), lambda i: (0, 0))
    anys = pl.BlockSpec(memory_space=pl.ANY)
    return pl.pallas_call(
        functools.partial(feed_kernel, block, steps, "seq"),
        grid=(steps + 2 * chunks + 1,),
        in_specs=[tile, tile, whole, tile, vec, vec, vec, vec]
        + [anys] * 6,
        out_specs=[tile, tile, tile, vec, vec, anys],
        out_shape=[
            jax.ShapeDtypeStruct((rows, width), BF),
            jax.ShapeDtypeStruct((rows, width), F32),
            jax.ShapeDtypeStruct((rows, width), BF),
            jax.ShapeDtypeStruct((1, width), F32),
            jax.ShapeDtypeStruct((1, width), F32),
            jax.ShapeDtypeStruct((2, grad_rows, width), BF),
        ],
        scratch_shapes=[
            pltpu.VMEM((width, width), BF),
            pltpu.VMEM((chunks, width, width), BF),
            pltpu.VMEM((chunks, width, width), BF),
            pltpu.VMEM((chunks, rows, width), BF),
            pltpu.VMEM((chunks, rows, width), BF),
            pltpu.VMEM((rows, width), BF),
            pltpu.VMEM((rows, width), BF),
            pltpu.VMEM((rows, width), BF),
            pltpu.VMEM((block, width), F32),
            pltpu.VMEM((block, width), F32),
            pltpu.VMEM((block, width), F32),
            pltpu.VMEM((2, width, width), BF),
            pltpu.SemaphoreType.DMA((2, 1 + chunks + chunks // 2)),
            pltpu.SemaphoreType.DMA((2, 2)),
        ],
        compiler_params=params(),
    )(frame, attended, attended, target, emb, gain, shift, weight, *halves)


def split_three(x):
    first = x.astype(BF)
    rest = x - first.astype(F32)
    second = rest.astype(BF)
    rest = rest - second.astype(F32)
    return first, second, rest.astype(BF)


def attend_back_kernel(
    dp, parts, q_ref, k_ref, v_ref, g_ref, o_ref, l_ref, source, result,
    gq_ref, gk_ref, gv_ref, out, result_out,
    qm, km, vm, gm, acc, trade_sems, *refs
):
    rows = q_ref.shape[0]
    pair, i = pl.program_id(0), pl.program_id(1)
    pairs, blocks = pl.num_programs(0), pl.num_programs(1)
    block = gv_ref.shape[0]
    slot = pair * blocks + i
    slots = 6 * (rows // block)
    place = Place(dp)

    near = result_out.shape[1]
    seq = place.seq
    trade = send(
        place, "seq", result.at[pl.ds(near, near), :], result_out.at[seq], trade_sems
    )
    keep = pltpu.make_async_copy(
        result.at[pl.ds(0, near), :], result_out.at[seq], trade_sems.at[2]
    )

    @pl.when(slot == 0)
    def _():
        place.meet()
        keep.start()

    @pl.when(slot == slots // 2)
    def _():
        trade.start()

    @pl.when(slot == slots - 1)
    def _():
        trade.wait()
        keep.wait()

    for n, reducer in enumerate(reducers(place, parts, source, out, refs)):
        events = reducer.events(n < WHOLE_PARTS)
        for at, event in zip(reduce_slots(len(events), slots, n), events):
            pl.when(slot == at)(event)

    lane = lax.broadcasted_iota(jnp.int32, (rows, PAIR), 1)

    @pl.when(i == 0)
    def _():
        low = lane < HEAD_DIM
        sub = lane % HEAD_DIM
        product = g_ref[...].astype(F32) * o_ref[...].astype(F32)
        first = product.astype(BF)
        line = lax.broadcasted_iota(jnp.int32, (PAIR, PAIR), 0)
        column = lax.broadcasted_iota(jnp.int32, (PAIR, PAIR), 1)
        cross = jnp.where((line < HEAD_DIM) != (column < HEAD_DIM), -1.0, 0.0).astype(BF)
        inner = dot(first, cross) + dot((product - first.astype(F32)).astype(BF), cross)

        def tail(x):
            terms = split_three(x)
            zero = jnp.zeros_like(terms[0])
            return jnp.where(
                sub == 0, terms[0], jnp.where(sub == 1, terms[1], jnp.where(sub == 2, terms[2], zero))
            )

        log_tail = tail(-pltpu.roll(l_ref[...], HEAD_DIM, 1))
        inner_tail = tail(inner)
        ones = jnp.where(sub < 3, 1.0, 0.0).astype(BF)
        for ref, x, extra in (
            (qm, q_ref[...], log_tail), (gm, g_ref[...], inner_tail),
            (km, k_ref[...], ones), (vm, v_ref[...], ones),
        ):
            ref[0] = jnp.where(low, x, extra)
            ref[1] = jnp.where(low, extra, x)
        acc[...] = jnp.zeros_like(acc)

    low_block = lax.broadcasted_iota(jnp.int32, (block, PAIR), 1) < HEAD_DIM
    here = pl.ds(pl.multiple_of(i * block, block), block)
    value_terms, key_terms = [], []
    turned = k_ref[here, :].T
    for h in range(2):
        prob = jnp.exp2(EXP2_SCALE * dot_t(km[h, here, :], qm[h]))
        score = (prob * dot_t(vm[h, here, :], gm[h])).astype(BF)
        value_terms.append(dot(prob.astype(BF), g_ref[...]))
        key_terms.append(dot(score, q_ref[...]))
        acc[h] += dot(turned, score)
    gv_ref[...] = jnp.where(low_block, value_terms[0], value_terms[1]).astype(BF)
    gk_ref[...] = (SCORE_SCALE * jnp.where(low_block, key_terms[0], key_terms[1])).astype(BF)

    @pl.when(i == blocks - 1)
    def _():
        gq_ref[...] = (SCORE_SCALE * jnp.where(lane < HEAD_DIM, acc[0].T, acc[1].T)).astype(BF)


WHOLE_PARTS = 2
REDUCE_SLOTS = (
    (0, 2, 6, 9, 11, 13, 15, 17, 20, 22),
    (0, 2, 6, 9, 11, 13, 15, 17, 20, 22),
    (3, 6, 10, 13, 16, 19, 23),
    (3, 6, 10, 13, 16, 19, 23),
)


def reduce_slots(count, slots, part):
    known = REDUCE_SLOTS[part]
    if len(known) == count:
        return [at * (slots - 1) // known[-1] if slots != 24 else at for at in known]
    return [n * (slots - 1) // (count - 1) for n in range(count)]


def attend_back_call(queries, keys, values, grad, attended, logs, source, result, dp, block):
    rows, width = queries.shape
    tile = pl.BlockSpec((rows, PAIR), lambda i, j: (0, i))
    part_tile = pl.BlockSpec((block, PAIR), lambda i, j: (j, i))
    anys = pl.BlockSpec(memory_space=pl.ANY)
    parts = reduce_parts(source.shape[1], dp)
    return pl.pallas_call(
        functools.partial(attend_back_kernel, dp, parts),
        grid=(width // PAIR, rows // block),
        in_specs=[tile] * 6 + [anys] * 2,
        out_specs=[tile, part_tile, part_tile, anys, anys],
        out_shape=[jax.ShapeDtypeStruct((rows, width), BF)] * 3
        + [
            jax.ShapeDtypeStruct(source.shape[1:], BF),
            jax.ShapeDtypeStruct((2, rows // 2, width), BF),
        ],
        scratch_shapes=[pltpu.VMEM((2, rows, PAIR), BF)] * 4
        + [pltpu.VMEM((2, PAIR, rows), F32), pltpu.SemaphoreType.DMA((3,))]
        + reduce_scratch(parts, width),
        compiler_params=pltpu.CompilerParams(
            vmem_limit_bytes=VMEM_BYTES, collective_id=1, has_side_effects=True
        ),
    )(queries, keys, values, grad, attended, logs, source, result)


def last_kernel(
    dp, parts, late_parts, block,
    frame_ref, gh_ref, gq_ref, gk_ref, gv_ref, table_ref, sg2_ref, ss2_ref, weight_ref, late_in,
    out, gi_out, small_ref, lead_ref, late,
    weights, first_in, source, gi, sums, trade, gathered, weight_sem, gi_sems, keep_sems, small_sems, late_sems,
    *refs,
):
    parts_in = (gq_ref, gk_ref, gv_ref)
    i = pl.program_id(0)
    place = Place(dp)
    seq = place.seq
    rows, width = gq_ref.shape
    half = width // 2
    near = rows // 2
    steps = rows // block
    pieces = near // block
    emb, gain, shift = table_ref[4:5, :], table_ref[0:1, :], table_ref[1:2, :]
    fetch = pltpu.make_async_copy(weight_ref, weights, weight_sem)
    made = [r.events() for r in reducers(place, parts, source, out, refs)]
    late_made = [
        Reducer(place, part, n, None, late, (), late_sems, None).gather_events()
        for n, part in enumerate(late_parts)
    ]

    def late_on(n):
        for events in late_made:
            if n < len(events) - 1:
                events[n]()

    def normed_rows(at):
        hidden = frame_ref[pl.ds(at, block), :].astype(F32) + emb
        return norm_rows(hidden)

    @pl.when(i == 0)
    def _():
        place.meet()
        fetch.start()
        late_on(0)
        sums[...] = jnp.zeros_like(sums)
        if source.shape[1] > 3 * width:
            source[...] = jnp.zeros_like(source)
        fetch.wait()

    for n in range(3):

        @pl.when(i == pieces + n)
        def _():
            if n == 0:

                def some(m, _):
                    at = pl.multiple_of(m * block, block)
                    normed, _ = normed_rows(at)
                    first_in[pl.ds(at, block), :] = (normed * gain + shift).astype(BF)
                    return 0

                lax.fori_loop(0, pieces, some, 0)
            term = dot_l(first_in[...], parts_in[n][...]).astype(BF)
            base = parts[n][0]
            for h in range(2):
                for m in range(2):
                    source[h, pl.ds(base + m * half, half), :] = term[
                        h * half : (h + 1) * half, m * half : (m + 1) * half
                    ]
            made[n][0]()
            late_on(2 + n)

    def gi_copies(n):
        if n < pieces:
            src = gi.at[pl.ds(n * block, block), :]
            return send(place, "seq", src, gi_out.at[seq, pl.ds(n * block, block), :], gi_sems.at[n])
        n -= pieces
        return pltpu.make_async_copy(
            gi.at[pl.ds(near + n * block, block), :],
            gi_out.at[seq, pl.ds(n * block, block), :],
            keep_sems.at[n],
        )

    for n in range(steps):

        @pl.when(i == (n if n < pieces else n + 3))
        def _():
            at = n * block + (near if n < pieces else -near)
            here = pl.ds(at, block)
            grad = dot_t(gq_ref[here, :], weights[0])
            grad += dot_t(gk_ref[here, :], weights[1])
            grad += dot_t(gv_ref[here, :], weights[2])
            normed, inv_std = normed_rows(at)
            if n < pieces:
                first_in[here, :] = (normed * gain + shift).astype(BF)
            sums[1:2, :] += jnp.sum(grad, axis=0, keepdims=True)
            sums[0:1, :] += jnp.sum(grad * normed, axis=0, keepdims=True)
            grad = gh_ref[...] + norm_rows_back(grad, normed, inv_std, gain)
            sums[4:5, :] += jnp.sum(grad, axis=0, keepdims=True)
            gi[pl.ds(n * block, block), :] = grad.astype(BF)
            gi_copies(n).start()
            if n == pieces - 1:
                late_on(1)
            if n >= pieces:
                for events in made:
                    events[n - pieces + 1]()

    def small_copy(step):
        if step == 0:
            return send(place, "seq", trade.at[0], trade.at[1], small_sems.at[0])
        b = step - 1
        start = (place.dp // (1 << b)) * (1 << b)
        group = gathered.at[pl.ds(start, 1 << b)]
        return send(place, b, group, group, small_sems.at[step])

    @pl.when(i == 3 + steps)
    def _():
        sums[2:3, :] = sg2_ref[...]
        sums[3:4, :] = ss2_ref[...]
        here = pl.ds(pl.multiple_of(seq * half, 128), half)
        there = pl.ds(pl.multiple_of((1 - seq) * half, 128), half)
        trade[0] = sums[:, there]
        small_copy(0).start()
        left = [events[pieces + 1 :] for events in made]
        todo = [events[n] for n in range(len(left[0])) for events in left]
        share = -(-len(todo) // (place.bits + 2))
        for event in todo[:share]:
            event()
        small_copy(0).wait()
        mine, theirs = sums[:, here], trade[1]
        line = lax.broadcasted_iota(jnp.int32, (8, half), 0)
        turned = jnp.broadcast_to(theirs[4:5, :], (8, half))
        value = jnp.where(line < 4, mine + theirs, jnp.where(line == 4, mine, turned))
        value = jnp.where(line == 6, table_ref[6:7, 0:half], value)
        value = jnp.where(line == 7, table_ref[7:8, 0:half], value)
        gathered[place.dp] = value
        for step in range(1, place.bits + 1):
            small_copy(step).start()
            for event in todo[step * share : (step + 1) * share]:
                event()
            small_copy(step).wait()
        for event in todo[(place.bits + 1) * share :]:
            event()
        index = lax.broadcasted_iota(jnp.int32, lead_ref.shape, 0).astype(F32)
        small_ref[...] = jnp.zeros_like(small_ref)
        lead_ref[...] = jnp.zeros_like(lead_ref)

        def add_device(d, _):
            value = gathered[d]
            small_ref[...] += value
            lead_ref[...] += jnp.where(index == value[6:7, :], value[4:5, :], 0.0) + jnp.where(
                index == value[7:8, :], value[5:6, :], 0.0
            )
            return 0

        lax.fori_loop(0, dp, add_device, 0)
        for n in range(steps):
            gi_copies(n).wait()
        for n in range(5, place.bits):
            late_on(n)
        for events in late_made:
            events[-1]()


def last_call(
    frame, hidden_grad, gq, gk, gv, table, sg2, ss2, weights, late, dp, lead_count, block
):
    rows, width = frame.shape
    half = width // 2
    steps = rows // block
    pieces = steps // 2
    size = padded_rows(width, dp)
    bits = dp.bit_length() - 1
    middle = list(range(1, bits))
    orders = [middle + ["seq"], middle[1:] + ["seq"] + middle[:1], ["seq"] + middle]
    late_parts = reduce_parts(late.shape[0], dp)[WHOLE_PARTS:]
    parts = [(n * size, size, [0] + order) for n, order in enumerate(orders)]
    whole = pl.BlockSpec((rows, width), lambda i: (0, 0))

    def turn(i):
        return (jnp.where(i < pieces, i + pieces, jnp.clip(i - 3 - pieces, 0, pieces - 1)), 0)

    def fixed(*shape):
        return pl.BlockSpec(shape, lambda i: (0,) * len(shape))

    vec = fixed(1, width)
    anys = pl.BlockSpec(memory_space=pl.ANY)
    return pl.pallas_call(
        functools.partial(last_kernel, dp, parts, late_parts, block),
        grid=(4 + steps,),
        in_specs=[whole, pl.BlockSpec((block, width), turn), whole, whole, whole]
        + [fixed(8, width), vec, vec, anys, anys],
        out_specs=[anys, anys, fixed(8, half), fixed(lead_count, half), anys],
        input_output_aliases={9: 4},
        out_shape=[
            jax.ShapeDtypeStruct((3 * size, half), BF),
            jax.ShapeDtypeStruct((2, rows // 2, width), BF),
            jax.ShapeDtypeStruct((8, half), F32),
            jax.ShapeDtypeStruct((lead_count, half), F32),
            jax.ShapeDtypeStruct(late.shape, BF),
        ],
        scratch_shapes=[
            pltpu.VMEM((3, width, width), BF),
            pltpu.VMEM((rows, width), BF),
            pltpu.VMEM((2, 3 * size, half), BF),
            pltpu.VMEM((rows, width), BF),
            pltpu.VMEM((8, width), F32),
            pltpu.VMEM((2, 8, half), F32),
            pltpu.VMEM((dp, 8, half), F32),
            pltpu.SemaphoreType.DMA,
            pltpu.SemaphoreType.DMA((pieces, 2)),
            pltpu.SemaphoreType.DMA((pieces,)),
            pltpu.SemaphoreType.DMA((bits + 1, 2)),
            pltpu.SemaphoreType.DMA((max(len(late_parts), 1), 2 * (bits + 1), 2)),
        ]
        + reduce_scratch(parts, half),
        compiler_params=pltpu.CompilerParams(
            vmem_limit_bytes=VMEM_BYTES, collective_id=4, has_side_effects=True
        ),
    )(frame, hidden_grad, gq, gk, gv, table, sg2, ss2, weights, late)


def body(
    frames, targets, lead_index, lead_counts,
    first_gain, first_shift, query_weight, key_weight, value_weight, output_weight,
    second_gain, second_shift, up_weight, down_weight, lead_table,
):
    dp = lax.axis_size("dp")
    rows, width = frames.shape[1] * 2, frames.shape[2]
    half = width // 2
    vectors = jnp.concatenate([first_gain, first_shift, second_gain, second_shift]).reshape(4, half)

    early = (query_weight, key_weight, value_weight)
    late = (output_weight, up_weight, down_weight)
    queries, keys, values, frame, weights, table, bound = start_call(
        frames, lead_index, lead_counts, vectors, lead_table, early, dp, rows // 6
    )
    gain2, shift2, emb, frame_weight = (table[n : n + 1] for n in (2, 3, 4, 5))
    attended, logs, target, wu_other, wd_other, wo_other = attend_call(
        queries, keys, values, targets, late, dp, rows // 2
    )
    attended, logs = shifted_call(bound, queries, keys, values, attended, logs, rows // 4)
    halves = (output_weight, wo_other, up_weight, wu_other, down_weight, wd_other)
    result, hidden_grad, attended_grad, sg2, ss2, grads = feed_call(
        frame, attended, target, emb, gain2, shift2, frame_weight, halves,
        padded_rows(9 * half, dp), rows // 6,
    )
    gq, gk, gv, late_sum, output = attend_back_call(
        queries, keys, values, attended_grad, attended, logs, grads, result, dp, rows // 4
    )
    early_sum, input_grad, small, lead_grad, late_sum = last_call(
        frame, hidden_grad, gq, gk, gv, table, sg2, ss2, weights, late_sum, dp,
        lead_table.shape[0], rows // 6,
    )

    rows_ff = 4 * half
    late_sum = late_sum.astype(F32)
    down_grad = late_sum[:rows_ff]
    up_grad = late_sum[rows_ff : 2 * rows_ff].reshape(4, half, width)
    up_grad = jnp.moveaxis(up_grad, 0, 1).reshape(half, 4 * width)
    output_grad = late_sum[2 * rows_ff : 2 * rows_ff + half]
    size = early_sum.shape[0] // 3
    early_grads = [
        jnp.concatenate([early_sum[at : at + half], early_sum[at + half : at + 2 * half]], 1).astype(F32)
        for at in (0, size, 2 * size)
    ]
    return (
        output, input_grad, small[0], small[1], *early_grads, output_grad,
        small[2], small[3], up_grad, down_grad, lead_grad,
    )


def solution(mesh):
    weight = P("seq", None)
    vector = P("seq")
    batch = P("dp", "seq", None)
    table = P(None, "seq")
    return jax.shard_map(
        body,
        mesh=mesh,
        in_specs=(
            batch, batch, P("dp"), P("dp", None), vector, vector, weight, weight, weight, weight,
            vector, vector, weight, weight, table,
        ),
        out_specs=(
            batch, batch, vector, vector, weight, weight, weight, weight, vector, vector, weight,
            weight, table,
        ),
        check_vma=False,
    )
```

```python
import functools

import jax
import jax.numpy as jnp
from jax import lax
from jax.experimental import pallas as pl
from jax.experimental.pallas import tpu as pltpu
from jax.sharding import PartitionSpec as P

HEAD_DIM = 64
PAIR = 128
EPSILON = 1e-06
LOG2E = 1.4426950408889634
SCORE_SCALE = HEAD_DIM**-0.5
EXP2_SCALE = SCORE_SCALE * LOG2E
BF = jnp.bfloat16
F32 = jnp.float32
VMEM_BYTES = 61 * 2**20
SAFE_LOG2 = 100.0


def dot(left, right):
    return jnp.dot(left, right, preferred_element_type=F32)


def dot_t(left, right):
    return lax.dot_general(left, right, (((1,), (1,)), ((), ())), preferred_element_type=F32)


def dot_l(left, right):
    return lax.dot_general(left, right, (((0,), (0,)), ((), ())), preferred_element_type=F32)


def row_mean(x):
    return jnp.mean(x, axis=1, keepdims=True)


def norm_rows(hidden):
    center = hidden - row_mean(hidden)
    inv_std = lax.rsqrt(row_mean(center * center) + EPSILON)
    return center * inv_std, inv_std


def norm_rows_back(grad_out, normed, inv_std, gain):
    scaled = grad_out * gain
    return inv_std * (scaled - row_mean(scaled) - normed * row_mean(scaled * normed))


def gelu_pair(u):
    z = jnp.abs(u) * 0.7071067811865476
    d = 1.0 + 0.3275911 * z
    t = pl.reciprocal(d, approx=True)
    t = t * (2.0 - d * t)
    e = jnp.exp2(u * u * (-0.5 * LOG2E))
    poly = t * (
        0.127414796
        + t * (-0.142248368 + t * (0.7107068705 + t * (-0.7265760135 + t * 0.5307027145)))
    )
    tail = poly * e
    cdf = jnp.where(u >= 0, 1.0 - tail, tail)
    return u * cdf, cdf + u * (e * 0.3989422804014327)


def params(limit=VMEM_BYTES):
    return pltpu.CompilerParams(vmem_limit_bytes=limit)


def reduce_parts(rows, dp):
    bits = dp.bit_length() - 1
    unit = 16 * dp
    units = rows // unit
    middle = list(range(1, bits))
    orders = [["seq"] + middle, middle + ["seq"]] * 2
    sizes = [(units + 3 - n) // 4 for n in range(4)]
    parts, base = [], 0
    for size, order in zip(sizes, orders):
        if size > 0:
            parts.append((base, size * unit, [0] + order))
            base += size * unit
    return parts


def padded_rows(rows, dp):
    unit = 16 * dp
    return -(-rows // unit) * unit


class Place:
    def __init__(self, dp):
        self.bits = dp.bit_length() - 1
        self.dp = lax.axis_index("dp")
        self.seq = lax.axis_index("seq")

    def bit(self, key):
        return self.seq if key == "seq" else (self.dp // (1 << key)) % 2

    def partner(self, key):
        if key == "seq":
            return (self.dp, 1 - self.seq)
        return (self.dp + (1 << key) * (1 - 2 * self.bit(key)), self.seq)

    def meet(self, keys=None):
        barrier = pltpu.get_barrier_semaphore()
        keys = keys or ["seq"] + list(range(self.bits))
        for key in keys:
            pl.semaphore_signal(
                barrier, inc=1, device_id=self.partner(key), device_id_type=pl.DeviceIdType.MESH
            )
        pl.semaphore_wait(barrier, len(keys))


def send(place, key, src, dst, sems):
    return pltpu.make_async_remote_copy(
        src_ref=src,
        dst_ref=dst,
        send_sem=sems.at[0],
        recv_sem=sems.at[1],
        device_id=place.partner(key),
        device_id_type=pl.DeviceIdType.MESH,
    )


def fetch_other(place, own, full, base, sems):
    eighth = own.shape[0] // 8
    mine, theirs = base
    at = [0]
    for b in range(3):
        at.append(at[-1] + place.bit(b) * (4 * eighth // (1 << b)))

    def rows(start, n):
        return pl.ds(pl.multiple_of(start, 16), n)

    copies = [
        send(
            place, "seq", own.at[rows(at[3], eighth), :], full.at[rows(mine + at[3], eighth), :],
            sems.at[0],
        )
    ]
    for n, b in enumerate((2, 1, 0)):
        there = full.at[rows(theirs + at[b + 1], eighth << n), :]
        copies.append(send(place, b, there, there, sems.at[1 + n]))
    return copies


def reduce_scratch(parts, width):
    shapes = []
    for _, rows, order in parts:
        lead, n = 2, rows // 2
        shapes += [pltpu.VMEM((2, n, width), BF), pltpu.VMEM((2, n, width), BF)]
        for key in order[1:]:
            lead, n = (1, n) if key == "seq" else (lead, n // 2)
            shapes.append(pltpu.VMEM((lead, n, width), BF))
    steps = max(len(order) for _, _, order in parts)
    shapes += [pltpu.SemaphoreType.DMA((len(parts), 2 * steps, 2))]
    shapes += [pltpu.SemaphoreType.DMA((len(parts), 2))]
    return shapes


class Reducer:
    def __init__(self, place, part, index, source, out, refs, sems, local_sems):
        self.place, self.index, self.source, self.out = place, index, source, out
        self.base, self.rows, self.order = part
        self.acc, self.landing = (refs[0], refs[1:]) if refs else (None, None)
        self.sems, self.local = sems, local_sems
        self.copies = {}
        half = self.rows // 2
        seq = place.seq
        off, n, cut = 0, half, False
        self.plan = []
        for key in self.order[1:]:
            if key == "seq":
                leave = (pl.ds(1 - seq, 1), pl.ds(off, n))
                cut = True
                stay = (pl.ds(seq, 1), pl.ds(off, n))
            else:
                n //= 2
                bit = place.bit(key)
                lead = pl.ds(seq, 1) if cut else slice(None)
                leave = (lead, pl.ds(self.row(off + (1 - bit) * n), n))
                off = self.row(off + bit * n)
                stay = (lead, pl.ds(off, n))
            self.plan.append((key, leave, stay))
        self.final_off, self.final_rows = off, n

    @staticmethod
    def row(x):
        return x if isinstance(x, int) else pl.multiple_of(x, 16)

    def absolute(self, off):
        return pl.multiple_of(self.base + self.place.bit(0) * (self.rows // 2) + off, 16)

    def remote(self, step, src, dst, key):
        return pltpu.make_async_remote_copy(
            src_ref=src,
            dst_ref=dst,
            send_sem=self.sems.at[self.index, step, 0],
            recv_sem=self.sems.at[self.index, step, 1],
            device_id=self.place.partner(key),
            device_id_type=pl.DeviceIdType.MESH,
        )

    def scatter(self, step):
        if step == 0:
            half = self.rows // 2
            there = pl.multiple_of(self.base + (1 - self.place.bit(0)) * half, 16)
            return self.remote(0, self.source.at[:, pl.ds(there, half), :], self.landing[0], 0)
        key, leave, _ = self.plan[step - 1]
        return self.remote(step, self.acc.at[leave[0], leave[1], :], self.landing[step], key)

    def keep_copy(self):
        half = self.rows // 2
        here = pl.multiple_of(self.base + self.place.bit(0) * half, 16)
        return pltpu.make_async_copy(
            self.source.at[:, pl.ds(here, half), :], self.acc, self.local.at[self.index, 0]
        )

    def final_copy(self):
        return pltpu.make_async_copy(
            self.acc.at[self.place.seq, pl.ds(self.final_off, self.final_rows), :],
            self.out.at[pl.ds(self.absolute(self.final_off), self.final_rows), :],
            self.local.at[self.index, 1],
        )

    def gather(self, j):
        keys = [key for key in reversed(self.order) if key != "seq"]
        off, n = self.absolute(self.final_off), self.final_rows
        for key in keys[:j]:
            off = off - self.place.bit(key) * n
            n *= 2
        off = pl.multiple_of(off, 16)
        here = self.out.at[pl.ds(off, n), :]
        src = here
        if j == 0 and self.acc is not None:
            src = self.acc.at[self.place.seq, pl.ds(self.final_off, n), :]
        return self.remote(len(self.order) + j, src, here, keys[j])

    def add(self, step):
        landing = self.landing[step]
        if step == 0:
            lead, rows = (0, 2), pl.ds(0, self.rows // 2)
            first = 0
        else:
            _, _, stay = self.plan[step - 1]
            first = stay[0].start if isinstance(stay[0], pl.Slice) else 0
            lead, rows = (0, landing.shape[0]), stay[1]
        n = landing.shape[1]
        size = 32 if n % 32 == 0 else 16
        start = rows.start
        for m in range(lead[1]):

            def some(i, _):
                at = pl.multiple_of(i * size, size)
                here = pl.ds(pl.multiple_of(start + at, 16), size)
                self.acc[first + m, here, :] = (
                    self.acc[first + m, here, :] + landing[m, pl.ds(at, size), :]
                )
                return 0

            lax.fori_loop(0, n // size, some, 0)

    def gather_events(self):
        last = self.place.bits - 1

        def onward(j):
            def run():
                if j > 0:
                    self.gather(j - 1).wait_recv()
                self.gather(j).start()

            return run

        def finish():
            self.gather(last).wait_recv()
            for j in range(last + 1):
                self.gather(j).wait_send()

        return [onward(j) for j in range(last + 1)] + [finish]

    def events(self, gathered=True):
        steps = len(self.order)
        gathers = self.place.bits

        def begin():
            self.keep_copy().start()
            self.scatter(0).start()

        def middle(step):
            def run():
                if step == 1:
                    self.keep_copy().wait()
                self.scatter(step - 1).wait_recv()
                self.add(step - 1)
                if step < steps:
                    self.scatter(step).start()
                else:
                    self.final_copy().start()
                    if gathered:
                        self.gather(0).start()

            return run

        def end_scatter():
            self.final_copy().wait()
            for step in range(steps):
                self.scatter(step).wait_send()

        def onward(j):
            def run():
                if j == 1:
                    self.final_copy().wait()
                self.gather(j - 1).wait_recv()
                self.gather(j).start()

            return run

        def finish():
            self.gather(gathers - 1).wait_recv()
            for step in range(steps):
                self.scatter(step).wait_send()
            for j in range(gathers):
                self.gather(j).wait_send()

        if not gathered:
            return [begin] + [middle(step) for step in range(1, steps + 1)] + [end_scatter]
        return (
            [begin]
            + [middle(step) for step in range(1, steps + 1)]
            + [onward(j) for j in range(1, gathers)]
            + [finish]
        )


def reducers(place, parts, source, out, refs):
    sems, local_sems = refs[-2:]
    made, at = [], 0
    for index, part in enumerate(parts):
        count = 1 + len(part[2])
        made.append(Reducer(place, part, index, source, out, refs[at : at + count], sems, local_sems))
        at += count
    return made


def start_kernel(
    dp, frames, leads_ref, counts_ref, vectors_ref, lead_table, wq, wk, wv,
    q_ref, k_ref, v_ref, frame_out, weight_out, table_ref, bound_ref,
    weights, frame, longest, pack, pack_in, counts, counts_in,
    weight_sems, frame_sems, pack_sems, count_sems, local_sems,
):
    i = pl.program_id(0)
    steps = pl.num_programs(0)
    place = Place(dp)
    seq = place.seq
    rows = frame.shape[0] // 2
    half = wq.shape[0]
    block = q_ref.shape[0]
    pieces = rows // block
    own = (wq, wk, wv)
    chains = [
        fetch_other(place, own[n], weights.at[n], (seq * half, (1 - seq) * half), weight_sems.at[n])
        for n in range(3)
    ]
    pack_copy = send(place, "seq", pack, pack_in, pack_sems)
    count_copies = [
        send(place, b, counts.at[b], counts_in.at[b], count_sems.at[b]) for b in range(place.bits)
    ]

    def count_on(b):
        if b > 0:
            count_copies[b - 1].wait()
            counts[b] = counts[b - 1] + counts_in[b - 1]
        if b < place.bits:
            count_copies[b].start()
    frame_copies = [
        send(
            place, "seq",
            frames.at[1 - seq, pl.ds(c * block, block), :],
            frame.at[pl.ds(rows + c * block, block), :],
            frame_sems.at[c],
        )
        for c in range(pieces)
    ]
    keep = [
        pltpu.make_async_copy(
            own[n], weights.at[n, pl.ds(pl.multiple_of(seq * half, 128), half), :], local_sems.at[n]
        )
        for n in range(3)
    ] + [pltpu.make_async_copy(frames.at[seq], frame.at[pl.ds(0, rows), :], local_sems.at[3])]
    weights_back = pltpu.make_async_copy(weights, weight_out, local_sems.at[4])
    frame_back = pltpu.make_async_copy(frame, frame_out, local_sems.at[5])

    @pl.when(i == 0)
    def _():
        longest[...] = jnp.zeros_like(longest)
        lead, other = leads_ref[seq], leads_ref[1 - seq]
        leads = lead_table.shape[0]
        line = lax.broadcasted_iota(jnp.int32, (8, leads), 0)
        index = lax.broadcasted_iota(jnp.int32, (8, leads), 1)
        hot = jnp.where(line == 4, lead, jnp.where(line == 5, other, -1)) == index
        pack[...] = dot(jnp.where(hot, 1.0, 0.0).astype(BF), lead_table[...])
        pack[0:4, :] = vectors_ref[...].astype(F32)
        counts[0] = jnp.zeros_like(counts[0])
        counts[0, 0:1, 0:leads] = counts_ref[...].astype(F32)
        place.meet()
        pack_copy.start()
        for chain in chains:
            chain[0].start()
        for copy in keep:
            copy.start()
        count_on(0)
        for step in range(3):
            for chain in chains:
                chain[step].wait_recv()
                chain[step + 1].start()
            if step < pieces:
                frame_copies[step].start()
            count_on(step + 1)
        pack_copy.wait()
        here = pl.ds(pl.multiple_of(seq * half, 128), half)
        there = pl.ds(pl.multiple_of((1 - seq) * half, 128), half)
        table_ref[:, here] = pack[...]
        table_ref[:, there] = pack_in[...]
        table_ref[4:5, there] = pack_in[5:6, :]
        table_ref[6:7, :] = jnp.full((1, 2 * half), lead.astype(F32))
        table_ref[7:8, :] = jnp.full((1, 2 * half), other.astype(F32))
        for copy in keep:
            copy.wait()
        for chain in chains:
            chain[3].wait_recv()
            for step in range(4):
                chain[step].wait_send()
        weights_back.start()
        for copy in frame_copies[3:]:
            copy.start()

    for c in range(pieces):

        @pl.when(i == pieces + c)
        def _():
            frame_copies[c].wait()

    @pl.when(i == steps - 1)
    def _():
        frame_back.start()
        for b in range(4, place.bits + 1):
            count_on(b)
        totals = counts[place.bits, 0:1, :]
        lane = lax.broadcasted_iota(jnp.int32, totals.shape, 1)
        leads = lead_table.shape[0]
        mean = jnp.sum(jnp.where(lane < leads, totals, 0.0), axis=1, keepdims=True) / leads
        share = mean / jnp.where(lane < leads, totals, 1.0)
        weight = jnp.sum(jnp.where(lane == leads_ref[seq], share, 0.0), axis=1, keepdims=True)
        table_ref[5:6, :] = jnp.broadcast_to(weight, (1, 2 * half))

    hidden = frame[pl.ds(pl.multiple_of(i * block, block), block), :].astype(F32)
    normed, _ = norm_rows(hidden + table_ref[4:5, :])
    first_in = (normed * table_ref[0:1, :] + table_ref[1:2, :]).astype(BF)
    line = lax.broadcasted_iota(jnp.int32, (2 * half, PAIR), 0)
    column = lax.broadcasted_iota(jnp.int32, (2 * half, PAIR), 1)
    heads = jnp.where(line // HEAD_DIM == column, 1.0, 0.0).astype(BF)
    for n, ref in enumerate((q_ref, k_ref, v_ref)):
        made = dot(first_in, weights[n]).astype(BF)
        ref[...] = made
        if n < 2:
            square = (made.astype(F32) * made.astype(F32)).astype(BF)
            most = jnp.max(dot(square, heads), axis=0, keepdims=True) * 1.02
            longest[n : n + 1, :] = jnp.maximum(longest[n : n + 1, :], most)

    @pl.when(i == steps - 1)
    def _():
        bound_ref[...] = jnp.max(longest[0:1, :] * longest[1:2, :], axis=1, keepdims=True)
        weights_back.wait()
        frame_back.wait()


def start_call(frames, lead_index, lead_counts, vectors, lead_table, own, dp, block):
    rows, width = 2 * frames.shape[1], frames.shape[2]
    pieces = frames.shape[1] // block
    bits = dp.bit_length() - 1
    tile = pl.BlockSpec((block, width), lambda i: (i, 0))
    anys = pl.BlockSpec(memory_space=pl.ANY)
    return pl.pallas_call(
        functools.partial(start_kernel, dp),
        grid=(rows // block,),
        in_specs=[anys, pl.BlockSpec(memory_space=pltpu.SMEM)]
        + [pl.BlockSpec(memory_space=pltpu.VMEM)] * 3
        + [anys] * 3,
        out_specs=[tile] * 3 + [
            anys, anys,
            pl.BlockSpec((8, width), lambda i: (0, 0)),
            pl.BlockSpec((1, 1), lambda i: (0, 0)),
        ],
        out_shape=[jax.ShapeDtypeStruct((rows, width), BF)] * 4
        + [
            jax.ShapeDtypeStruct((3, width, width), BF),
            jax.ShapeDtypeStruct((8, width), F32),
            jax.ShapeDtypeStruct((1, 1), F32),
        ],
        scratch_shapes=[
            pltpu.VMEM((3, width, width), BF),
            pltpu.VMEM((rows, width), BF),
            pltpu.VMEM((8, PAIR), F32),
            pltpu.VMEM((8, width // 2), F32),
            pltpu.VMEM((8, width // 2), F32),
            pltpu.VMEM((bits + 1, 8, PAIR), F32),
            pltpu.VMEM((bits, 8, PAIR), F32),
            pltpu.SemaphoreType.DMA((3, 4, 2)),
            pltpu.SemaphoreType.DMA((pieces, 2)),
            pltpu.SemaphoreType.DMA((2,)),
            pltpu.SemaphoreType.DMA((bits, 2)),
            pltpu.SemaphoreType.DMA((6,)),
        ],
        compiler_params=pltpu.CompilerParams(
            vmem_limit_bytes=VMEM_BYTES, collective_id=2, has_side_effects=True
        ),
    )(frames, lead_index, lead_counts, vectors, lead_table, *own)


def masked_pair(k, v):
    low = lax.broadcasted_iota(jnp.int32, k.shape, 1) < HEAD_DIM
    return (
        (jnp.where(low, k, 0).astype(BF), jnp.where(low, 0, k).astype(BF)),
        (jnp.where(low, v, 1).astype(BF), jnp.where(low, 1, v).astype(BF)),
    )


def attend_rows(query, keys, values, shifted):
    mixed, logs = [], []
    for h in range(2):
        scores = dot_t(query, keys[h])
        if shifted:
            peak = jnp.max(scores, axis=1, keepdims=True)
            scores = scores - peak
        weight = jnp.exp2(scores * EXP2_SCALE).astype(BF)
        total = dot(weight, values[h])
        turned = pltpu.roll(total, HEAD_DIM, 1)
        mixed.append(total / turned)
        log = jnp.log2(turned) * (1.0 / EXP2_SCALE)
        logs.append(log + peak if shifted else log)
    low = lax.broadcasted_iota(jnp.int32, mixed[0].shape, 1) < HEAD_DIM
    return jnp.where(low, mixed[0], mixed[1]).astype(BF), jnp.where(low, logs[0], logs[1])


def attend_kernel(
    dp, q_ref, k_ref, v_ref, targets, wu_own, wd_own, wo_own,
    o_ref, l_ref, target, wu_other, wd_other, wo_other,
    keys, values, chain_sems, target_sems, local_sem,
):
    pair, i = pl.program_id(0), pl.program_id(1)
    pairs, blocks = pl.num_programs(0), pl.num_programs(1)
    slot = pair * blocks + i
    rows, block = k_ref.shape[0], q_ref.shape[0]
    slots = 6 * (rows // block)
    place = Place(dp)
    wu, wd, wo = (
        fetch_other(place, own, other, (0, 0), chain_sems.at[n])
        for n, (own, other) in enumerate(((wu_own, wu_other), (wd_own, wd_other), (wo_own, wo_other)))
    )
    near = targets.shape[1]
    trade = send(
        place, "seq", targets.at[1 - place.seq], target.at[pl.ds(near, near), :], target_sems
    )
    keep = pltpu.make_async_copy(targets.at[place.seq], target.at[pl.ds(0, near), :], local_sem)

    def begin():
        place.meet(["seq", 0, 1, 2])
        wu[0].start()
        keep.start()

    def step_on(chain, step):
        chain[step].wait_recv()
        chain[step + 1].start()

    def first():
        step_on(wu, 0)
        wd[0].start()
        wo[0].start()

    def second():
        step_on(wu, 1)
        step_on(wd, 0)
        step_on(wo, 0)
        trade.start()

    def third():
        step_on(wd, 1)
        step_on(wo, 1)

    def fourth():
        step_on(wd, 2)
        step_on(wo, 2)

    def end():
        for chain in (wu, wd, wo):
            chain[3].wait_recv()
            for copy in chain:
                copy.wait_send()
        trade.wait()
        keep.wait()

    events = [
        (0, begin),
        (2, first),
        (4, second),
        (6, third),
        (8, lambda: step_on(wu, 2)),
        (11, fourth),
    ]
    for at, event in events:
        pl.when(slot == (at * slots) // 12)(event)

    @pl.when(i == 0)
    def _():
        ks, vs = masked_pair(k_ref[...], v_ref[...])
        for h in range(2):
            keys[h] = ks[h]
            values[h] = vs[h]

    o_ref[...], l_ref[...] = attend_rows(q_ref[...], keys, values, False)

    pl.when(slot == slots - 1)(end)


def attend_call(queries, keys, values, targets, late, dp, block):
    rows, width = queries.shape
    tile = pl.BlockSpec((block, PAIR), lambda i, j: (j, i))
    whole = pl.BlockSpec((rows, PAIR), lambda i, j: (0, i))
    anys = pl.BlockSpec(memory_space=pl.ANY)
    wo, wu, wd = late
    return pl.pallas_call(
        functools.partial(attend_kernel, dp),
        grid=(width // PAIR, rows // block),
        in_specs=[tile, whole, whole] + [anys] * 4,
        out_specs=[tile] * 2 + [anys] * 4,
        out_shape=[
            jax.ShapeDtypeStruct((rows, width), BF),
            jax.ShapeDtypeStruct((rows, width), F32),
            jax.ShapeDtypeStruct((rows, width), BF),
        ]
        + [jax.ShapeDtypeStruct(w.shape, BF) for w in (wu, wd, wo)],
        scratch_shapes=[pltpu.VMEM((2, rows, PAIR), BF)] * 2
        + [
            pltpu.SemaphoreType.DMA((3, 4, 2)),
            pltpu.SemaphoreType.DMA((2,)),
            pltpu.SemaphoreType.DMA,
        ],
        compiler_params=pltpu.CompilerParams(
            vmem_limit_bytes=VMEM_BYTES, collective_id=3, has_side_effects=True
        ),
    )(queries, keys, values, targets, wu, wd, wo)


def shifted_kernel(block, bound_ref, q_ref, k_ref, v_ref, o_in, l_in, o_ref, l_ref, q, k, v, o, log):
    @pl.when(jnp.logical_not(bound_ref[0, 0] <= (SAFE_LOG2 / EXP2_SCALE) ** 2))
    def _():
        rows, width = q_ref.shape

        def one_pair(n, _):
            columns = pl.ds(pl.multiple_of(n * PAIR, PAIR), PAIR)
            for src, dst in ((q_ref, q), (k_ref, k), (v_ref, v)):
                pltpu.sync_copy(src.at[:, columns], dst)
            keys, values = masked_pair(k[...], v[...])

            def some(i, _):
                here = pl.ds(pl.multiple_of(i * block, block), block)
                o[here, :], log[here, :] = attend_rows(q[here, :], keys, values, True)
                return 0

            lax.fori_loop(0, rows // block, some, 0)
            pltpu.sync_copy(o, o_ref.at[:, columns])
            pltpu.sync_copy(log, l_ref.at[:, columns])
            return 0

        lax.fori_loop(0, width // PAIR, one_pair, 0)


def shifted_call(bound, queries, keys, values, attended, logs, block):
    rows, width = queries.shape
    anys = pl.BlockSpec(memory_space=pl.ANY)
    return pl.pallas_call(
        functools.partial(shifted_kernel, block),
        in_specs=[pl.BlockSpec(memory_space=pltpu.SMEM)] + [anys] * 5,
        out_specs=[anys] * 2,
        out_shape=[
            jax.ShapeDtypeStruct((rows, width), BF),
            jax.ShapeDtypeStruct((rows, width), F32),
        ],
        input_output_aliases={4: 0, 5: 1},
        scratch_shapes=[pltpu.VMEM((rows, PAIR), BF)] * 4 + [pltpu.VMEM((rows, PAIR), F32)],
        compiler_params=params(),
    )(bound, queries, keys, values, attended, logs)


def feed_kernel(
    block, steps, seq_axis,
    frame_ref, o_ref, o_full, target_ref, table_ref,
    wo_own, wo_other, wu_own, wu_other, wd_own, wd_other,
    y_ref, gh_ref, go_ref, sg_ref, ss_ref, grads,
    wo, wu, wd, act, slope, second_in, result_grad, hidden_grad, normed_s, hidden_s, acc, stage,
    sems, out_sems,
):
    i = pl.program_id(0)
    seq = lax.axis_index(seq_axis)
    width = wo.shape[0]
    half = width // 2
    chunks = act.shape[0]

    @pl.when(i == 0)
    def _():
        copies = []
        for m, (place, wo_h, wu_h, wd_h) in enumerate(
            ((seq, wo_own, wu_own, wd_own), (1 - seq, wo_other, wu_other, wd_other))
        ):
            rows = pl.ds(pl.multiple_of(place * half, 128), half)
            copies.append(pltpu.make_async_copy(wo_h, wo.at[rows, :], sems.at[m, 0]))
            for c in range(chunks):
                copies.append(
                    pltpu.make_async_copy(
                        wu_h.at[:, pl.ds(c * width, width)], wu.at[c, rows, :], sems.at[m, 1 + c]
                    )
                )
            for c in range(chunks // 2):
                copies.append(
                    pltpu.make_async_copy(
                        wd_h.at[pl.ds(c * width, width), :],
                        wd.at[place * (chunks // 2) + c],
                        sems.at[m, 1 + chunks + c],
                    )
                )
        for copy in copies:
            copy.start()
        for copy in copies:
            copy.wait()
        sg_ref[...] = jnp.zeros_like(sg_ref)
        ss_ref[...] = jnp.zeros_like(ss_ref)
        spare = grads.shape[1] - (2 * chunks + 1) * half
        if spare > 0:
            stage[0] = jnp.zeros_like(stage[0])
            fills = [
                pltpu.make_async_copy(
                    stage.at[0, pl.ds(0, spare), :],
                    grads.at[h, pl.ds((2 * chunks + 1) * half, spare), :],
                    out_sems.at[0, h],
                )
                for h in range(2)
            ]
            for fill in fills:
                fill.start()
            for fill in fills:
                fill.wait()

    @pl.when(i < steps)
    def _():
        rows = pl.ds(pl.multiple_of(i * block, block), block)
        hidden = frame_ref[...].astype(F32) + table_ref[4:5, :] + dot(o_ref[...], wo[...])
        normed, inv_std = norm_rows(hidden)
        normed_s[...] = normed
        second_in[rows, :] = (normed * table_ref[2:3, :] + table_ref[3:4, :]).astype(BF)
        acc[...] = hidden

        u = dot(second_in[rows, :], wu[0])
        for c in range(chunks):
            later = dot(second_in[rows, :], wu[c + 1]) if c + 1 < chunks else None
            a, s = gelu_pair(u)
            a = a.astype(BF)
            act[c, rows, :] = a
            slope[c, rows, :] = s.astype(BF)
            acc[...] += dot(a, wd[c])
            u = later
        result = acc[...]
        y_ref[...] = result.astype(BF)
        grad = table_ref[5:6, :] * (result - target_ref[...].astype(F32))
        result_grad[rows, :] = grad.astype(BF)
        hidden_s[...] = grad
        acc[...] = jnp.zeros_like(acc)

        back = dot_t(result_grad[rows, :], wd[0])
        for c in range(chunks):
            later = dot_t(result_grad[rows, :], wd[c + 1]) if c + 1 < chunks else None
            back = (back * slope[c, rows, :].astype(F32)).astype(BF)
            slope[c, rows, :] = back
            acc[...] += dot_t(back, wu[c])
            back = later
        grad = acc[...]
        normed = normed_s[...]
        ss_ref[...] += jnp.sum(grad, axis=0, keepdims=True)
        sg_ref[...] += jnp.sum(grad * normed, axis=0, keepdims=True)
        grad = hidden_s[...] + norm_rows_back(grad, normed, inv_std, table_ref[2:3, :])
        gh_ref[...] = grad
        grad = grad.astype(BF)
        hidden_grad[rows, :] = grad
        go_ref[...] = dot_t(grad, wo[...]).astype(BF)

    def out_copies(n):
        slot = n % 2
        if n < chunks:
            at = grads.at[n // (chunks // 2), pl.ds((n % (chunks // 2)) * width, width), :]
            return [pltpu.make_async_copy(stage.at[slot], at, out_sems.at[slot, 0])]
        base = (chunks // 2) * width + (n - chunks) * half
        return [
            pltpu.make_async_copy(
                stage.at[slot, pl.ds(h * half, half), :],
                grads.at[h, pl.ds(base, half), :],
                out_sems.at[slot, h],
            )
            for h in range(2)
        ]

    last = 2 * chunks
    for n in range(last + 1):

        @pl.when(i == steps + n)
        def _():
            if n >= 2:
                for copy in out_copies(n - 2):
                    copy.wait()
            if n < chunks:
                term = dot_l(act[n], result_grad[...])
            elif n < last:
                term = dot_l(second_in[...], slope[n - chunks])
            else:
                term = dot_l(o_full[...], hidden_grad[...])
            stage[n % 2] = term.astype(BF)
            for copy in out_copies(n):
                copy.start()
            if n == last:
                for m in (n - 1, n):
                    for copy in out_copies(m):
                        copy.wait()


def feed_call(frame, attended, target, table, halves, grad_rows, block):
    rows, width = frame.shape
    chunks = halves[2].shape[1] // width
    steps = rows // block
    tile = pl.BlockSpec((block, width), lambda i: (jnp.minimum(i, steps - 1), 0))
    whole = pl.BlockSpec((rows, width), lambda i: (0, 0), pipeline_mode=pl.Buffered(1))
    vec = pl.BlockSpec((1, width), lambda i: (0, 0))
    anys = pl.BlockSpec(memory_space=pl.ANY)
    return pl.pallas_call(
        functools.partial(feed_kernel, block, steps, "seq"),
        grid=(steps + 2 * chunks + 1,),
        in_specs=[tile, tile, whole, tile, pl.BlockSpec((8, width), lambda i: (0, 0))]
        + [anys] * 6,
        out_specs=[tile, tile, tile, vec, vec, anys],
        out_shape=[
            jax.ShapeDtypeStruct((rows, width), BF),
            jax.ShapeDtypeStruct((rows, width), F32),
            jax.ShapeDtypeStruct((rows, width), BF),
            jax.ShapeDtypeStruct((1, width), F32),
            jax.ShapeDtypeStruct((1, width), F32),
            jax.ShapeDtypeStruct((2, grad_rows, width), BF),
        ],
        scratch_shapes=[
            pltpu.VMEM((width, width), BF),
            pltpu.VMEM((chunks, width, width), BF),
            pltpu.VMEM((chunks, width, width), BF),
            pltpu.VMEM((chunks, rows, width), BF),
            pltpu.VMEM((chunks, rows, width), BF),
            pltpu.VMEM((rows, width), BF),
            pltpu.VMEM((rows, width), BF),
            pltpu.VMEM((rows, width), BF),
            pltpu.VMEM((block, width), F32),
            pltpu.VMEM((block, width), F32),
            pltpu.VMEM((block, width), F32),
            pltpu.VMEM((2, width, width), BF),
            pltpu.SemaphoreType.DMA((2, 1 + chunks + chunks // 2)),
            pltpu.SemaphoreType.DMA((2, 2)),
        ],
        compiler_params=params(),
    )(frame, attended, attended, target, table, *halves)


def split_three(x):
    first = x.astype(BF)
    rest = x - first.astype(F32)
    second = rest.astype(BF)
    rest = rest - second.astype(F32)
    return first, second, rest.astype(BF)


def attend_back_kernel(
    dp, parts, q_ref, k_ref, v_ref, g_ref, o_ref, l_ref, source, result,
    gq_ref, gk_ref, gv_ref, out, result_out,
    qm, km, vm, gm, acc, trade_sems, *refs
):
    rows = q_ref.shape[0]
    pair, i = pl.program_id(0), pl.program_id(1)
    pairs, blocks = pl.num_programs(0), pl.num_programs(1)
    block = gv_ref.shape[0]
    slot = pair * blocks + i
    slots = 6 * (rows // block)
    place = Place(dp)

    near = result_out.shape[1]
    seq = place.seq
    trade = send(
        place, "seq", result.at[pl.ds(near, near), :], result_out.at[seq], trade_sems
    )
    keep = pltpu.make_async_copy(
        result.at[pl.ds(0, near), :], result_out.at[seq], trade_sems.at[2]
    )

    @pl.when(slot == 0)
    def _():
        place.meet()
        keep.start()

    @pl.when(slot == slots // 2)
    def _():
        trade.start()

    @pl.when(slot == slots - 1)
    def _():
        trade.wait()
        keep.wait()

    for n, reducer in enumerate(reducers(place, parts, source, out, refs)):
        events = reducer.events(n < WHOLE_PARTS)
        for at, event in zip(reduce_slots(len(events), slots, n), events):
            pl.when(slot == at)(event)

    lane = lax.broadcasted_iota(jnp.int32, (rows, PAIR), 1)

    @pl.when(i == 0)
    def _():
        low = lane < HEAD_DIM
        sub = lane % HEAD_DIM
        product = g_ref[...].astype(F32) * o_ref[...].astype(F32)
        first = product.astype(BF)
        line = lax.broadcasted_iota(jnp.int32, (PAIR, PAIR), 0)
        column = lax.broadcasted_iota(jnp.int32, (PAIR, PAIR), 1)
        cross = jnp.where((line < HEAD_DIM) != (column < HEAD_DIM), -1.0, 0.0).astype(BF)
        inner = dot(first, cross) + dot((product - first.astype(F32)).astype(BF), cross)

        def tail(x):
            terms = split_three(x)
            zero = jnp.zeros_like(terms[0])
            return jnp.where(
                sub == 0, terms[0], jnp.where(sub == 1, terms[1], jnp.where(sub == 2, terms[2], zero))
            )

        log_tail = tail(-pltpu.roll(l_ref[...], HEAD_DIM, 1))
        inner_tail = tail(inner)
        ones = jnp.where(sub < 3, 1.0, 0.0).astype(BF)
        for ref, x, extra in (
            (qm, q_ref[...], log_tail), (gm, g_ref[...], inner_tail),
            (km, k_ref[...], ones), (vm, v_ref[...], ones),
        ):
            ref[0] = jnp.where(low, x, extra)
            ref[1] = jnp.where(low, extra, x)
        acc[...] = jnp.zeros_like(acc)

    low_block = lax.broadcasted_iota(jnp.int32, (block, PAIR), 1) < HEAD_DIM
    here = pl.ds(pl.multiple_of(i * block, block), block)
    value_terms, key_terms = [], []
    turned = k_ref[here, :].T
    for h in range(2):
        prob = jnp.exp2(EXP2_SCALE * dot_t(km[h, here, :], qm[h]))
        score = (prob * dot_t(vm[h, here, :], gm[h])).astype(BF)
        value_terms.append(dot(prob.astype(BF), g_ref[...]))
        key_terms.append(dot(score, q_ref[...]))
        acc[h] += dot(turned, score)
    gv_ref[...] = jnp.where(low_block, value_terms[0], value_terms[1]).astype(BF)
    gk_ref[...] = (SCORE_SCALE * jnp.where(low_block, key_terms[0], key_terms[1])).astype(BF)

    @pl.when(i == blocks - 1)
    def _():
        gq_ref[...] = (SCORE_SCALE * jnp.where(lane < HEAD_DIM, acc[0].T, acc[1].T)).astype(BF)


WHOLE_PARTS = 2
REDUCE_SLOTS = (
    (0, 2, 6, 9, 11, 13, 15, 17, 20, 22),
    (0, 2, 6, 9, 11, 13, 15, 17, 20, 22),
    (3, 6, 10, 13, 16, 19, 23),
    (3, 6, 10, 13, 16, 19, 23),
)


def reduce_slots(count, slots, part):
    known = REDUCE_SLOTS[part]
    if len(known) == count:
        return [at * (slots - 1) // known[-1] if slots != 24 else at for at in known]
    return [n * (slots - 1) // (count - 1) for n in range(count)]


def attend_back_call(queries, keys, values, grad, attended, logs, source, result, dp, block):
    rows, width = queries.shape
    tile = pl.BlockSpec((rows, PAIR), lambda i, j: (0, i))
    part_tile = pl.BlockSpec((block, PAIR), lambda i, j: (j, i))
    anys = pl.BlockSpec(memory_space=pl.ANY)
    parts = reduce_parts(source.shape[1], dp)
    return pl.pallas_call(
        functools.partial(attend_back_kernel, dp, parts),
        grid=(width // PAIR, rows // block),
        in_specs=[tile] * 6 + [anys] * 2,
        out_specs=[tile, part_tile, part_tile, anys, anys],
        out_shape=[jax.ShapeDtypeStruct((rows, width), BF)] * 3
        + [
            jax.ShapeDtypeStruct(source.shape[1:], BF),
            jax.ShapeDtypeStruct((2, rows // 2, width), BF),
        ],
        scratch_shapes=[pltpu.VMEM((2, rows, PAIR), BF)] * 4
        + [pltpu.VMEM((2, PAIR, rows), F32), pltpu.SemaphoreType.DMA((3,))]
        + reduce_scratch(parts, width),
        compiler_params=pltpu.CompilerParams(
            vmem_limit_bytes=VMEM_BYTES, collective_id=1, has_side_effects=True
        ),
    )(queries, keys, values, grad, attended, logs, source, result)


def last_kernel(
    dp, parts, late_parts, block,
    frame_ref, gh_ref, gq_ref, gk_ref, gv_ref, table_ref, sg2_ref, ss2_ref, weight_ref, late_in,
    out, gi_out, small_ref, lead_ref, late,
    weights, first_in, source, gi, sums, trade, gathered, weight_sem, gi_sems, keep_sems, small_sems, late_sems,
    *refs,
):
    parts_in = (gq_ref, gk_ref, gv_ref)
    i = pl.program_id(0)
    place = Place(dp)
    seq = place.seq
    rows, width = gq_ref.shape
    half = width // 2
    near = rows // 2
    steps = rows // block
    pieces = near // block
    emb, gain, shift = table_ref[4:5, :], table_ref[0:1, :], table_ref[1:2, :]
    fetch = pltpu.make_async_copy(weight_ref, weights, weight_sem)
    made = [r.events() for r in reducers(place, parts, source, out, refs)]
    late_made = [
        Reducer(place, part, n, None, late, (), late_sems, None).gather_events()
        for n, part in enumerate(late_parts)
    ]

    def late_on(n):
        for events in late_made:
            if n < len(events) - 1:
                events[n]()

    def normed_rows(at):
        hidden = frame_ref[pl.ds(at, block), :].astype(F32) + emb
        return norm_rows(hidden)

    @pl.when(i == 0)
    def _():
        place.meet()
        fetch.start()
        late_on(0)
        sums[...] = jnp.zeros_like(sums)
        if source.shape[1] > 3 * width:
            source[...] = jnp.zeros_like(source)
        fetch.wait()

    for n in range(3):

        @pl.when(i == pieces + n)
        def _():
            if n == 0:

                def some(m, _):
                    at = pl.multiple_of(m * block, block)
                    normed, _ = normed_rows(at)
                    first_in[pl.ds(at, block), :] = (normed * gain + shift).astype(BF)
                    return 0

                lax.fori_loop(0, pieces, some, 0)
            term = dot_l(first_in[...], parts_in[n][...]).astype(BF)
            base = parts[n][0]
            for h in range(2):
                for m in range(2):
                    source[h, pl.ds(base + m * half, half), :] = term[
                        h * half : (h + 1) * half, m * half : (m + 1) * half
                    ]
            made[n][0]()
            late_on(2 + n)

    def gi_copies(n):
        if n < pieces:
            src = gi.at[pl.ds(n * block, block), :]
            return send(place, "seq", src, gi_out.at[seq, pl.ds(n * block, block), :], gi_sems.at[n])
        n -= pieces
        return pltpu.make_async_copy(
            gi.at[pl.ds(near + n * block, block), :],
            gi_out.at[seq, pl.ds(n * block, block), :],
            keep_sems.at[n],
        )

    for n in range(steps):

        @pl.when(i == (n if n < pieces else n + 3))
        def _():
            at = n * block + (near if n < pieces else -near)
            here = pl.ds(at, block)
            grad = dot_t(gq_ref[here, :], weights[0])
            grad += dot_t(gk_ref[here, :], weights[1])
            grad += dot_t(gv_ref[here, :], weights[2])
            normed, inv_std = normed_rows(at)
            if n < pieces:
                first_in[here, :] = (normed * gain + shift).astype(BF)
            sums[1:2, :] += jnp.sum(grad, axis=0, keepdims=True)
            sums[0:1, :] += jnp.sum(grad * normed, axis=0, keepdims=True)
            grad = gh_ref[...] + norm_rows_back(grad, normed, inv_std, gain)
            sums[4:5, :] += jnp.sum(grad, axis=0, keepdims=True)
            gi[pl.ds(n * block, block), :] = grad.astype(BF)
            gi_copies(n).start()
            if n == pieces - 1:
                late_on(1)
            if n >= pieces:
                for events in made:
                    events[n - pieces + 1]()

    def small_copy(step):
        if step == 0:
            return send(place, "seq", trade.at[0], trade.at[1], small_sems.at[0])
        b = step - 1
        start = (place.dp // (1 << b)) * (1 << b)
        group = gathered.at[pl.ds(start, 1 << b)]
        return send(place, b, group, group, small_sems.at[step])

    @pl.when(i == 3 + steps)
    def _():
        sums[2:3, :] = sg2_ref[...]
        sums[3:4, :] = ss2_ref[...]
        here = pl.ds(pl.multiple_of(seq * half, 128), half)
        there = pl.ds(pl.multiple_of((1 - seq) * half, 128), half)
        trade[0] = sums[:, there]
        small_copy(0).start()
        left = [events[pieces + 1 :] for events in made]
        todo = [events[n] for n in range(len(left[0])) for events in left]
        share = -(-len(todo) // (place.bits + 2))
        for event in todo[:share]:
            event()
        small_copy(0).wait()
        mine, theirs = sums[:, here], trade[1]
        line = lax.broadcasted_iota(jnp.int32, (8, half), 0)
        turned = jnp.broadcast_to(theirs[4:5, :], (8, half))
        value = jnp.where(line < 4, mine + theirs, jnp.where(line == 4, mine, turned))
        value = jnp.where(line == 6, table_ref[6:7, 0:half], value)
        value = jnp.where(line == 7, table_ref[7:8, 0:half], value)
        gathered[place.dp] = value
        for step in range(1, place.bits + 1):
            small_copy(step).start()
            for event in todo[step * share : (step + 1) * share]:
                event()
            small_copy(step).wait()
        for event in todo[(place.bits + 1) * share :]:
            event()
        index = lax.broadcasted_iota(jnp.int32, lead_ref.shape, 0).astype(F32)
        small_ref[...] = jnp.zeros_like(small_ref)
        lead_ref[...] = jnp.zeros_like(lead_ref)

        def add_device(d, _):
            value = gathered[d]
            small_ref[...] += value
            lead_ref[...] += jnp.where(index == value[6:7, :], value[4:5, :], 0.0) + jnp.where(
                index == value[7:8, :], value[5:6, :], 0.0
            )
            return 0

        lax.fori_loop(0, dp, add_device, 0)
        for n in range(steps):
            gi_copies(n).wait()
        for n in range(5, place.bits):
            late_on(n)
        for events in late_made:
            events[-1]()


def last_call(
    frame, hidden_grad, gq, gk, gv, table, sg2, ss2, weights, late, dp, lead_count, block
):
    rows, width = frame.shape
    half = width // 2
    steps = rows // block
    pieces = steps // 2
    size = padded_rows(width, dp)
    bits = dp.bit_length() - 1
    middle = list(range(1, bits))
    orders = [middle + ["seq"], middle[1:] + ["seq"] + middle[:1], ["seq"] + middle]
    late_parts = reduce_parts(late.shape[0], dp)[WHOLE_PARTS:]
    parts = [(n * size, size, [0] + order) for n, order in enumerate(orders)]
    whole = pl.BlockSpec((rows, width), lambda i: (0, 0))

    def turn(i):
        return (jnp.where(i < pieces, i + pieces, jnp.clip(i - 3 - pieces, 0, pieces - 1)), 0)

    def fixed(*shape):
        return pl.BlockSpec(shape, lambda i: (0,) * len(shape))

    vec = fixed(1, width)
    anys = pl.BlockSpec(memory_space=pl.ANY)
    return pl.pallas_call(
        functools.partial(last_kernel, dp, parts, late_parts, block),
        grid=(4 + steps,),
        in_specs=[whole, pl.BlockSpec((block, width), turn), whole, whole, whole]
        + [fixed(8, width), vec, vec, anys, anys],
        out_specs=[anys, anys, fixed(8, half), fixed(lead_count, half), anys],
        input_output_aliases={9: 4},
        out_shape=[
            jax.ShapeDtypeStruct((3 * size, half), BF),
            jax.ShapeDtypeStruct((2, rows // 2, width), BF),
            jax.ShapeDtypeStruct((8, half), F32),
            jax.ShapeDtypeStruct((lead_count, half), F32),
            jax.ShapeDtypeStruct(late.shape, BF),
        ],
        scratch_shapes=[
            pltpu.VMEM((3, width, width), BF),
            pltpu.VMEM((rows, width), BF),
            pltpu.VMEM((2, 3 * size, half), BF),
            pltpu.VMEM((rows, width), BF),
            pltpu.VMEM((8, width), F32),
            pltpu.VMEM((2, 8, half), F32),
            pltpu.VMEM((dp, 8, half), F32),
            pltpu.SemaphoreType.DMA,
            pltpu.SemaphoreType.DMA((pieces, 2)),
            pltpu.SemaphoreType.DMA((pieces,)),
            pltpu.SemaphoreType.DMA((bits + 1, 2)),
            pltpu.SemaphoreType.DMA((max(len(late_parts), 1), 2 * (bits + 1), 2)),
        ]
        + reduce_scratch(parts, half),
        compiler_params=pltpu.CompilerParams(
            vmem_limit_bytes=VMEM_BYTES, collective_id=4, has_side_effects=True
        ),
    )(frame, hidden_grad, gq, gk, gv, table, sg2, ss2, weights, late)


def body(
    frames, targets, lead_index, lead_counts,
    first_gain, first_shift, query_weight, key_weight, value_weight, output_weight,
    second_gain, second_shift, up_weight, down_weight, lead_table,
):
    dp = lax.axis_size("dp")
    rows, width = frames.shape[1] * 2, frames.shape[2]
    half = width // 2
    vectors = jnp.concatenate([first_gain, first_shift, second_gain, second_shift]).reshape(4, half)

    early = (query_weight, key_weight, value_weight)
    late = (output_weight, up_weight, down_weight)
    queries, keys, values, frame, weights, table, bound = start_call(
        frames, lead_index, lead_counts, vectors, lead_table, early, dp, rows // 6
    )
    attended, logs, target, wu_other, wd_other, wo_other = attend_call(
        queries, keys, values, targets, late, dp, rows // 2
    )
    attended, logs = shifted_call(bound, queries, keys, values, attended, logs, rows // 4)
    halves = (output_weight, wo_other, up_weight, wu_other, down_weight, wd_other)
    result, hidden_grad, attended_grad, sg2, ss2, grads = feed_call(
        frame, attended, target, table, halves,
        padded_rows(9 * half, dp), rows // 6,
    )
    gq, gk, gv, late_sum, output = attend_back_call(
        queries, keys, values, attended_grad, attended, logs, grads, result, dp, rows // 4
    )
    early_sum, input_grad, small, lead_grad, late_sum = last_call(
        frame, hidden_grad, gq, gk, gv, table, sg2, ss2, weights, late_sum, dp,
        lead_table.shape[0], rows // 6,
    )

    rows_ff = 4 * half
    late_sum = late_sum.astype(F32)
    down_grad = late_sum[:rows_ff]
    up_grad = late_sum[rows_ff : 2 * rows_ff].reshape(4, half, width)
    up_grad = jnp.moveaxis(up_grad, 0, 1).reshape(half, 4 * width)
    output_grad = late_sum[2 * rows_ff : 2 * rows_ff + half]
    size = early_sum.shape[0] // 3
    early_grads = [
        jnp.concatenate([early_sum[at : at + half], early_sum[at + half : at + 2 * half]], 1).astype(F32)
        for at in (0, size, 2 * size)
    ]
    return (
        output, input_grad, small[0], small[1], *early_grads, output_grad,
        small[2], small[3], up_grad, down_grad, lead_grad,
    )


def solution(mesh):
    weight = P("seq", None)
    vector = P("seq")
    batch = P("dp", "seq", None)
    table = P(None, "seq")
    return jax.shard_map(
        body,
        mesh=mesh,
        in_specs=(
            batch, batch, P("dp"), P("dp", None), vector, vector, weight, weight, weight, weight,
            vector, vector, weight, weight, table,
        ),
        out_specs=(
            batch, batch, vector, vector, weight, weight, weight, weight, vector, vector, weight,
            weight, table,
        ),
        check_vma=False,
    )
```
